32 devices in a mesh: layer: 2 (over y), pos: 16 (over z, x, core).
Axes of the slice: x: 2, y: 2, z: 4, core: 2. Of those that a mesh axis runs over, the one named last changes fastest.
Arguments:
- layer_inputs: bfloat16 [2, 32, 16, 16, 128], P('layer', 'pos'), may hold values from -6 to 6
- output_grads: bfloat16 [2, 32, 16, 16, 128], P('layer', 'pos'), may hold values from -2 to 2
- input_inverse: float32 [2, 1152, 1152], P('layer', 'pos'), may hold values from -0.06 to 2.1
- grad_inverse: float32 [2, 128, 128], P('layer'), may hold values from -4 to 54
Outputs:
- update: float32 [2, 1152, 128], P('layer', 'pos')
- grad_grams: float32 [2, 2, 128, 128], P('layer')
The draws below stay inside these ranges and needn't reach their ends.
All inputs are finite; a program needn't handle non-finite values.
Results may differ from the reference program's by a relative error of at most 0.0023.
Values may be sent and summed in bfloat16 or wider, within the bound.
No kernel may reach another device: no remote copies, remote signals or barrier semaphores. Data moves between devices by JAX's collectives and lax.ppermute only.
A program may use at most 64 MiB of HBM per device.

```python
import jax
import jax.numpy as jnp
from jax import lax

CH = 128
KK = 9
SIDE = 16
LAYERS = 2
IMAGES = 32
POSITIONS = 8192


def fresh_noise(key, shape):
    return jnp.clip(jax.random.normal(key, shape, jnp.float32), -4.0, 4.0)


def layer_chain(prev, fresh):
    nxt = 0.6 * prev + 0.8 * fresh
    return (nxt, nxt)


def joint_fields(key):
    base = jax.random.fold_in(key, 7)
    key_input, key_grad = jax.random.split(base)
    shape = (LAYERS, IMAGES, SIDE, SIDE, CH)
    noise_input = fresh_noise(key_input, shape)
    _, rest_input = lax.scan(layer_chain, noise_input[0], noise_input[1:])
    inputs = jnp.concatenate([noise_input[:1], rest_input], axis=0)
    noise_grad = fresh_noise(key_grad, shape)
    _, rest_grad = lax.scan(layer_chain, noise_grad[0], noise_grad[1:])
    hidden_part = jnp.concatenate([noise_grad[:1], rest_grad], axis=0)
    image_scale = 1.0 + 2.0 * jnp.arange(IMAGES, dtype=jnp.float32) / max(IMAGES - 1, 1)
    image_scale = image_scale.reshape(1, IMAGES, 1, 1, 1)
    grads = 0.1 * image_scale * (0.8 * hidden_part + 0.6 * inputs)
    return (jnp.clip(inputs, -6.0, 6.0), jnp.clip(grads, -2.0, 2.0))


def stale_inverse(key, order, level):
    key_diag, key_off = jax.random.split(key)
    diagonal = level * jnp.exp(jax.random.uniform(key_diag, (LAYERS, order), jnp.float32, -0.6931472, 0.6931472))
    off_part = fresh_noise(key_off, (LAYERS, order, order)) * (level * 0.3 / order ** 0.5)
    return off_part + diagonal[:, :, None] * jnp.eye(order, dtype=jnp.float32)[None]


def draw_layer_inputs(key, part):
    return joint_fields(key)[0].astype(jnp.bfloat16)


def draw_output_grads(key, part):
    return joint_fields(key)[1].astype(jnp.bfloat16)


def draw_input_inverse(key, part):
    return stale_inverse(jax.random.fold_in(key, 21), KK * CH, 1.0)


def draw_grad_inverse(key, part):
    return stale_inverse(jax.random.fold_in(key, 22), CH, 25.0)


def setup_inputs(seed: int = 0) -> dict:
    keys = jax.random.split(jax.random.key(seed), 5)
    return {
        "layer_inputs": draw_layer_inputs(jax.random.fold_in(keys[4], 71), 0),
        "output_grads": draw_output_grads(jax.random.fold_in(keys[4], 71), 0),
        "input_inverse": draw_input_inverse(jax.random.fold_in(keys[4], 71), 0),
        "grad_inverse": draw_grad_inverse(jax.random.fold_in(keys[4], 71), 0),
    }


def pad_maps(layer_maps):
    return jnp.pad(layer_maps, ((0, 0), (1, 1), (1, 1), (0, 0)))


def unfold_piece(padded, kernel_tap):
    offset_row = kernel_tap // 3
    offset_col = kernel_tap % 3
    return padded[:, offset_row:offset_row + SIDE, offset_col:offset_col + SIDE, :].reshape(-1, CH)


def reference(layer_inputs, output_grads, input_inverse, grad_inverse):
    scale_all = 1.0 / POSITIONS
    next_inputs = jnp.concatenate([layer_inputs[1:], jnp.zeros_like(layer_inputs[:1])], axis=0)
    next_grads = jnp.concatenate([output_grads[1:], jnp.zeros_like(output_grads[:1])], axis=0)

    def first_pass(inputs):
        layer_maps, grad_maps, grad_after = inputs
        padded = pad_maps(layer_maps)
        grad_rows = grad_maps.reshape(-1, CH)
        blocks = [jnp.dot(unfold_piece(padded, kernel_tap).T, grad_rows, preferred_element_type=jnp.float32) for kernel_tap in range(KK)]
        grad_w = jnp.concatenate(blocks, axis=0) * scale_all
        g_own = jnp.dot(grad_rows.T, grad_rows, preferred_element_type=jnp.float32) * scale_all
        g_cross = jnp.dot(grad_rows.T, grad_after.reshape(-1, CH), preferred_element_type=jnp.float32) * scale_all
        return grad_w, g_own, g_cross

    grad_w, g_own, g_cross = lax.map(first_pass, (layer_inputs, output_grads, next_grads))
    high = lax.Precision.HIGHEST
    precond = jnp.einsum("lij,ljk->lik", input_inverse, grad_w, precision=high)
    precond = jnp.einsum("lik,lkm->lim", precond, grad_inverse, precision=high).astype(jnp.bfloat16)
    precond_next = jnp.concatenate([precond[1:], jnp.zeros_like(precond[:1])], axis=0)

    def second_pass(inputs):
        layer_maps, maps_after, precond_after = inputs
        padded = pad_maps(layer_maps)
        padded_after = pad_maps(maps_after)
        mapped = jnp.zeros((layer_maps.shape[0] * SIDE * SIDE, CH), jnp.float32)
        for kernel_tap in range(KK):
            mapped = mapped + jnp.dot(unfold_piece(padded_after, kernel_tap), precond_after[kernel_tap * CH:(kernel_tap + 1) * CH], preferred_element_type=jnp.float32)
        mapped = mapped.astype(jnp.bfloat16)
        blocks = [jnp.dot(unfold_piece(padded, kernel_tap).T, mapped, preferred_element_type=jnp.float32) for kernel_tap in range(KK)]
        return jnp.concatenate(blocks, axis=0) * scale_all

    cross_term = lax.map(second_pass, (layer_inputs, next_inputs, precond_next))
    corrected = grad_w - jnp.einsum("lij,lkj->lik", cross_term, g_cross, precision=high)
    update = jnp.einsum("lij,ljk->lik", input_inverse, corrected, precision=high)
    update = jnp.einsum("lik,lkm->lim", update, grad_inverse, precision=high)
    grad_grams = jnp.stack([g_own, g_cross], axis=1)
    return update, grad_grams
```

```python
import jax
import jax.numpy as jnp
from jax import lax
from jax.sharding import PartitionSpec as P

F32 = jnp.float32
BF16 = jnp.bfloat16
HIGH = lax.Precision.HIGHEST


def after(block):
    devices = range(lax.axis_size("layer"))
    route = [(i + 1, i) for i in devices if i + 1 in devices]
    return lax.ppermute(block, "layer", route)


def swap(block, bit):
    return lax.ppermute(block, "pos", [(i, i ^ bit) for i in range(lax.axis_size("pos"))])


def pad_maps(layer_maps):
    return jnp.pad(layer_maps, ((0, 0), (1, 1), (1, 1), (0, 0)))


def patches(layer_maps):
    side = layer_maps.shape[1]
    width = layer_maps.shape[3]
    padded = pad_maps(layer_maps)
    return jnp.concatenate(
        [
            padded[:, r : r + side, s : s + side, :].reshape(-1, width)
            for r in range(3)
            for s in range(3)
        ],
        axis=1,
    )


def dot_t(a, b, **kw):
    return lax.dot_general(a, b, (((0,), (0,)), ((), ())), preferred_element_type=F32, **kw)


def dot_nt(a, b, **kw):
    return lax.dot_general(a, b, (((1,), (1,)), ((), ())), preferred_element_type=F32, **kw)


def blocks_from(own, block, count):
    parts = own.reshape((count, own.shape[0] // count) + own.shape[1:])
    return jnp.stack([lax.dynamic_index_in_dim(parts, block ^ j, 0, False) for j in range(count)])


def per_device(layer_inputs, output_grads, input_inverse, grad_inverse):
    maps = layer_inputs[0]
    grads = output_grads[0]
    k_rows = input_inverse[0]
    g_inv = grad_inverse[0]
    width = maps.shape[3]
    group = lax.axis_size("pos")
    rows = k_rows.shape[0]
    full = k_rows.shape[1]
    scale = 1.0 / (maps.shape[0] * maps.shape[1] * maps.shape[2] * group)
    me = lax.axis_index("pos")
    core = me & 1
    xbit = (me >> 1) & 1
    cols = 2 * core + xbit
    zbits = [b for b in (1 << i for i in range(2, 32)) if b < group]
    quarter = width // 4

    maps_next = after(maps)
    grads_next = after(grads)
    k_two = [k_rows, swap(k_rows, 2)]

    grad_rows = grads.reshape(-1, width)
    cuts = patches(maps)
    part_t = dot_t(grad_rows, cuts)
    e_t = dot_t(g_inv, part_t, precision=HIGH)
    e_blocks = blocks_from(e_t, cols, 4)

    h = e_blocks[:2] + swap(e_blocks[2:], 1)
    h = h[0] + swap(h[1], 2)
    for b in zbits:
        h = h + swap(h, b)
    e_mine = h * scale

    own_part = dot_t(grad_rows, grad_rows)
    cross_part = dot_t(grad_rows, grads_next.reshape(-1, width))
    gram = blocks_from(jnp.concatenate([own_part, cross_part], axis=1), cols, 4)
    gram = gram[:2] + swap(gram[2:], 1)
    gram = gram[0] + swap(gram[1], 2)
    for b in zbits:
        gram = gram + swap(gram, b)
    gram = gram * scale
    other = swap(gram, 2)
    gram = jnp.where(xbit == 0, jnp.concatenate([gram, other]), jnp.concatenate([other, gram]))
    other = swap(gram, 1)
    gram = jnp.where(core == 0, jnp.concatenate([gram, other]), jnp.concatenate([other, gram]))
    g_own, g_cross = gram[:, :width], gram[:, width:]
    big_h = dot_t(g_cross, g_inv, precision=HIGH)
    h_mine = lax.dynamic_slice_in_dim(big_h, cols * quarter, quarter, 0)

    k_x = jnp.where(xbit == 0, jnp.stack(k_two), jnp.stack(k_two[::-1]))
    k_c = swap(k_x, 1)
    k_z = jnp.where(core == 0, jnp.stack([k_x, k_c], 1), jnp.stack([k_c, k_x], 1)).reshape(4 * rows, full)

    p_t = dot_nt(e_mine, k_z, precision=HIGH).astype(BF16)
    for b in zbits:
        other = swap(p_t, b)
        p_t = jnp.where((me & b) == 0, jnp.concatenate([p_t, other], 1), jnp.concatenate([other, p_t], 1))
    p_t = after(p_t)

    def gathered(m):
        m = jnp.concatenate([m, swap(m, 2)], 0)
        return jnp.concatenate([m, swap(m, 1)], 0)

    maps_z = gathered(maps)
    next_z = gathered(maps_next)
    taps = p_t.T.reshape(3, 3, width, quarter)
    mapped = lax.conv_general_dilated(
        next_z, taps, (1, 1), "SAME", dimension_numbers=("NHWC", "HWIO", "NHWC"), preferred_element_type=F32
    ).astype(BF16)
    cross_t = dot_t(mapped.reshape(-1, quarter), patches(maps_z))
    for b in zbits:
        cross_t = cross_t + swap(cross_t.astype(BF16), b).astype(F32)
    cross_t = cross_t * scale

    main = dot_nt(k_z, e_mine, precision=HIGH)
    fix = jnp.dot(dot_nt(k_z, cross_t, precision=HIGH), h_mine, precision=HIGH)
    out = lax.dynamic_update_slice(jnp.zeros((4 * rows, width), F32), main, (0, cols * quarter)) - fix
    out = out.reshape(2, 2, rows, width)
    keep = lax.dynamic_index_in_dim(out, xbit, 0, False)
    send = lax.dynamic_index_in_dim(out, 1 - xbit, 0, False)
    out = keep + swap(send, 2)
    keep = lax.dynamic_index_in_dim(out, core, 0, False)
    send = lax.dynamic_index_in_dim(out, 1 - core, 0, False)
    update = keep + swap(send, 1)
    return (update[None], jnp.stack([g_own, g_cross])[None])


def solution(mesh):
    return jax.shard_map(
        per_device,
        mesh=mesh,
        in_specs=(
            P("layer", "pos", None, None, None),
            P("layer", "pos", None, None, None),
            P("layer", "pos", None),
            P("layer", None, None),
        ),
        out_specs=(P("layer", "pos", None), P("layer", None, None, None)),
        check_vma=False,
    )
```

```python
import functools

import jax
import jax.numpy as jnp
from jax import lax
from jax.experimental import pallas as pl
from jax.experimental.pallas import tpu as pltpu
from jax.sharding import PartitionSpec as P

F32 = jnp.float32
BF16 = jnp.bfloat16
HIGH = lax.Precision.HIGHEST
hold = lax.optimization_barrier


def after(block):
    devices = range(lax.axis_size("layer"))
    route = [(i + 1, i) for i in devices if i + 1 in devices]
    return lax.ppermute(block, "layer", route)


def swap(block, bit):
    return lax.ppermute(block, "pos", [(i, i ^ bit) for i in range(lax.axis_size("pos"))])


def dot_t(a, b, **kw):
    return lax.dot_general(a, b, (((0,), (0,)), ((), ())), preferred_element_type=F32, **kw)


def dot_nt(a, b, **kw):
    return lax.dot_general(a, b, (((1,), (1,)), ((), ())), preferred_element_type=F32, **kw)


def shifted(block, dy, dx, side):
    lanes = block.shape[1]
    place = lax.broadcasted_iota(jnp.int32, (1, lanes), 1)
    x = place % side
    y = (place // side) % side
    if dx:
        block = jnp.where((x + dx >= 0) & (x + dx < side), pltpu.roll(block, (-dx) % lanes, 1), 0.0)
    if dy:
        block = jnp.where((y + dy >= 0) & (y + dy < side), pltpu.roll(block, (-dy * side) % lanes, 1), 0.0)
    return block


def taps_to_rows(block, side):
    moved = []
    for r in range(3):
        for s in range(3):
            moved.append(shifted(shifted(block, 0, 1 - s, side), 1 - r, 0, side).astype(BF16))
    return jnp.concatenate(moved, axis=0)


def grad_kernel(side, maps, grads, g_two, out):
    quarter = out.shape[0]
    width = maps.shape[1]
    first = g_two[...].astype(BF16)
    rest = g_two[...] - first.astype(F32)
    second = rest.astype(BF16)
    third = (rest - second.astype(F32)).astype(BF16)
    g = grads[...]
    mixed = dot_nt(first, g) + (dot_nt(second, g) + dot_nt(third, g))
    high = mixed.astype(BF16).astype(F32)
    row = lax.broadcasted_iota(jnp.int32, mixed.shape, 0)
    mixed = jnp.where(row < quarter, high, mixed - high)
    both = jnp.dot(taps_to_rows(mixed, side), maps[...], preferred_element_type=F32)
    for tap in range(9):
        low = 2 * quarter * tap
        out[:, tap * width : (tap + 1) * width] = (
            both[low : low + quarter] + both[low + quarter : low + 2 * quarter]
        )


def cross_kernel(side, maps, maps_next, precond_t, out, out_half):
    quarter = precond_t.shape[0]
    width = maps.shape[1]
    taps = jnp.concatenate([precond_t[:, t * width : (t + 1) * width] for t in range(9)], axis=0)
    spread = dot_nt(taps, maps_next[...])
    mapped = None
    for s in range(3):
        column = None
        for r in range(3):
            low = quarter * (3 * r + s)
            part = shifted(spread[low : low + quarter], r - 1, 0, side)
            column = part if column is None else column + part
        column = shifted(column, 0, s - 1, side)
        mapped = column if mapped is None else mapped + column
    mapped = mapped.astype(BF16).astype(F32)
    both = jnp.dot(taps_to_rows(mapped, side), maps[...], preferred_element_type=F32)
    for tap in range(9):
        part = both[quarter * tap : quarter * (tap + 1)]
        out[:, tap * width : (tap + 1) * width] = part
        out_half[:, tap * width : (tap + 1) * width] = part.astype(BF16)


VMEM = pl.BlockSpec(memory_space=pltpu.VMEM)
PARAMS = pltpu.CompilerParams(vmem_limit_bytes=32 * 1024 * 1024)


def per_device(layer_inputs, output_grads, input_inverse, grad_inverse):
    maps = layer_inputs[0]
    grads = output_grads[0]
    k_rows = input_inverse[0]
    g_inv = grad_inverse[0]
    side = maps.shape[1]
    width = maps.shape[3]
    group = lax.axis_size("pos")
    rows, full = k_rows.shape
    scale = 1.0 / (maps.shape[0] * maps.shape[1] * maps.shape[2] * group)
    me = lax.axis_index("pos")
    core = me & 1
    xbit = (me >> 1) & 1
    cols = 2 * core + xbit
    zbits = [b for b in (1 << i for i in range(2, 32)) if b < group]
    quarter = width // 4
    flat_maps = maps.reshape(-1, width)
    flat_grads = grads.reshape(-1, width)

    own = jnp.concatenate([flat_grads, flat_maps], axis=0)
    pair = jnp.concatenate([own[None], swap(own, 2)[None]], axis=0)
    four = jnp.concatenate([pair, swap(pair, 1)], axis=0)
    count = flat_maps.shape[0]
    grads_z = four[:, :count].reshape(-1, width)
    maps_z = four[:, count:].reshape(-1, width)

    next_both = after(own)
    k_x = swap(k_rows, 2)

    g_cols = lax.dynamic_slice_in_dim(g_inv, cols * quarter, quarter, 1).T
    h = pl.pallas_call(
        functools.partial(grad_kernel, side),
        out_shape=jax.ShapeDtypeStruct((quarter, full), F32),
        in_specs=[VMEM] * 3,
        out_specs=VMEM,
        compiler_params=PARAMS,
    )(maps_z, grads_z, jnp.concatenate([g_cols, g_cols], axis=0))

    h, k_x, k_rows, next_both = hold((h, k_x, k_rows, next_both))
    k_two = jnp.where(xbit == 0, jnp.stack([k_rows, k_x]), jnp.stack([k_x, k_rows]))
    k_c = swap(k_two, 1)
    next_pair = jnp.concatenate([next_both[None], swap(next_both, 2)[None]], axis=0)
    h = h + swap(h, zbits[0])

    h, k_c, k_two, next_pair = hold((h, k_c, k_two, next_pair))
    k_z = jnp.where(core == 0, jnp.stack([k_two, k_c], 1), jnp.stack([k_c, k_two], 1)).reshape(4 * rows, full)
    next_four = jnp.concatenate([next_pair, swap(next_pair, 1)], axis=0)
    next_maps_z = next_four[:, :, :].reshape(4, 2, count, width)[:, 1].reshape(-1, width)
    next_grads_z = next_four.reshape(4, 2, count, width)[:, 0].reshape(-1, width)
    for b in zbits[1:]:
        h = h + swap(h, b)
    e_mine = h * scale

    p_t = dot_nt(e_mine, k_z, precision=HIGH).astype(BF16)
    p_t, next_grads_z, next_maps_z = hold((p_t, next_grads_z, next_maps_z))
    p_t = after(p_t)

    g_mine = lax.dynamic_slice_in_dim(grads_z, cols * quarter, quarter, 1)
    gram = dot_t(g_mine, jnp.concatenate([grads_z, next_grads_z], axis=1))
    p_t, gram = hold((p_t, gram))
    for b in zbits:
        gram_other = swap(gram, b)
        other = swap(p_t, b)
        p_t = jnp.where((me & b) == 0, jnp.concatenate([p_t, other], 1), jnp.concatenate([other, p_t], 1))
        gram = gram + gram_other
        p_t, gram = hold((p_t, gram))
    gram = gram * scale

    cross_t, cross_half = pl.pallas_call(
        functools.partial(cross_kernel, side),
        out_shape=[jax.ShapeDtypeStruct((quarter, full), F32), jax.ShapeDtypeStruct((quarter, full), BF16)],
        in_specs=[VMEM] * 3,
        out_specs=[VMEM] * 2,
        compiler_params=PARAMS,
    )(maps_z, next_maps_z, p_t)

    cross_t, cross_half, gram = hold((cross_t, cross_half, gram))
    other = swap(gram, 2)
    cross_t = cross_t + swap(cross_half, zbits[0]).astype(F32)
    cross_t, other, gram = hold((cross_t, other, gram))
    gram = jnp.where(xbit == 0, jnp.concatenate([gram, other]), jnp.concatenate([other, gram]))
    other = swap(gram, 1)
    for b in zbits[1:]:
        cross_t = cross_t + swap(cross_t.astype(BF16), b).astype(F32)
    gram = jnp.where(core == 0, jnp.concatenate([gram, other]), jnp.concatenate([other, gram]))
    g_own, g_cross = gram[:, :width], gram[:, width:]
    big_h = dot_t(g_cross, g_inv, precision=HIGH)
    h_mine = lax.dynamic_slice_in_dim(big_h, cols * quarter, quarter, 0) * scale

    main = dot_nt(k_z, e_mine, precision=HIGH)
    main = lax.dynamic_update_slice(jnp.zeros((4 * rows, width), F32), main, (0, cols * quarter))
    fix = jnp.dot(dot_nt(k_z, cross_t, precision=HIGH), h_mine, precision=HIGH)
    out = (main - fix).reshape(2, 2, rows, width)
    keep = lax.dynamic_index_in_dim(out, xbit, 0, False)
    send = lax.dynamic_index_in_dim(out, 1 - xbit, 0, False)
    out = keep + swap(send, 2)
    keep = lax.dynamic_index_in_dim(out, core, 0, False)
    send = lax.dynamic_index_in_dim(out, 1 - core, 0, False)
    update = keep + swap(send, 1)
    return (update[None], jnp.stack([g_own, g_cross])[None])


def solution(mesh):
    return jax.shard_map(
        per_device,
        mesh=mesh,
        in_specs=(
            P("layer", "pos", None, None, None),
            P("layer", "pos", None, None, None),
            P("layer", "pos", None),
            P("layer", None, None),
        ),
        out_specs=(P("layer", "pos", None), P("layer", None, None, None)),
        check_vma=False,
    )
```

```python
import functools

import jax
import jax.numpy as jnp
from jax import lax
from jax.experimental import pallas as pl
from jax.experimental.pallas import tpu as pltpu
from jax.sharding import PartitionSpec as P

F32 = jnp.float32
BF16 = jnp.bfloat16
HIGH = lax.Precision.HIGHEST


def behind(block, point):
    return lax.optimization_barrier((block, point))[0]


def after(block):
    devices = range(lax.axis_size("layer"))
    route = [(i + 1, i) for i in devices if i + 1 in devices]
    return lax.ppermute(block, "layer", route)


def swap(block, bit):
    return lax.ppermute(block, "pos", [(i, i ^ bit) for i in range(lax.axis_size("pos"))])


def dot_t(a, b, **kw):
    return lax.dot_general(a, b, (((0,), (0,)), ((), ())), preferred_element_type=F32, **kw)


def dot_nt(a, b, **kw):
    return lax.dot_general(a, b, (((1,), (1,)), ((), ())), preferred_element_type=F32, **kw)


def shifted(block, dy, dx, side):
    lanes = block.shape[1]
    place = lax.broadcasted_iota(jnp.int32, (1, lanes), 1)
    x = place % side
    y = (place // side) % side
    if dx:
        block = jnp.where((x + dx >= 0) & (x + dx < side), pltpu.roll(block, (-dx) % lanes, 1), 0.0)
    if dy:
        block = jnp.where((y + dy >= 0) & (y + dy < side), pltpu.roll(block, (-dy * side) % lanes, 1), 0.0)
    return block


def taps_to_rows(block, side):
    moved = []
    for r in range(3):
        for s in range(3):
            moved.append(shifted(shifted(block, 0, 1 - s, side), 1 - r, 0, side).astype(BF16))
    return jnp.concatenate(moved, axis=0)


def grad_kernel(side, maps, grads, g_two, out):
    quarter = out.shape[0]
    width = maps.shape[1]
    first = g_two[...].astype(BF16)
    rest = g_two[...] - first.astype(F32)
    second = rest.astype(BF16)
    third = (rest - second.astype(F32)).astype(BF16)
    g = grads[...]
    mixed = dot_nt(first, g) + (dot_nt(second, g) + dot_nt(third, g))
    high = mixed.astype(BF16).astype(F32)
    row = lax.broadcasted_iota(jnp.int32, mixed.shape, 0)
    mixed = jnp.where(row < quarter, high, mixed - high)
    both = jnp.dot(taps_to_rows(mixed, side), maps[...], preferred_element_type=F32)
    for tap in range(9):
        low = 2 * quarter * tap
        out[:, tap * width : (tap + 1) * width] = (
            both[low : low + quarter] + both[low + quarter : low + 2 * quarter]
        )


def cross_kernel(side, maps, maps_next, precond_t, out, out_half):
    quarter = precond_t.shape[0]
    width = maps.shape[1]
    taps = jnp.concatenate([precond_t[:, t * width : (t + 1) * width] for t in range(9)], axis=0)
    spread = dot_nt(taps, maps_next[...])
    mapped = None
    for s in range(3):
        column = None
        for r in range(3):
            low = quarter * (3 * r + s)
            part = shifted(spread[low : low + quarter], r - 1, 0, side)
            column = part if column is None else column + part
        column = shifted(column, 0, s - 1, side)
        mapped = column if mapped is None else mapped + column
    mapped = mapped.astype(BF16).astype(F32)
    both = jnp.dot(taps_to_rows(mapped, side), maps[...], preferred_element_type=F32)
    for tap in range(9):
        part = both[quarter * tap : quarter * (tap + 1)]
        out[:, tap * width : (tap + 1) * width] = part
        out_half[:, tap * width : (tap + 1) * width] = part.astype(BF16)


VMEM = pl.BlockSpec(memory_space=pltpu.VMEM)
PARAMS = pltpu.CompilerParams(vmem_limit_bytes=32 * 1024 * 1024)


def per_device(layer_inputs, output_grads, input_inverse, grad_inverse):
    maps = layer_inputs[0]
    grads = output_grads[0]
    k_rows = input_inverse[0]
    g_inv = grad_inverse[0]
    side = maps.shape[1]
    width = maps.shape[3]
    group = lax.axis_size("pos")
    rows, full = k_rows.shape
    scale = 1.0 / (maps.shape[0] * maps.shape[1] * maps.shape[2] * group)
    me = lax.axis_index("pos")
    core = me & 1
    xbit = (me >> 1) & 1
    cols = 2 * core + xbit
    zbits = [b for b in (1 << i for i in range(2, 32)) if b < group]
    quarter = width // 4
    flat_maps = maps.reshape(-1, width)
    flat_grads = grads.reshape(-1, width)

    count = flat_maps.shape[0]
    own = jnp.concatenate([flat_grads, flat_maps], axis=0)
    pair = jnp.concatenate([own[None], swap(own, 2)[None]], axis=0)
    four = jnp.concatenate([pair, swap(pair, 1)], axis=0)
    grads_z = four[:, :count].reshape(-1, width)
    maps_z = four[:, count:].reshape(-1, width)

    g_cols = lax.dynamic_slice_in_dim(g_inv, cols * quarter, quarter, 1).T
    h = pl.pallas_call(
        functools.partial(grad_kernel, side),
        out_shape=jax.ShapeDtypeStruct((quarter, full), F32),
        in_specs=[VMEM] * 3,
        out_specs=VMEM,
        compiler_params=PARAMS,
    )(maps_z, grads_z, jnp.concatenate([g_cols, g_cols], axis=0))

    k_rows = behind(k_rows, h)
    k_x = swap(k_rows, 2)
    next_pair = after(behind(pair, h))
    h = h + swap(h, zbits[0])
    k_two = jnp.where(xbit == 0, jnp.stack([k_rows, k_x]), jnp.stack([k_x, k_rows]))
    k_two = behind(k_two, h)
    k_c = swap(k_two, 1)
    k_z = jnp.where(core == 0, jnp.stack([k_two, k_c], 1), jnp.stack([k_c, k_two], 1)).reshape(4 * rows, full)
    for b in zbits[1:]:
        h = h + swap(h, b)

    main_t = dot_nt(h * scale, k_z, precision=HIGH)
    p_t = main_t.astype(BF16)
    next_pair = behind(next_pair, p_t)
    next_four = jnp.concatenate([next_pair, swap(next_pair, 1)], axis=0)
    next_grads_z = next_four[:, :count].reshape(-1, width)
    next_maps_z = next_four[:, count:].reshape(-1, width)
    p_t = after(p_t)

    low = cols * quarter
    both = jnp.concatenate(
        [
            lax.dynamic_slice_in_dim(grads_z, low, quarter, 1),
            lax.dynamic_slice_in_dim(next_grads_z, low, quarter, 1),
        ],
        axis=1,
    )
    gram = dot_t(behind(both, p_t), grads_z)
    for b in zbits:
        gram = behind(gram, p_t)
        other = swap(p_t, b)
        gram = gram + swap(gram, b)
        p_t = jnp.where((me & b) == 0, jnp.concatenate([p_t, other], 1), jnp.concatenate([other, p_t], 1))
    gram = gram * scale

    cross_t, cross_half = pl.pallas_call(
        functools.partial(cross_kernel, side),
        out_shape=[jax.ShapeDtypeStruct((quarter, full), F32), jax.ShapeDtypeStruct((quarter, full), BF16)],
        in_specs=[VMEM] * 3,
        out_specs=[VMEM] * 2,
        compiler_params=PARAMS,
    )(maps_z, next_maps_z, p_t)

    gram = behind(gram, cross_half)
    main_t = behind(main_t, cross_half)
    h_mine = jnp.dot(gram[quarter:], g_inv, precision=HIGH) * scale
    place = (jnp.arange(width)[None, :] == low + jnp.arange(quarter)[:, None]).astype(F32)
    main = dot_t(main_t, place, precision=HIGH)
    cross_t = cross_t + swap(cross_half, zbits[0]).astype(F32)
    for b in zbits[1:]:
        cross_t = cross_t + swap(cross_t.astype(BF16), b).astype(F32)

    fix = jnp.dot(dot_nt(k_z, cross_t, precision=HIGH), h_mine, precision=HIGH)
    out = (main - fix).reshape(2, 2, rows, width)
    gram = behind(gram, fix)
    gram = jnp.stack([gram, swap(gram, 2)])
    keep = lax.dynamic_index_in_dim(out, xbit, 0, False)
    send = lax.dynamic_index_in_dim(out, 1 - xbit, 0, False)
    out = keep + swap(send, 2)
    gram = jnp.stack([gram, swap(gram, 1)])
    keep = lax.dynamic_index_in_dim(out, core, 0, False)
    send = lax.dynamic_index_in_dim(out, 1 - core, 0, False)
    update = keep + swap(send, 1)
    gram = jnp.where(xbit == 0, gram, gram[:, ::-1])
    gram = jnp.where(core == 0, gram, gram[::-1])
    gram = gram.reshape(4, 2, quarter, width).transpose(1, 3, 0, 2).reshape(2, width, width)
    return (update[None], gram[None])


def solution(mesh):
    return jax.shard_map(
        per_device,
        mesh=mesh,
        in_specs=(
            P("layer", "pos", None, None, None),
            P("layer", "pos", None, None, None),
            P("layer", "pos", None),
            P("layer", None, None),
        ),
        out_specs=(P("layer", "pos", None), P("layer", None, None, None)),
        check_vma=False,
    )
```

```python
import functools

import jax
import jax.numpy as jnp
from jax import lax
from jax.experimental import pallas as pl
from jax.experimental.pallas import tpu as pltpu
from jax.sharding import PartitionSpec as P

F32 = jnp.float32
BF16 = jnp.bfloat16
HIGH = lax.Precision.HIGHEST


def behind(block, point):
    return lax.optimization_barrier((block, point))[0]


def after(block):
    devices = range(lax.axis_size("layer"))
    route = [(i + 1, i) for i in devices if i + 1 in devices]
    return lax.ppermute(block, "layer", route)


def swap(block, bit):
    return lax.ppermute(block, "pos", [(i, i ^ bit) for i in range(lax.axis_size("pos"))])


def dot_t(a, b, **kw):
    return lax.dot_general(a, b, (((0,), (0,)), ((), ())), preferred_element_type=F32, **kw)


def dot_nt(a, b, **kw):
    return lax.dot_general(a, b, (((1,), (1,)), ((), ())), preferred_element_type=F32, **kw)


def shifted(block, dy, dx, side):
    lanes = block.shape[1]
    place = lax.broadcasted_iota(jnp.int32, (1, lanes), 1)
    x = place % side
    y = (place // side) % side
    if dx:
        block = jnp.where((x + dx >= 0) & (x + dx < side), pltpu.roll(block, (-dx) % lanes, 1), 0.0)
    if dy:
        block = jnp.where((y + dy >= 0) & (y + dy < side), pltpu.roll(block, (-dy * side) % lanes, 1), 0.0)
    return block


def taps_to_rows(block, side):
    moved = []
    for r in range(3):
        for s in range(3):
            moved.append(shifted(shifted(block, 0, 1 - s, side), 1 - r, 0, side).astype(BF16))
    return jnp.concatenate(moved, axis=0)


def grad_kernel(side, maps, grads, g_inv, keep, send, all_rows):
    width = maps.shape[1]
    g_t = g_inv[...]
    first = g_t.astype(BF16)
    rest = g_t - first.astype(F32)
    second = rest.astype(BF16)
    third = (rest - second.astype(F32)).astype(BF16)
    g = grads[...]

    def mix(part):
        return lax.dot_general(part, g, (((0,), (1,)), ((), ())), preferred_element_type=F32)

    mixed = mix(first) + (mix(second) + mix(third))
    high = mixed.astype(BF16).astype(F32)
    rows = taps_to_rows(jnp.concatenate([high, mixed - high], axis=0), side)
    both = jnp.dot(rows, maps[...], preferred_element_type=F32)
    for tap in range(9):
        low = 2 * width * tap
        all_rows[:, tap * width : (tap + 1) * width] = (
            both[low : low + width] + both[low + width : low + 2 * width]
        )
    me = lax.axis_index("pos")
    mine = 2 * (me & 1) + ((me >> 1) & 1)
    quarter = width // 4
    for j in range(4):
        block = all_rows[pl.ds(pl.multiple_of((mine ^ j) * quarter, quarter), quarter), :]
        (keep if j < 2 else send)[j % 2] = block


def cross_kernel(side, maps, maps_next, precond_t, out, out_half):
    quarter = precond_t.shape[0]
    width = maps.shape[1]
    taps = jnp.concatenate([precond_t[:, t * width : (t + 1) * width] for t in range(9)], axis=0)
    spread = dot_nt(taps, maps_next[...])
    mapped = None
    for s in range(3):
        column = None
        for r in range(3):
            low = quarter * (3 * r + s)
            part = shifted(spread[low : low + quarter], r - 1, 0, side)
            column = part if column is None else column + part
        column = shifted(column, 0, s - 1, side)
        mapped = column if mapped is None else mapped + column
    mapped = mapped.astype(BF16).astype(F32)
    both = jnp.dot(taps_to_rows(mapped, side), maps[...], preferred_element_type=F32)
    for tap in range(9):
        part = both[quarter * tap : quarter * (tap + 1)]
        out[:, tap * width : (tap + 1) * width] = part
        out_half[:, tap * width : (tap + 1) * width] = part.astype(BF16)


VMEM = pl.BlockSpec(memory_space=pltpu.VMEM)
PARAMS = pltpu.CompilerParams(vmem_limit_bytes=32 * 1024 * 1024)


def per_device(layer_inputs, output_grads, input_inverse, grad_inverse):
    maps = layer_inputs[0]
    grads = output_grads[0]
    k_rows = input_inverse[0]
    g_inv = grad_inverse[0]
    side = maps.shape[1]
    width = maps.shape[3]
    group = lax.axis_size("pos")
    rows, full = k_rows.shape
    scale = 1.0 / (maps.shape[0] * maps.shape[1] * maps.shape[2] * group)
    me = lax.axis_index("pos")
    core = me & 1
    xbit = (me >> 1) & 1
    cols = 2 * core + xbit
    zbits = [b for b in (1 << i for i in range(2, 32)) if b < group]
    quarter = width // 4
    flat_maps = maps.reshape(-1, width)
    flat_grads = grads.reshape(-1, width)

    keep, send = pl.pallas_call(
        functools.partial(grad_kernel, side),
        out_shape=[jax.ShapeDtypeStruct((2, quarter, full), F32)] * 2,
        in_specs=[VMEM] * 3,
        out_specs=[VMEM] * 2,
        scratch_shapes=[pltpu.VMEM((width, full), F32)],
        compiler_params=PARAMS,
    )(flat_maps, flat_grads, g_inv)
    own = jnp.concatenate([flat_grads, flat_maps], axis=0)
    next_own = after(own)
    k_x = swap(k_rows, 2)
    h = keep + swap(send, 1)
    h = h[0] + swap(h[1], 2)
    h, k_x, next_own = lax.optimization_barrier((h, k_x, next_own))

    k_two = jnp.where(xbit == 0, jnp.stack([k_rows, k_x]), jnp.stack([k_x, k_rows]))
    k_c = swap(k_two, 1)
    two_own = jnp.concatenate([own, next_own], axis=0)
    pair = jnp.stack([two_own, swap(two_own, 2)])
    h = h + swap(h, zbits[0])
    k_z = jnp.where(core == 0, jnp.stack([k_two, k_c], 1), jnp.stack([k_c, k_two], 1)).reshape(4 * rows, full)
    for b in zbits[1:]:
        h = h + swap(h, b)

    main_t = dot_nt(h * scale, k_z, precision=HIGH)
    p_t = main_t.astype(BF16)
    pair = behind(pair, p_t)
    four = jnp.concatenate([pair, swap(pair, 1)], axis=0).reshape(4, 4, -1, width)
    grads_z, maps_z, next_grads_z, next_maps_z = (four[:, i].reshape(-1, width) for i in range(4))
    p_t = after(p_t)

    low = cols * quarter
    both = jnp.concatenate(
        [
            lax.dynamic_slice_in_dim(grads_z, low, quarter, 1),
            lax.dynamic_slice_in_dim(next_grads_z, low, quarter, 1),
        ],
        axis=1,
    )
    gram = dot_t(behind(both, p_t), grads_z)
    for b in zbits:
        other = swap(p_t, b)
        p_t = jnp.where((me & b) == 0, jnp.concatenate([p_t, other], 1), jnp.concatenate([other, p_t], 1))

    cross_t, cross_half = pl.pallas_call(
        functools.partial(cross_kernel, side),
        out_shape=[jax.ShapeDtypeStruct((quarter, full), F32), jax.ShapeDtypeStruct((quarter, full), BF16)],
        in_specs=[VMEM] * 3,
        out_specs=[VMEM] * 2,
        compiler_params=PARAMS,
    )(maps_z, next_maps_z, p_t)

    gram = behind(gram, cross_half)
    main_t = behind(main_t, cross_half)
    place = (jnp.arange(width)[None, :] == low + jnp.arange(quarter)[:, None]).astype(F32)
    main = dot_t(main_t, place, precision=HIGH)
    for b in zbits:
        gram = gram + swap(gram, b)
        cross_t = cross_t + swap(cross_half, b).astype(F32)
        cross_half = cross_t.astype(BF16)
        gram = behind(gram, cross_half)
    gram = gram * scale
    h_mine = jnp.dot(gram[quarter:], g_inv, precision=HIGH) * scale

    fix = jnp.dot(dot_nt(k_z, cross_t, precision=HIGH), h_mine, precision=HIGH)
    out = (main - fix).reshape(2, 2, rows, width)
    gram = behind(gram, out)
    gram = jnp.stack([gram, swap(gram, 2)])
    keep = lax.dynamic_index_in_dim(out, xbit, 0, False)
    send = lax.dynamic_index_in_dim(out, 1 - xbit, 0, False)
    out = keep + swap(send, 2)
    gram = jnp.stack([gram, swap(gram, 1)])
    keep = lax.dynamic_index_in_dim(out, core, 0, False)
    send = lax.dynamic_index_in_dim(out, 1 - core, 0, False)
    update = keep + swap(send, 1)
    gram = jnp.where(xbit == 0, gram, gram[:, ::-1])
    gram = jnp.where(core == 0, gram, gram[::-1])
    gram = gram.reshape(4, 2, quarter, width).transpose(1, 3, 0, 2).reshape(2, width, width)
    return (update[None], gram[None])


def solution(mesh):
    return jax.shard_map(
        per_device,
        mesh=mesh,
        in_specs=(
            P("layer", "pos", None, None, None),
            P("layer", "pos", None, None, None),
            P("layer", "pos", None),
            P("layer", None, None),
        ),
        out_specs=(P("layer", "pos", None), P("layer", None, None, None)),
        check_vma=False,
    )
```

```python
import functools

import jax
import jax.numpy as jnp
from jax import lax
from jax.experimental import pallas as pl
from jax.experimental.pallas import tpu as pltpu
from jax.sharding import PartitionSpec as P

F32 = jnp.float32
BF16 = jnp.bfloat16
HIGH = lax.Precision.HIGHEST


def behind(block, point):
    return lax.optimization_barrier((block, point))[0]


def after(block, bit=0):
    layers, group = lax.axis_size("layer"), lax.axis_size("pos")
    route = [(((i + 1) % layers) * group + (p ^ bit), i * group + p) for i in range(layers) for p in range(group)]
    return lax.ppermute(block, ("layer", "pos"), route)


def swap(block, bit):
    return lax.ppermute(block, "pos", [(i, i ^ bit) for i in range(lax.axis_size("pos"))])


def dot_t(a, b, **kw):
    return lax.dot_general(a, b, (((0,), (0,)), ((), ())), preferred_element_type=F32, **kw)


def dot_nt(a, b, **kw):
    return lax.dot_general(a, b, (((1,), (1,)), ((), ())), preferred_element_type=F32, **kw)


def shifted(block, dy, dx, side):
    lanes = block.shape[1]
    place = lax.broadcasted_iota(jnp.int32, (1, lanes), 1)
    x = place % side
    y = (place // side) % side
    if dx:
        block = jnp.where((x + dx >= 0) & (x + dx < side), pltpu.roll(block, (-dx) % lanes, 1), 0.0)
    if dy:
        block = jnp.where((y + dy >= 0) & (y + dy < side), pltpu.roll(block, (-dy * side) % lanes, 1), 0.0)
    return block


def taps_to_rows(block, side):
    moved = []
    for r in range(3):
        for s in range(3):
            moved.append(shifted(shifted(block, 0, 1 - s, side), 1 - r, 0, side).astype(BF16))
    return jnp.concatenate(moved, axis=0)


def grad_kernel(side, maps_in, grads_in, g_in, keep, send, all_rows, maps, grads, g_inv, sems):
    copies = [
        pltpu.make_async_copy(source, target, sems.at[i])
        for i, (source, target) in enumerate([(g_in, g_inv), (grads_in, grads), (maps_in, maps)])
    ]
    for copy in copies:
        copy.start()
    for copy in copies:
        copy.wait()
    width = maps.shape[1]
    g_t = g_inv[...]
    first = g_t.astype(BF16)
    rest = g_t - first.astype(F32)
    second = rest.astype(BF16)
    third = (rest - second.astype(F32)).astype(BF16)
    g = grads[...]

    def mix(part):
        return lax.dot_general(part, g, (((0,), (1,)), ((), ())), preferred_element_type=F32)

    mixed = mix(first) + (mix(second) + mix(third))
    high = mixed.astype(BF16).astype(F32)
    rows = taps_to_rows(jnp.concatenate([high, mixed - high], axis=0), side)
    both = jnp.dot(rows, maps[...], preferred_element_type=F32)
    for tap in range(9):
        low = 2 * width * tap
        all_rows[:, tap * width : (tap + 1) * width] = (
            both[low : low + width] + both[low + width : low + 2 * width]
        )
    me = lax.axis_index("pos")
    mine = 2 * (me & 1) + ((me >> 1) & 1)
    quarter = width // 4
    for j in range(4):
        block = all_rows[pl.ds(pl.multiple_of((mine ^ j) * quarter, quarter), quarter), :]
        (keep if j < 2 else send)[j % 2] = block


def cross_kernel(side, half_a, half_b, precond_t, gram, out, out_half):
    quarter = precond_t.shape[0]
    width = half_a.shape[3]
    full = precond_t.shape[1]
    taps = jnp.concatenate([precond_t[:, t * width : (t + 1) * width] for t in range(9)], axis=0)
    both = None
    for half in (half_a, half_b):
        for d in range(2):
            spread = dot_nt(taps, half[d, 1])
            mapped = None
            for s in range(3):
                column = None
                for r in range(3):
                    low = quarter * (3 * r + s)
                    part = shifted(spread[low : low + quarter], r - 1, 0, side)
                    column = part if column is None else column + part
                column = shifted(column, 0, s - 1, side)
                mapped = column if mapped is None else mapped + column
            mapped = mapped.astype(BF16).astype(F32)
            part = jnp.dot(taps_to_rows(mapped, side), half[d, 0], preferred_element_type=F32)
            both = part if both is None else both + part
    for tap in range(9):
        part = both[quarter * tap : quarter * (tap + 1)]
        out[:, tap * width : (tap + 1) * width] = part
        out_half[:, tap * width : (tap + 1) * width] = part.astype(BF16)
    for i in range(2):
        part = gram[i * quarter : (i + 1) * quarter]
        high = part.astype(BF16)
        rest = (part - high.astype(F32)).astype(BF16)
        low = full + i * width
        out[:, low : low + width] = high.astype(F32) + rest.astype(F32)
        out_half[:, low : low + width] = high
        out_half[:, low + 2 * width : low + 3 * width] = rest


VMEM = pl.BlockSpec(memory_space=pltpu.VMEM)
ANY = pl.BlockSpec(memory_space=pl.ANY)
PARAMS = pltpu.CompilerParams(vmem_limit_bytes=32 * 1024 * 1024)


def per_device(layer_inputs, output_grads, input_inverse, grad_inverse):
    maps = layer_inputs[0]
    grads = output_grads[0]
    k_rows = input_inverse[0]
    g_inv = grad_inverse[0]
    side = maps.shape[1]
    width = maps.shape[3]
    group = lax.axis_size("pos")
    rows, full = k_rows.shape
    scale = 1.0 / (maps.shape[0] * maps.shape[1] * maps.shape[2] * group)
    me = lax.axis_index("pos")
    core = me & 1
    xbit = (me >> 1) & 1
    cols = 2 * core + xbit
    zbits = [b for b in (1 << i for i in range(2, 32)) if b < group]
    quarter = width // 4
    flat_maps = maps.reshape(-1, width)
    flat_grads = grads.reshape(-1, width)

    keep, send = pl.pallas_call(
        functools.partial(grad_kernel, side),
        out_shape=[jax.ShapeDtypeStruct((2, quarter, full), F32)] * 2,
        in_specs=[ANY] * 3,
        out_specs=[VMEM] * 2,
        scratch_shapes=[
            pltpu.VMEM((width, full), F32),
            pltpu.VMEM(flat_maps.shape, BF16),
            pltpu.VMEM(flat_grads.shape, BF16),
            pltpu.VMEM(g_inv.shape, F32),
            pltpu.SemaphoreType.DMA((3,)),
        ],
        compiler_params=PARAMS,
    )(flat_maps, flat_grads, g_inv)
    h = keep + swap(send, 1)
    h = h[0] + swap(h[1], 2)
    h = h + swap(h, zbits[0])
    for b in zbits[1:]:
        h = h + swap(h, b)

    k_x = swap(k_rows, 2)
    k_two = jnp.where(xbit == 0, jnp.stack([k_rows, k_x]), jnp.stack([k_x, k_rows]))
    k_c = swap(k_two, 1)

    own = jnp.stack([flat_maps, flat_grads])
    next_own = after(own)
    two_own = jnp.stack([own[0], next_own[0], own[1], next_own[1]])
    half_a = jnp.stack([two_own, swap(two_own, 2)])
    half_b = swap(half_a, 1)

    def k_times(k_part, e_t):
        return dot_nt(e_t, k_part.reshape(2 * rows, full), precision=HIGH).reshape(-1, 2, rows)

    h = h * scale
    main_a = k_times(k_two, h)
    main_b = k_times(k_c, h)
    main_t = jnp.where(core == 0, jnp.stack([main_a, main_b], 2), jnp.stack([main_b, main_a], 2))
    main_t = main_t.reshape(quarter, 4 * rows)
    p_t = main_t.astype(BF16)

    def by_bit(mine, other, b):
        return jnp.where((me & b) == 0, jnp.concatenate([mine, other], 1), jnp.concatenate([other, mine], 1))

    for b in zbits[:-1]:
        p_t = by_bit(p_t, swap(p_t, b), b)
    p_t = by_bit(after(p_t), after(p_t, zbits[-1]), zbits[-1])
    last = lax.axis_index("layer") == lax.axis_size("layer") - 1
    p_t = jnp.where(last, jnp.zeros_like(p_t), p_t)

    low = cols * quarter
    grads_a, grads_b = (half[:, 2].reshape(-1, width) for half in (half_a, half_b))
    gram = 0.0
    for half in (half_a, half_b):
        here, following = (
            lax.dynamic_slice_in_dim(half[:, i].reshape(-1, width), low, quarter, 1) for i in (2, 3)
        )
        following = jnp.where(last, jnp.zeros_like(following), following)
        gram = gram + dot_t(jnp.concatenate([here, following], axis=1), half[:, 2].reshape(-1, width))

    out_width = full + 2 * width
    cross_t, cross_half = pl.pallas_call(
        functools.partial(cross_kernel, side),
        out_shape=[
            jax.ShapeDtypeStruct((quarter, out_width), F32),
            jax.ShapeDtypeStruct((quarter, out_width + 2 * width), BF16),
        ],
        in_specs=[VMEM] * 4,
        out_specs=[VMEM] * 2,
        compiler_params=PARAMS,
    )(half_a, half_b, p_t, gram)

    place = (jnp.arange(width)[None, :] == low + jnp.arange(quarter)[:, None]).astype(F32)
    main = dot_t(main_t, place, precision=HIGH)
    cross_t, gram = cross_t[:, :full], cross_t[:, full:]
    for b in zbits:
        other = swap(cross_half, b).astype(F32)
        cross_t = cross_t + other[:, :full]
        gram = gram + (other[:, full:out_width] + other[:, out_width:])
        high = lax.reduce_precision(gram, 8, 7)
        rest = lax.reduce_precision(gram - high, 8, 7)
        gram = high + rest
        cross_half = jnp.concatenate([cross_t, high, rest], axis=1).astype(BF16)
    gram = gram * scale
    h_mine = jnp.dot(gram[:, width:], g_inv, precision=HIGH) * scale

    fix_a = dot_nt(k_two.reshape(2 * rows, full), cross_t, precision=HIGH).reshape(2, 1, rows, quarter)
    fix_b = dot_nt(k_c.reshape(2 * rows, full), cross_t, precision=HIGH).reshape(2, 1, rows, quarter)
    fix = jnp.where(core == 0, jnp.concatenate([fix_a, fix_b], 1), jnp.concatenate([fix_b, fix_a], 1))
    out = main - jnp.dot(fix.reshape(4 * rows, quarter), h_mine, precision=HIGH)
    out = out.reshape(2, 2, rows, width)
    gram = behind(gram, out)
    gram = jnp.stack([gram, swap(gram, 2)])
    keep = lax.dynamic_index_in_dim(out, xbit, 0, False)
    send = lax.dynamic_index_in_dim(out, 1 - xbit, 0, False)
    out = keep + swap(send, 2)
    gram = jnp.stack([gram, swap(gram, 1)])
    keep = lax.dynamic_index_in_dim(out, core, 0, False)
    send = lax.dynamic_index_in_dim(out, 1 - core, 0, False)
    update = keep + swap(send, 1)
    gram = jnp.where(xbit == 0, gram, gram[:, ::-1])
    gram = jnp.where(core == 0, gram, gram[::-1])
    gram = gram.reshape(width, 2, width).transpose(1, 2, 0)
    return (update[None], gram[None])


def solution(mesh):
    return jax.shard_map(
        per_device,
        mesh=mesh,
        in_specs=(
            P("layer", "pos", None, None, None),
            P("layer", "pos", None, None, None),
            P("layer", "pos", None),
            P("layer", None, None),
        ),
        out_specs=(P("layer", "pos", None), P("layer", None, None, None)),
        check_vma=False,
    )
```

```python
import functools

import jax
import jax.numpy as jnp
from jax import lax
from jax.experimental import pallas as pl
from jax.experimental.pallas import tpu as pltpu
from jax.sharding import PartitionSpec as P

F32 = jnp.float32
BF16 = jnp.bfloat16
HIGH = lax.Precision.HIGHEST


def behind(block, point):
    return lax.optimization_barrier((block, point))[0]


def after(block, bit=0):
    layers, group = lax.axis_size("layer"), lax.axis_size("pos")
    route = [(((i + 1) % layers) * group + (p ^ bit), i * group + p) for i in range(layers) for p in range(group)]
    return lax.ppermute(block, ("layer", "pos"), route)


def swap(block, bit):
    return lax.ppermute(block, "pos", [(i, i ^ bit) for i in range(lax.axis_size("pos"))])


def dot_t(a, b, **kw):
    return lax.dot_general(a, b, (((0,), (0,)), ((), ())), preferred_element_type=F32, **kw)


def dot_nt(a, b, **kw):
    return lax.dot_general(a, b, (((1,), (1,)), ((), ())), preferred_element_type=F32, **kw)


def shifted(block, dy, dx, side):
    lanes = block.shape[1]
    place = lax.broadcasted_iota(jnp.int32, (1, lanes), 1)
    x = place % side
    y = (place // side) % side
    if dx:
        block = jnp.where((x + dx >= 0) & (x + dx < side), pltpu.roll(block, (-dx) % lanes, 1), 0.0)
    if dy:
        block = jnp.where((y + dy >= 0) & (y + dy < side), pltpu.roll(block, (-dy * side) % lanes, 1), 0.0)
    return block


def taps_to_rows(block, side):
    moved = []
    for r in range(3):
        for s in range(3):
            moved.append(shifted(shifted(block, 0, 1 - s, side), 1 - r, 0, side).astype(BF16))
    return jnp.concatenate(moved, axis=0)


def grad_kernel(side, maps_in, grads_in, g_in, keep, send, all_rows, maps, grads, g_inv, sems):
    copies = [
        pltpu.make_async_copy(source, target, sems.at[i])
        for i, (source, target) in enumerate([(g_in, g_inv), (grads_in, grads), (maps_in, maps)])
    ]
    for copy in copies:
        copy.start()
    for copy in copies:
        copy.wait()
    width = maps.shape[1]
    g_t = g_inv[...]
    first = g_t.astype(BF16)
    rest = g_t - first.astype(F32)
    second = rest.astype(BF16)
    third = (rest - second.astype(F32)).astype(BF16)
    g = grads[...]

    def mix(part):
        return lax.dot_general(part, g, (((0,), (1,)), ((), ())), preferred_element_type=F32)

    mixed = mix(first) + (mix(second) + mix(third))
    high = mixed.astype(BF16).astype(F32)
    rows = taps_to_rows(jnp.concatenate([high, mixed - high], axis=0), side)
    both = jnp.dot(rows, maps[...], preferred_element_type=F32)
    for tap in range(9):
        low = 2 * width * tap
        all_rows[:, tap * width : (tap + 1) * width] = (
            both[low : low + width] + both[low + width : low + 2 * width]
        )
    me = lax.axis_index("pos")
    mine = 2 * (me & 1) + ((me >> 1) & 1)
    quarter = width // 4
    for j in range(4):
        block = all_rows[pl.ds(pl.multiple_of((mine ^ j) * quarter, quarter), quarter), :]
        (keep if j < 2 else send)[j % 2] = block


def cross_kernel(side, half_a, half_b, precond_t, gram, out, out_half):
    quarter = precond_t.shape[0]
    width = half_a.shape[3]
    full = precond_t.shape[1]
    taps = jnp.concatenate([precond_t[:, t * width : (t + 1) * width] for t in range(9)], axis=0)
    both = None
    for half in (half_a, half_b):
        for d in range(2):
            spread = dot_nt(taps, half[d, 1])
            mapped = None
            for s in range(3):
                column = None
                for r in range(3):
                    low = quarter * (3 * r + s)
                    part = shifted(spread[low : low + quarter], r - 1, 0, side)
                    column = part if column is None else column + part
                column = shifted(column, 0, s - 1, side)
                mapped = column if mapped is None else mapped + column
            mapped = mapped.astype(BF16).astype(F32)
            part = jnp.dot(taps_to_rows(mapped, side), half[d, 0], preferred_element_type=F32)
            both = part if both is None else both + part
    for tap in range(9):
        part = both[quarter * tap : quarter * (tap + 1)]
        out[:, tap * width : (tap + 1) * width] = part
        out_half[:, tap * width : (tap + 1) * width] = part.astype(BF16)
    for i in range(2):
        part = gram[i * quarter : (i + 1) * quarter]
        high = part.astype(BF16)
        rest = (part - high.astype(F32)).astype(BF16)
        low = full + i * width
        out[:, low : low + width] = high.astype(F32) + rest.astype(F32)
        out_half[:, low : low + width] = high
        out_half[:, low + 2 * width : low + 3 * width] = rest


VMEM = pl.BlockSpec(memory_space=pltpu.VMEM)
ANY = pl.BlockSpec(memory_space=pl.ANY)
PARAMS = pltpu.CompilerParams(vmem_limit_bytes=32 * 1024 * 1024)


def per_device(layer_inputs, output_grads, input_inverse, grad_inverse):
    maps = layer_inputs[0]
    grads = output_grads[0]
    k_rows = input_inverse[0]
    g_inv = grad_inverse[0]
    side = maps.shape[1]
    width = maps.shape[3]
    group = lax.axis_size("pos")
    rows, full = k_rows.shape
    scale = 1.0 / (maps.shape[0] * maps.shape[1] * maps.shape[2] * group)
    me = lax.axis_index("pos")
    core = me & 1
    xbit = (me >> 1) & 1
    cols = 2 * core + xbit
    zbits = [b for b in (1 << i for i in range(2, 32)) if b < group]
    quarter = width // 4
    flat_maps = maps.reshape(-1, width)
    flat_grads = grads.reshape(-1, width)

    keep, send = pl.pallas_call(
        functools.partial(grad_kernel, side),
        out_shape=[jax.ShapeDtypeStruct((2, quarter, full), F32)] * 2,
        in_specs=[ANY] * 3,
        out_specs=[VMEM] * 2,
        scratch_shapes=[
            pltpu.VMEM((width, full), F32),
            pltpu.VMEM(flat_maps.shape, BF16),
            pltpu.VMEM(flat_grads.shape, BF16),
            pltpu.VMEM(g_inv.shape, F32),
            pltpu.SemaphoreType.DMA((3,)),
        ],
        compiler_params=PARAMS,
    )(flat_maps, flat_grads, g_inv)
    h = keep + swap(send, 1)
    k_rows = behind(k_rows, h)
    own = behind(jnp.stack([flat_maps, flat_grads]), h)
    h = h[0] + swap(h[1], 2)
    h = h + swap(h, zbits[0])
    point = h
    for b in zbits[1:]:
        h = h + swap(h, b)

    k_a = jnp.concatenate([k_rows, swap(k_rows, 2)], axis=0)
    k_b = swap(k_a, 1)

    next_own = after(own)
    two_own = behind(jnp.stack([own[0], next_own[0], own[1], next_own[1]]), point)
    half_a = jnp.stack([two_own, swap(two_own, 2)])
    half_b = swap(half_a, 1)

    h = h * scale
    main_t = jnp.concatenate(
        [dot_nt(h, k_a, precision=HIGH), dot_nt(h, k_b, precision=HIGH)], axis=1
    )
    p_t = main_t.astype(BF16)

    def by_bit(mine, other, b):
        return jnp.where((me & b) == 0, jnp.concatenate([mine, other], 1), jnp.concatenate([other, mine], 1))

    for b in zbits[:-1]:
        p_t = by_bit(p_t, swap(p_t, b), b)
    last = lax.axis_index("layer") == lax.axis_size("layer") - 1
    early = p_t

    def in_order(p_t):
        p_t = by_bit(after(p_t), after(p_t, zbits[-1]), zbits[-1])
        p_t = jnp.where(last, jnp.zeros_like(p_t), p_t)
        p_t = p_t.reshape(quarter, -1, 2, 2, rows).transpose(0, 1, 3, 2, 4)
        p_t = jnp.where(xbit == 0, p_t, p_t[:, :, ::-1])
        p_t = jnp.where(core == 0, p_t, p_t[:, :, :, ::-1])
        return p_t.reshape(quarter, full)

    low = cols * quarter
    gram = 0.0
    for half in (half_a, half_b):
        here, following = (
            lax.dynamic_slice_in_dim(half[:, i].reshape(-1, width), low, quarter, 1) for i in (2, 3)
        )
        following = jnp.where(last, jnp.zeros_like(following), following)
        gram = gram + dot_t(jnp.concatenate([here, following], axis=1), half[:, 2].reshape(-1, width))

    p_t = in_order(behind(early, gram))

    out_width = full + 2 * width
    cross_t, cross_half = pl.pallas_call(
        functools.partial(cross_kernel, side),
        out_shape=[
            jax.ShapeDtypeStruct((quarter, out_width), F32),
            jax.ShapeDtypeStruct((quarter, out_width + 2 * width), BF16),
        ],
        in_specs=[VMEM] * 4,
        out_specs=[VMEM] * 2,
        compiler_params=PARAMS,
    )(half_a, half_b, p_t, gram)

    place = (jnp.arange(width)[None, :] == low + jnp.arange(quarter)[:, None]).astype(F32)
    main = dot_t(main_t, place, precision=HIGH)
    cross_t, gram = cross_t[:, :full], cross_t[:, full:]
    for b in zbits:
        other = swap(cross_half, b).astype(F32)
        cross_t = cross_t + other[:, :full]
        gram = gram + (other[:, full:out_width] + other[:, out_width:])
        high = lax.reduce_precision(gram, 8, 7)
        rest = lax.reduce_precision(gram - high, 8, 7)
        gram = high + rest
        cross_half = jnp.concatenate([cross_t, high, rest], axis=1).astype(BF16)
    gram = gram * scale
    h_mine = jnp.dot(gram[:, width:], g_inv, precision=HIGH) * scale

    fix = jnp.concatenate(
        [dot_nt(k_a, cross_t, precision=HIGH), dot_nt(k_b, cross_t, precision=HIGH)], axis=0
    )
    out = main - jnp.dot(fix, h_mine, precision=HIGH)
    out = out.reshape(2, 2, rows, width)
    gram = behind(gram, out)
    gram = jnp.stack([gram, swap(gram, 2)])
    out = out[:, 0] + swap(out[:, 1], 2)
    gram = jnp.stack([gram, swap(gram, 1)])
    update = out[0] + swap(out[1], 1)
    gram = jnp.where(xbit == 0, gram, gram[:, ::-1])
    gram = jnp.where(core == 0, gram, gram[::-1])
    gram = gram.reshape(width, 2, width).transpose(1, 2, 0)
    return (update[None], gram[None])


def solution(mesh):
    return jax.shard_map(
        per_device,
        mesh=mesh,
        in_specs=(
            P("layer", "pos", None, None, None),
            P("layer", "pos", None, None, None),
            P("layer", "pos", None),
            P("layer", None, None),
        ),
        out_specs=(P("layer", "pos", None), P("layer", None, None, None)),
        check_vma=False,
    )
```

```python
import functools

import jax
import jax.numpy as jnp
from jax import lax
from jax.experimental import pallas as pl
from jax.experimental.pallas import tpu as pltpu
from jax.sharding import PartitionSpec as P

F32 = jnp.float32
BF16 = jnp.bfloat16
HIGH = lax.Precision.HIGHEST


def behind(block, point):
    return lax.optimization_barrier((block, point))[0]


def after(block, bit=0):
    layers, group = lax.axis_size("layer"), lax.axis_size("pos")
    route = [(((i + 1) % layers) * group + (p ^ bit), i * group + p) for i in range(layers) for p in range(group)]
    return lax.ppermute(block, ("layer", "pos"), route)


def swap(block, bit):
    return lax.ppermute(block, "pos", [(i, i ^ bit) for i in range(lax.axis_size("pos"))])


def dot_t(a, b, **kw):
    return lax.dot_general(a, b, (((0,), (0,)), ((), ())), preferred_element_type=F32, **kw)


def dot_nt(a, b, **kw):
    return lax.dot_general(a, b, (((1,), (1,)), ((), ())), preferred_element_type=F32, **kw)


def shifted(block, dy, dx, side):
    lanes = block.shape[1]
    place = lax.broadcasted_iota(jnp.int32, (1, lanes), 1)
    x = place % side
    y = (place // side) % side
    if dx:
        block = jnp.where((x + dx >= 0) & (x + dx < side), pltpu.roll(block, (-dx) % lanes, 1), 0.0)
    if dy:
        block = jnp.where((y + dy >= 0) & (y + dy < side), pltpu.roll(block, (-dy * side) % lanes, 1), 0.0)
    return block


def taps_to_rows(block, side):
    moved = []
    for r in range(3):
        for s in range(3):
            moved.append(shifted(shifted(block, 0, 1 - s, side), 1 - r, 0, side).astype(BF16))
    return jnp.concatenate(moved, axis=0)


def grad_kernel(side, maps_in, grads_in, g_in, keep, send, all_rows, maps, grads, g_inv, sems):
    copies = [
        pltpu.make_async_copy(source, target, sems.at[i])
        for i, (source, target) in enumerate([(g_in, g_inv), (grads_in, grads), (maps_in, maps)])
    ]
    for copy in copies:
        copy.start()
    for copy in copies:
        copy.wait()
    width = maps.shape[1]
    g_t = g_inv[...]
    first = g_t.astype(BF16)
    rest = g_t - first.astype(F32)
    second = rest.astype(BF16)
    third = (rest - second.astype(F32)).astype(BF16)
    g = grads[...]

    def mix(part):
        return lax.dot_general(part, g, (((0,), (1,)), ((), ())), preferred_element_type=F32)

    mixed = mix(first) + (mix(second) + mix(third))
    high = mixed.astype(BF16).astype(F32)
    rows = taps_to_rows(jnp.concatenate([high, mixed - high], axis=0), side)
    both = jnp.dot(rows, maps[...], preferred_element_type=F32)
    for tap in range(9):
        low = 2 * width * tap
        all_rows[:, tap * width : (tap + 1) * width] = (
            both[low : low + width] + both[low + width : low + 2 * width]
        )
    core, xbit = place_bits()
    mine = 2 * core + xbit
    quarter = width // 4
    for j in range(4):
        block = all_rows[pl.ds(pl.multiple_of((mine ^ j) * quarter, quarter), quarter), :]
        (keep if j < 2 else send)[j % 2] = block


def cross_kernel(side, half_a, half_b, precond_t, gram, out, out_half):
    quarter = precond_t.shape[0]
    width = half_a.shape[3]
    full = precond_t.shape[1]
    taps = jnp.concatenate([precond_t[:, t * width : (t + 1) * width] for t in range(9)], axis=0)
    both = None
    for half in (half_a, half_b):
        for d in range(2):
            spread = dot_nt(taps, half[d, 1])
            mapped = None
            for s in range(3):
                column = None
                for r in range(3):
                    low = quarter * (3 * r + s)
                    part = shifted(spread[low : low + quarter], r - 1, 0, side)
                    column = part if column is None else column + part
                column = shifted(column, 0, s - 1, side)
                mapped = column if mapped is None else mapped + column
            mapped = mapped.astype(BF16).astype(F32)
            part = jnp.dot(taps_to_rows(mapped, side), half[d, 0], preferred_element_type=F32)
            both = part if both is None else both + part
    for tap in range(9):
        part = both[quarter * tap : quarter * (tap + 1)]
        out[:, tap * width : (tap + 1) * width] = part
        out_half[:, tap * width : (tap + 1) * width] = part.astype(BF16)
    for i in range(2):
        part = gram[i * quarter : (i + 1) * quarter]
        high = part.astype(BF16)
        rest = (part - high.astype(F32)).astype(BF16)
        low = full + i * width
        out[:, low : low + width] = high.astype(F32) + rest.astype(F32)
        out_half[:, low : low + width] = high
        out_half[:, low + 2 * width : low + 3 * width] = rest


def two_parts(block):
    high = block.astype(BF16)
    return jnp.concatenate([high, (block - high.astype(F32)).astype(BF16)], axis=0)


def place_bits():
    me = lax.axis_index("pos")
    return me & 1, (me >> 1) & 1


def precond_kernel(scale, e_t, k_a, k_b, main_a, main_b, precond_t):
    core, xbit = place_bits()
    count = e_t.shape[0]
    rows = k_a.shape[0] // 2
    parts = two_parts(e_t[...] * scale)
    total = None
    for flip, k, main in ((0, k_a, main_a), (1, k_b, main_b)):
        k_parts = two_parts(k[...])
        product = dot_nt(parts, k_parts[: 2 * rows]) + dot_nt(parts, k_parts[2 * rows :])
        product = product[:count] + product[count:]
        main[...] = product
        source = lax.broadcasted_iota(jnp.int32, (2 * rows, 4 * rows), 0)
        target = lax.broadcasted_iota(jnp.int32, (2 * rows, 4 * rows), 1)
        second = (source >= rows).astype(jnp.int32)
        block = 2 * (xbit ^ second) + (core ^ flip)
        one_hot = (source - second * rows + block * rows == target).astype(F32).astype(BF16)
        placed = jnp.dot(product.astype(BF16), one_hot, preferred_element_type=F32)
        total = placed if total is None else total + placed
    precond_t[...] = total.astype(BF16)


def update_kernel(scale, cross_t, gram, g_inv, k_a, k_b, main, keep, send):
    rows = k_a.shape[0] // 2
    mixed = jnp.dot(gram[...], g_inv[...], precision=HIGH) * (scale * scale)
    mixed = jnp.concatenate([mixed, mixed], axis=0)
    parts = two_parts(cross_t[...])
    for i, k in enumerate((k_a, k_b)):
        k_parts = two_parts(k[...])
        product = dot_nt(k_parts[: 2 * rows], parts) + dot_nt(k_parts[2 * rows :], parts)
        result = main[i] - jnp.dot(product, mixed, precision=HIGH)
        keep[i] = result[:rows]
        send[i] = result[rows:]


def gram_kernel(half_a, half_b, out, scratch):
    core, xbit = place_bits()
    mine = 2 * core + xbit
    width = half_a.shape[3]
    quarter = width // 4
    here = following = None
    for half in (half_a, half_b):
        for d in range(2):
            g = half[d, 2]
            part = dot_t(g, g)
            here = part if here is None else here + part
            part = dot_t(half[d, 3], g)
            following = part if following is None else following + part
    last = lax.axis_index("layer") == lax.axis_size("layer") - 1
    scratch[0] = here
    scratch[1] = jnp.where(last, 0.0, following)
    for i in range(2):
        out[i * quarter : (i + 1) * quarter] = scratch[i, pl.ds(pl.multiple_of(mine * quarter, quarter), quarter), :]


VMEM = pl.BlockSpec(memory_space=pltpu.VMEM)
ANY = pl.BlockSpec(memory_space=pl.ANY)
PARAMS = pltpu.CompilerParams(vmem_limit_bytes=32 * 1024 * 1024)
ALONE = pltpu.CompilerParams(vmem_limit_bytes=60 * 1024 * 1024)


def per_device(layer_inputs, output_grads, input_inverse, grad_inverse):
    maps = layer_inputs[0]
    grads = output_grads[0]
    k_rows = input_inverse[0]
    g_inv = grad_inverse[0]
    side = maps.shape[1]
    width = maps.shape[3]
    group = lax.axis_size("pos")
    rows, full = k_rows.shape
    scale = 1.0 / (maps.shape[0] * maps.shape[1] * maps.shape[2] * group)
    me = lax.axis_index("pos")
    core = me & 1
    xbit = (me >> 1) & 1
    cols = 2 * core + xbit
    zbits = [b for b in (1 << i for i in range(2, 32)) if b < group]
    quarter = width // 4
    flat_maps = maps.reshape(-1, width)
    flat_grads = grads.reshape(-1, width)

    keep, send = pl.pallas_call(
        functools.partial(grad_kernel, side),
        out_shape=[jax.ShapeDtypeStruct((2, quarter, full), F32)] * 2,
        in_specs=[ANY] * 3,
        out_specs=[VMEM] * 2,
        scratch_shapes=[
            pltpu.VMEM((width, full), F32),
            pltpu.VMEM(flat_maps.shape, BF16),
            pltpu.VMEM(flat_grads.shape, BF16),
            pltpu.VMEM(g_inv.shape, F32),
            pltpu.SemaphoreType.DMA((3,)),
        ],
        compiler_params=ALONE,
    )(flat_maps, flat_grads, g_inv)
    h = keep + swap(send, 1)
    k_rows = behind(k_rows, h)
    k_x = swap(k_rows, 2)
    own = behind(jnp.stack([flat_maps, flat_grads]), h)
    next_own = after(own)
    h = h[0] + swap(h[1], 2)
    own, next_own = behind((own, next_own), h)
    two_own = jnp.stack([own[0], next_own[0], own[1], next_own[1]])
    two_x = swap(two_own, 2)
    h = h + swap(h, zbits[0])
    k_rows, k_x = behind((k_rows, k_x), h)
    k_a = jnp.concatenate([k_rows, k_x], axis=0)
    k_b = swap(k_a, 1)
    for b in zbits[1:]:
        h = h + swap(h, b)

    main_a, main_b, p_t = pl.pallas_call(
        functools.partial(precond_kernel, scale),
        out_shape=[jax.ShapeDtypeStruct((quarter, 2 * rows), F32)] * 2
        + [jax.ShapeDtypeStruct((quarter, 4 * rows), BF16)],
        in_specs=[VMEM] * 3,
        out_specs=[VMEM] * 3,
        compiler_params=PARAMS,
    )(h, k_a, k_b)

    two_own, two_x = behind((two_own, two_x), p_t)
    half_a = jnp.stack([two_own, two_x])
    half_b = swap(half_a, 1)

    def by_bit(mine, other, b):
        return jnp.where((me & b) == 0, jnp.concatenate([mine, other], 1), jnp.concatenate([other, mine], 1))

    for b in zbits[:-1]:
        p_t = by_bit(p_t, swap(p_t, b), b)

    half_a, half_b = behind((half_a, half_b), p_t)
    gram = pl.pallas_call(
        gram_kernel,
        out_shape=jax.ShapeDtypeStruct((2 * quarter, width), F32),
        in_specs=[VMEM] * 2,
        out_specs=VMEM,
        scratch_shapes=[pltpu.VMEM((2, width, width), F32)],
        compiler_params=PARAMS,
    )(half_a, half_b)
    low = cols * quarter
    last = lax.axis_index("layer") == lax.axis_size("layer") - 1
    p_same, p_other = behind((after(p_t), after(p_t, zbits[-1])), gram)
    p_t = by_bit(p_same, p_other, zbits[-1])
    p_t = jnp.where(last, jnp.zeros_like(p_t), p_t)

    out_width = full + 2 * width
    cross_t, cross_half = pl.pallas_call(
        functools.partial(cross_kernel, side),
        out_shape=[
            jax.ShapeDtypeStruct((quarter, out_width), F32),
            jax.ShapeDtypeStruct((quarter, out_width + 2 * width), BF16),
        ],
        in_specs=[VMEM] * 4,
        out_specs=[VMEM] * 2,
        compiler_params=PARAMS,
    )(half_a, half_b, p_t, gram)

    place = (jnp.arange(width)[None, :] == low + jnp.arange(quarter)[:, None]).astype(F32)
    main_a, main_b = behind((main_a, main_b), cross_half)
    main = jnp.stack([dot_t(main_a, place, precision=HIGH), dot_t(main_b, place, precision=HIGH)])
    cross_t, gram = cross_t[:, :full], cross_t[:, full:]
    for b in zbits:
        other = swap(cross_half, b).astype(F32)
        cross_t = cross_t + other[:, :full]
        gram = gram + (other[:, full:out_width] + other[:, out_width:])
        high = lax.reduce_precision(gram, 8, 7)
        rest = lax.reduce_precision(gram - high, 8, 7)
        gram = high + rest
        cross_half = jnp.concatenate([cross_t, high, rest], axis=1).astype(BF16)

    out, send = pl.pallas_call(
        functools.partial(update_kernel, scale),
        out_shape=[jax.ShapeDtypeStruct((2, rows, width), F32)] * 2,
        in_specs=[VMEM] * 6,
        out_specs=[VMEM] * 2,
        compiler_params=PARAMS,
    )(cross_t, gram[:, width:], g_inv, k_a, k_b, main)
    gram = behind(gram, out) * scale
    gram = jnp.stack([gram, swap(gram, 2)])
    out = out + swap(send, 2)
    gram = jnp.stack([gram, swap(gram, 1)])
    update = out[0] + swap(out[1], 1)
    gram = jnp.where(xbit == 0, gram, gram[:, ::-1])
    gram = jnp.where(core == 0, gram, gram[::-1])
    gram = gram.reshape(width, 2, width).transpose(1, 2, 0)
    return (update[None], gram[None])


def solution(mesh):
    return jax.shard_map(
        per_device,
        mesh=mesh,
        in_specs=(
            P("layer", "pos", None, None, None),
            P("layer", "pos", None, None, None),
            P("layer", "pos", None),
            P("layer", None, None),
        ),
        out_specs=(P("layer", "pos", None), P("layer", None, None, None)),
        check_vma=False,
    )
```

```python
import functools

import jax
import jax.numpy as jnp
from jax import lax
from jax.experimental import pallas as pl
from jax.experimental.pallas import tpu as pltpu
from jax.sharding import PartitionSpec as P

F32 = jnp.float32
BF16 = jnp.bfloat16
HIGH = lax.Precision.HIGHEST


def behind(block, point):
    return lax.optimization_barrier((block, point))[0]


def after(block, bit=0):
    layers, group = lax.axis_size("layer"), lax.axis_size("pos")
    route = [(((i + 1) % layers) * group + (p ^ bit), i * group + p) for i in range(layers) for p in range(group)]
    return lax.ppermute(block, ("layer", "pos"), route)


def swap(block, bit):
    return lax.ppermute(block, "pos", [(i, i ^ bit) for i in range(lax.axis_size("pos"))])


def dot_t(a, b, **kw):
    return lax.dot_general(a, b, (((0,), (0,)), ((), ())), preferred_element_type=F32, **kw)


def dot_nt(a, b, **kw):
    return lax.dot_general(a, b, (((1,), (1,)), ((), ())), preferred_element_type=F32, **kw)


def shifted(block, dy, dx, side):
    lanes = block.shape[1]
    place = lax.broadcasted_iota(jnp.int32, (1, lanes), 1)
    x = place % side
    y = (place // side) % side
    if dx:
        block = jnp.where((x + dx >= 0) & (x + dx < side), pltpu.roll(block, (-dx) % lanes, 1), 0.0)
    if dy:
        block = jnp.where((y + dy >= 0) & (y + dy < side), pltpu.roll(block, (-dy * side) % lanes, 1), 0.0)
    return block


def taps_to_rows(block, side):
    moved = []
    for r in range(3):
        for s in range(3):
            moved.append(shifted(shifted(block, 0, 1 - s, side), 1 - r, 0, side).astype(BF16))
    return jnp.concatenate(moved, axis=0)


def patches(maps, side):
    count, width = maps.shape
    wide = maps.astype(F32)
    x = lax.broadcasted_iota(jnp.int32, (count, 1), 0) % side
    area = side * side
    edge = jnp.zeros((side, width), BF16)
    columns = []
    for s in range(3):
        moved = maps
        if s != 1:
            inside = (x + (s - 1) >= 0) & (x + (s - 1) < side)
            moved = jnp.where(inside, pltpu.roll(wide, (1 - s) % count, 0), 0.0).astype(BF16)
        columns.append(moved)
    pieces = []
    for r in range(3):
        for s in range(3):
            parts = []
            for first in range(0, count, area):
                image = columns[s][first : first + area]
                if r == 0:
                    parts += [edge, image[: area - side]]
                elif r == 1:
                    parts += [image]
                else:
                    parts += [image[side:], edge]
            pieces.append(jnp.concatenate(parts, axis=0))
    return jnp.concatenate(pieces, axis=1)


def grad_kernel(
    side, maps_in, grads_in, g_in, k_in, keep, send, k_parts, all_rows, maps, grads, g_inv, k_rows, sems
):
    copies = [
        pltpu.make_async_copy(source, target, sems.at[i])
        for i, (source, target) in enumerate(
            [(g_in, g_inv), (grads_in, grads), (maps_in, maps), (k_in, k_rows)]
        )
    ]
    for copy in copies:
        copy.start()
    copies[0].wait()
    copies[1].wait()
    width = maps.shape[1]
    g_t = g_inv[...]
    first = g_t.astype(BF16)
    rest = g_t - first.astype(F32)
    second = rest.astype(BF16)
    third = (rest - second.astype(F32)).astype(BF16)
    g = grads[...]

    def mix(part):
        return lax.dot_general(part, g, (((0,), (1,)), ((), ())), preferred_element_type=F32)

    mixed = mix(first) + (mix(second) + mix(third))
    copies[2].wait()
    both = jnp.dot(two_parts(mixed), patches(maps[...], side), preferred_element_type=F32)
    all_rows[...] = both[:width] + both[width:]
    core, xbit = place_bits()
    mine = 2 * core + xbit
    quarter = width // 4
    for j in range(4):
        block = all_rows[pl.ds(pl.multiple_of((mine ^ j) * quarter, quarter), quarter), :]
        (keep if j < 2 else send)[j % 2] = block
    copies[3].wait()
    k = k_rows[...]
    high = k.astype(BF16)
    k_parts[0] = high
    k_parts[1] = (k - high.astype(F32)).astype(BF16)


def cross_kernel(side, half_a, half_b, precond_t, gram, out, out_half):
    quarter = precond_t.shape[0]
    width = half_a.shape[3]
    full = precond_t.shape[1]
    taps = jnp.concatenate([precond_t[:, t * width : (t + 1) * width] for t in range(9)], axis=0)
    both = None
    for half in (half_a, half_b):
        for d in range(2):
            spread = dot_nt(taps, half[d, 1])
            mapped = None
            for s in range(3):
                column = None
                for r in range(3):
                    low = quarter * (3 * r + s)
                    part = shifted(spread[low : low + quarter], r - 1, 0, side)
                    column = part if column is None else column + part
                column = shifted(column, 0, s - 1, side)
                mapped = column if mapped is None else mapped + column
            mapped = mapped.astype(BF16).astype(F32)
            part = jnp.dot(taps_to_rows(mapped, side), half[d, 0], preferred_element_type=F32)
            both = part if both is None else both + part
    for tap in range(9):
        part = both[quarter * tap : quarter * (tap + 1)]
        out[:, tap * width : (tap + 1) * width] = part
        out_half[:, tap * width : (tap + 1) * width] = part.astype(BF16)
    for i in range(2):
        part = gram[i * quarter : (i + 1) * quarter]
        high = part.astype(BF16)
        rest = (part - high.astype(F32)).astype(BF16)
        low = full + i * width
        out[:, low : low + width] = high.astype(F32) + rest.astype(F32)
        out_half[:, low : low + width] = high
        out_half[:, low + 2 * width : low + 3 * width] = rest


def two_parts(block):
    high = block.astype(BF16)
    return jnp.concatenate([high, (block - high.astype(F32)).astype(BF16)], axis=0)


def place_bits():
    me = lax.axis_index("pos")
    return me & 1, (me >> 1) & 1


def precond_kernel(scale, e_t, k_a, k_b, main_a, main_b, precond_t):
    core, xbit = place_bits()
    count = e_t.shape[0]
    rows = k_a.shape[1] // 2
    parts = two_parts(e_t[...] * scale)
    total = None
    for flip, k, main in ((0, k_a, main_a), (1, k_b, main_b)):
        product = dot_nt(parts, k[0]) + dot_nt(parts, k[1])
        product = product[:count] + product[count:]
        main[...] = product
        source = lax.broadcasted_iota(jnp.int32, (2 * rows, 4 * rows), 0)
        target = lax.broadcasted_iota(jnp.int32, (2 * rows, 4 * rows), 1)
        second = (source >= rows).astype(jnp.int32)
        block = 2 * (xbit ^ second) + (core ^ flip)
        one_hot = (source - second * rows + block * rows == target).astype(F32).astype(BF16)
        placed = jnp.dot(product.astype(BF16), one_hot, preferred_element_type=F32)
        total = placed if total is None else total + placed
    precond_t[...] = total.astype(BF16)


def update_kernel(cross_t, gram, g_inv, k_a, k_b, main, keep, send):
    rows = k_a.shape[1] // 2
    mixed = jnp.dot(gram[...], g_inv[...], precision=HIGH)
    mixed = jnp.concatenate([mixed, mixed], axis=0)
    parts = two_parts(cross_t[...])
    for i, k in enumerate((k_a, k_b)):
        product = dot_nt(k[0], parts) + dot_nt(k[1], parts)
        result = main[i] - jnp.dot(product, mixed, precision=HIGH)
        keep[i] = result[:rows]
        send[i] = result[rows:]


def gram_kernel(half_a, half_b, out, scratch):
    core, xbit = place_bits()
    mine = 2 * core + xbit
    width = half_a.shape[3]
    quarter = width // 4
    here = following = None
    for half in (half_a, half_b):
        for d in range(2):
            g = half[d, 2]
            part = dot_t(g, g)
            here = part if here is None else here + part
            part = dot_t(half[d, 3], g)
            following = part if following is None else following + part
    last = lax.axis_index("layer") == lax.axis_size("layer") - 1
    scratch[0] = here
    scratch[1] = jnp.where(last, 0.0, following)
    for i in range(2):
        out[i * quarter : (i + 1) * quarter] = scratch[i, pl.ds(pl.multiple_of(mine * quarter, quarter), quarter), :]


VMEM = pl.BlockSpec(memory_space=pltpu.VMEM)
HBM = pl.BlockSpec(memory_space=pltpu.HBM)
PARAMS = pltpu.CompilerParams(vmem_limit_bytes=16 * 1024 * 1024)


def per_device(layer_inputs, output_grads, input_inverse, grad_inverse):
    maps = layer_inputs[0]
    grads = output_grads[0]
    k_rows = input_inverse[0]
    g_inv = grad_inverse[0]
    side = maps.shape[1]
    width = maps.shape[3]
    group = lax.axis_size("pos")
    rows, full = k_rows.shape
    scale = 1.0 / (maps.shape[0] * maps.shape[1] * maps.shape[2] * group)
    me = lax.axis_index("pos")
    core = me & 1
    xbit = (me >> 1) & 1
    cols = 2 * core + xbit
    zbits = [b for b in (1 << i for i in range(2, 32)) if b < group]
    quarter = width // 4
    flat_maps = maps.reshape(-1, width)
    flat_grads = grads.reshape(-1, width)

    keep, send, k_own = pl.pallas_call(
        functools.partial(grad_kernel, side),
        out_shape=[jax.ShapeDtypeStruct((2, quarter, full), F32)] * 2
        + [jax.ShapeDtypeStruct((2, rows, full), BF16)],
        in_specs=[HBM] * 4,
        out_specs=[VMEM] * 3,
        scratch_shapes=[
            pltpu.VMEM((width, full), F32),
            pltpu.VMEM(flat_maps.shape, BF16),
            pltpu.VMEM(flat_grads.shape, BF16),
            pltpu.VMEM(g_inv.shape, F32),
            pltpu.VMEM(k_rows.shape, F32),
            pltpu.SemaphoreType.DMA((4,)),
        ],
        compiler_params=PARAMS,
    )(flat_maps, flat_grads, g_inv, k_rows)
    h = keep + swap(send, 1)
    k_own = behind(k_own, h)
    k_x = swap(k_own, 2)
    own = behind(jnp.stack([flat_maps, flat_grads]), h)
    next_own = after(own)
    h = h[0] + swap(h[1], 2)
    own, next_own, k_own = behind((own, next_own, k_own), h)
    two_own = jnp.stack([own[0], next_own[0], own[1], next_own[1]])
    two_x = swap(two_own, 2)
    k_core = swap(k_own, 1)
    h = h + swap(h, zbits[0])
    k_own, k_x = behind((k_own, k_x), h)
    k_a = jnp.concatenate([k_own, k_x], axis=1)
    third = full // 3
    k_pieces = [swap(k_x[:, :, i * third : (i + 1) * third], 1) for i in range(3)]
    k_b = jnp.concatenate([k_core, jnp.concatenate(k_pieces, axis=2)], axis=1)
    for b in zbits[1:]:
        h = h + swap(h, b)

    main_a, main_b, p_t = pl.pallas_call(
        functools.partial(precond_kernel, scale),
        out_shape=[jax.ShapeDtypeStruct((quarter, 2 * rows), F32)] * 2
        + [jax.ShapeDtypeStruct((quarter, 4 * rows), BF16)],
        in_specs=[VMEM] * 3,
        out_specs=[VMEM] * 3,
        compiler_params=PARAMS,
    )(h, k_a, k_b)

    def by_bit(mine, other, b):
        return jnp.where((me & b) == 0, jnp.concatenate([mine, other], 1), jnp.concatenate([other, mine], 1))

    for b in zbits[:-1]:
        p_t = by_bit(p_t, swap(p_t, b), b)

    two_own, two_x = behind((two_own, two_x), p_t)
    half_a = jnp.stack([two_own, two_x])
    half_b = swap(half_a, 1)

    gram = pl.pallas_call(
        gram_kernel,
        out_shape=jax.ShapeDtypeStruct((2 * quarter, width), F32),
        in_specs=[VMEM] * 2,
        out_specs=VMEM,
        scratch_shapes=[pltpu.VMEM((2, width, width), F32)],
        compiler_params=PARAMS,
    )(half_a, half_b)
    low = cols * quarter
    last = lax.axis_index("layer") == lax.axis_size("layer") - 1
    p_same, p_other = behind((after(p_t), after(p_t, zbits[-1])), gram)
    p_t = by_bit(p_same, p_other, zbits[-1])
    p_t = jnp.where(last, jnp.zeros_like(p_t), p_t)

    out_width = full + 2 * width
    cross_t, cross_half = pl.pallas_call(
        functools.partial(cross_kernel, side),
        out_shape=[
            jax.ShapeDtypeStruct((quarter, out_width), F32),
            jax.ShapeDtypeStruct((quarter, out_width + 2 * width), BF16),
        ],
        in_specs=[VMEM] * 4,
        out_specs=[VMEM] * 2,
        compiler_params=PARAMS,
    )(half_a, half_b, p_t, gram)

    place = (jnp.arange(width)[None, :] == low + jnp.arange(quarter)[:, None]).astype(F32)
    main_a, main_b = behind((main_a, main_b), cross_half)
    g_scaled = behind(g_inv, cross_half) * (scale * scale)
    main = jnp.stack([dot_t(main_a, place, precision=HIGH), dot_t(main_b, place, precision=HIGH)])
    cross_t, gram = cross_t[:, :full], cross_t[:, full:]
    for b in zbits:
        other = swap(cross_half, b).astype(F32)
        cross_t = cross_t + other[:, :full]
        gram = gram + (other[:, full:out_width] + other[:, out_width:])
        high = lax.reduce_precision(gram, 8, 7)
        rest = lax.reduce_precision(gram - high, 8, 7)
        gram = high + rest
        cross_half = jnp.concatenate([cross_t, high, rest], axis=1).astype(BF16)

    out, send = pl.pallas_call(
        update_kernel,
        out_shape=[jax.ShapeDtypeStruct((2, rows, width), F32)] * 2,
        in_specs=[VMEM] * 6,
        out_specs=[VMEM] * 2,
        compiler_params=PARAMS,
    )(cross_t, gram[:, width:], g_scaled, k_a, k_b, main)
    gram = behind(gram, out) * scale
    gram = jnp.stack([gram, swap(gram, 2)])
    out = out + swap(send, 2)
    gram = jnp.stack([gram, swap(gram, 1)])
    update = out[0] + swap(out[1], 1)
    gram = jnp.where(xbit == 0, gram, gram[:, ::-1])
    gram = jnp.where(core == 0, gram, gram[::-1])
    gram = gram.reshape(width, 2, width).transpose(1, 2, 0)
    return (update[None], gram[None])


def solution(mesh):
    return jax.shard_map(
        per_device,
        mesh=mesh,
        in_specs=(
            P("layer", "pos", None, None, None),
            P("layer", "pos", None, None, None),
            P("layer", "pos", None),
            P("layer", None, None),
        ),
        out_specs=(P("layer", "pos", None), P("layer", None, None, None)),
        check_vma=False,
    )
```

```python
import functools

import jax
import jax.numpy as jnp
from jax import lax
from jax.experimental import pallas as pl
from jax.experimental.pallas import tpu as pltpu
from jax.sharding import PartitionSpec as P

F32 = jnp.float32
BF16 = jnp.bfloat16
HIGH = lax.Precision.HIGHEST
F16 = jnp.float16
TOP = 13.0


def behind(block, point):
    return lax.optimization_barrier((block, point))[0]


def after(block, bit=0):
    layers, group = lax.axis_size("layer"), lax.axis_size("pos")
    route = [(((i + 1) % layers) * group + (p ^ bit), i * group + p) for i in range(layers) for p in range(group)]
    return lax.ppermute(block, ("layer", "pos"), route)


def swap(block, bit):
    return lax.ppermute(block, "pos", [(i, i ^ bit) for i in range(lax.axis_size("pos"))])


def dot_t(a, b, **kw):
    return lax.dot_general(a, b, (((0,), (0,)), ((), ())), preferred_element_type=F32, **kw)


def dot_nt(a, b, **kw):
    return lax.dot_general(a, b, (((1,), (1,)), ((), ())), preferred_element_type=F32, **kw)


def shifted(block, dy, dx, side):
    lanes = block.shape[1]
    place = lax.broadcasted_iota(jnp.int32, (1, lanes), 1)
    x = place % side
    y = (place // side) % side
    if dx:
        block = jnp.where((x + dx >= 0) & (x + dx < side), pltpu.roll(block, (-dx) % lanes, 1), 0.0)
    if dy:
        block = jnp.where((y + dy >= 0) & (y + dy < side), pltpu.roll(block, (-dy * side) % lanes, 1), 0.0)
    return block


def taps_to_rows(block, side):
    moved = []
    for r in range(3):
        for s in range(3):
            moved.append(shifted(shifted(block, 0, 1 - s, side), 1 - r, 0, side).astype(BF16))
    return jnp.concatenate(moved, axis=0)


def patches(maps, side):
    count, width = maps.shape
    wide = maps.astype(F32)
    x = lax.broadcasted_iota(jnp.int32, (count, 1), 0) % side
    area = side * side
    edge = jnp.zeros((side, width), BF16)
    columns = []
    for s in range(3):
        moved = maps
        if s != 1:
            inside = (x + (s - 1) >= 0) & (x + (s - 1) < side)
            moved = jnp.where(inside, pltpu.roll(wide, (1 - s) % count, 0), 0.0).astype(BF16)
        columns.append(moved)
    pieces = []
    for r in range(3):
        for s in range(3):
            parts = []
            for first in range(0, count, area):
                image = columns[s][first : first + area]
                if r == 0:
                    parts += [edge, image[: area - side]]
                elif r == 1:
                    parts += [image]
                else:
                    parts += [image[side:], edge]
            pieces.append(jnp.concatenate(parts, axis=0))
    return jnp.concatenate(pieces, axis=1)


def exponent(block):
    top = jnp.maximum(jnp.max(jnp.abs(block)), 1e-30)
    return jnp.ceil(jnp.log2(top))


def grad_kernel(
    side, maps_in, grads_in, g_in, k_in, keep, send, k_parts, k_send, all_rows, maps, grads, g_inv, k_rows, sems
):
    copies = [
        pltpu.make_async_copy(source, target, sems.at[i])
        for i, (source, target) in enumerate(
            [(g_in, g_inv), (grads_in, grads), (maps_in, maps), (k_in, k_rows)]
        )
    ]
    for copy in copies:
        copy.start()
    copies[0].wait()
    copies[1].wait()
    width = maps.shape[1]
    g_t = g_inv[...]
    first = g_t.astype(BF16)
    rest = g_t - first.astype(F32)
    second = rest.astype(BF16)
    third = (rest - second.astype(F32)).astype(BF16)
    g = grads[...]

    def mix(part):
        return lax.dot_general(part, g, (((0,), (1,)), ((), ())), preferred_element_type=F32)

    mixed = mix(first) + (mix(second) + mix(third))
    copies[2].wait()
    both = jnp.dot(two_parts(mixed), patches(maps[...], side), preferred_element_type=F32)
    both = both[:width] + both[width:]
    all_rows[...] = both
    core, xbit = place_bits()
    mine = 2 * core + xbit
    quarter = width // 4
    level = jnp.full((quarter, width), exponent(both), F32)
    for j in range(4):
        block = all_rows[pl.ds(pl.multiple_of((mine ^ j) * quarter, quarter), quarter), :]
        target = keep if j < 2 else send
        for tap in range(9):
            target[j % 2, tap] = block[:, tap * width : (tap + 1) * width]
        target[j % 2, 9] = level
    copies[3].wait()
    k = k_rows[...]
    high = k.astype(BF16)
    rest = (k - high.astype(F32)).astype(BF16)
    level = jnp.maximum(exponent(k), -99.0)
    factor = jnp.exp2(jnp.full((1, width), TOP - level, F32))
    for tap in range(9):
        part = slice(tap * width, (tap + 1) * width)
        k_parts[0, tap] = high[:, part]
        k_parts[1, tap] = rest[:, part]
        k_send[tap] = k[:, part] * factor
    k_send[9] = jnp.full((k.shape[0], width), level, F32)


def cross_kernel(side, part_0, part_1, part_2, part_3, precond_t, gram, out, out_half):
    quarter = precond_t.shape[0]
    width = part_0.shape[2]
    full = precond_t.shape[1]
    taps = jnp.concatenate([precond_t[:, t * width : (t + 1) * width] for t in range(9)], axis=0)
    both = None
    for device in (part_0, part_1, part_2, part_3):
        spread = dot_nt(taps, device[1])
        mapped = None
        for s in range(3):
            column = None
            for r in range(3):
                low = quarter * (3 * r + s)
                part = shifted(spread[low : low + quarter], r - 1, 0, side)
                column = part if column is None else column + part
            column = shifted(column, 0, s - 1, side)
            mapped = column if mapped is None else mapped + column
        mapped = mapped.astype(BF16).astype(F32)
        part = jnp.dot(taps_to_rows(mapped, side), device[0], preferred_element_type=F32)
        both = part if both is None else both + part
    for tap in range(9):
        part = both[quarter * tap : quarter * (tap + 1)]
        out[:, tap * width : (tap + 1) * width] = part
        out_half[:, tap * width : (tap + 1) * width] = part.astype(BF16)
    for i in range(2):
        part = gram[i * quarter : (i + 1) * quarter]
        high = part.astype(BF16)
        rest = (part - high.astype(F32)).astype(BF16)
        low = full + i * width
        out[:, low : low + width] = high.astype(F32) + rest.astype(F32)
        out_half[:, low : low + width] = high
        out_half[:, low + 2 * width : low + 3 * width] = rest


def two_parts(block):
    high = block.astype(BF16)
    return jnp.concatenate([high, (block - high.astype(F32)).astype(BF16)], axis=0)


def place_bits():
    me = lax.axis_index("pos")
    return me & 1, (me >> 1) & 1


def taps_to_lanes(block):
    return jnp.concatenate([block[tap] for tap in range(9)], axis=1)


def precond_kernel(scale, e_t, k_a, k_b, main_a, main_b, precond_t):
    core, xbit = place_bits()
    count = e_t.shape[1]
    rows = k_a.shape[2] // 2
    parts = two_parts(taps_to_lanes(e_t) * scale)
    total = None
    for flip, k, main in ((0, k_a, main_a), (1, k_b, main_b)):
        product = dot_nt(parts, taps_to_lanes(k.at[0])) + dot_nt(parts, taps_to_lanes(k.at[1]))
        product = product[:count] + product[count:]
        main[...] = product
        source = lax.broadcasted_iota(jnp.int32, (2 * rows, 4 * rows), 0)
        target = lax.broadcasted_iota(jnp.int32, (2 * rows, 4 * rows), 1)
        second = (source >= rows).astype(jnp.int32)
        block = 2 * (xbit ^ second) + (core ^ flip)
        one_hot = (source - second * rows + block * rows == target).astype(F32).astype(BF16)
        placed = jnp.dot(product.astype(BF16), one_hot, preferred_element_type=F32)
        total = placed if total is None else total + placed
    precond_t[...] = total.astype(BF16)


def update_kernel(cross_t, gram, g_inv, k_a, k_b, main, keep, send):
    rows = k_a.shape[2] // 2
    mixed = jnp.dot(gram[...], g_inv[...], precision=HIGH)
    mixed = jnp.concatenate([mixed, mixed], axis=0)
    parts = two_parts(cross_t[...])
    for i, k in enumerate((k_a, k_b)):
        product = dot_nt(taps_to_lanes(k.at[0]), parts) + dot_nt(taps_to_lanes(k.at[1]), parts)
        result = main[i] - jnp.dot(product, mixed, precision=HIGH)
        keep[i] = result[:rows]
        send[i] = result[rows:]


def gram_kernel(grads, next_grads, keep, send, scratch):
    core, xbit = place_bits()
    mine = 2 * core + xbit
    width = grads.shape[1]
    quarter = width // 4
    g = grads[...]
    last = lax.axis_index("layer") == lax.axis_size("layer") - 1
    scratch[0] = dot_t(g, g)
    scratch[1] = jnp.where(last, 0.0, dot_t(next_grads[...], g))
    for j in range(4):
        for i in range(2):
            (keep if j < 2 else send)[j % 2, i * quarter : (i + 1) * quarter] = scratch[
                i, pl.ds(pl.multiple_of((mine ^ j) * quarter, quarter), quarter), :
            ]


VMEM = pl.BlockSpec(memory_space=pltpu.VMEM)
HBM = pl.BlockSpec(memory_space=pltpu.HBM)
PARAMS = pltpu.CompilerParams(vmem_limit_bytes=16 * 1024 * 1024)


def per_device(layer_inputs, output_grads, input_inverse, grad_inverse):
    maps = layer_inputs[0]
    grads = output_grads[0]
    k_rows = input_inverse[0]
    g_inv = grad_inverse[0]
    side = maps.shape[1]
    width = maps.shape[3]
    group = lax.axis_size("pos")
    rows, full = k_rows.shape
    scale = 1.0 / (maps.shape[0] * maps.shape[1] * maps.shape[2] * group)
    me = lax.axis_index("pos")
    core = me & 1
    xbit = (me >> 1) & 1
    cols = 2 * core + xbit
    zbits = [b for b in (1 << i for i in range(2, 32)) if b < group]
    quarter = width // 4
    flat_maps = maps.reshape(-1, width)
    flat_grads = grads.reshape(-1, width)

    keep, send, k_own, k_send = pl.pallas_call(
        functools.partial(grad_kernel, side),
        out_shape=[jax.ShapeDtypeStruct((2, 10, quarter, width), F32)] * 2
        + [
            jax.ShapeDtypeStruct((2, 9, rows, width), BF16),
            jax.ShapeDtypeStruct((10, rows, width), F32),
        ],
        in_specs=[HBM] * 4,
        out_specs=[VMEM] * 4,
        scratch_shapes=[
            pltpu.VMEM((width, full), F32),
            pltpu.VMEM(flat_maps.shape, BF16),
            pltpu.VMEM(flat_grads.shape, BF16),
            pltpu.VMEM(g_inv.shape, F32),
            pltpu.VMEM(k_rows.shape, F32),
            pltpu.SemaphoreType.DMA((4,)),
        ],
        compiler_params=PARAMS,
    )(flat_maps, flat_grads, g_inv, k_rows)

    def message(values, level):
        level = jnp.maximum(level, -99.0)
        return jnp.concatenate([values * jnp.exp2(TOP - level)[None], level[None]], axis=0).astype(F16)

    def received(parcel):
        parcel = parcel.astype(F32)
        return parcel[:9] * jnp.exp2(parcel[9] - TOP)[None], parcel[9]

    other = swap(send, 1)
    h = keep[:, :9] + other[:, :9]
    level = jnp.maximum(keep[:, 9], other[:, 9]) + 1
    k_half = behind(k_send, h).astype(F16)
    k_others = [swap(k_half, 2), swap(k_half, 1), swap(k_half, 3)]
    own = behind(jnp.stack([flat_maps, flat_grads]), h)
    next_own = after(own)

    def add(values, level, bit):
        more, other_level = received(swap(message(values[1], level[1]) if bit == 2 else message(values, level), bit))
        if bit == 2:
            values, level = values[0], level[0]
        return values + more, jnp.maximum(level, other_level) + 1

    h, level = add(h, level, 2)
    h, level = add(h, level, zbits[0])
    next_own = behind(next_own, h)
    two_own = jnp.stack([flat_maps, next_own[0]])
    two_x = swap(two_own, 2)
    for b in zbits[1:]:
        h, level = add(h, level, b)

    def k_pair(parts):
        return jnp.concatenate(parts, axis=2)

    def k_split(parcel):
        values, _ = received(parcel)
        high = lax.reduce_precision(values, 8, 7)
        return jnp.stack([high, values - high]).astype(BF16)

    k_a = k_pair([k_own, k_split(k_others[0])])
    k_b = k_pair([k_split(k_others[1]), k_split(k_others[2])])

    main_a, main_b, p_t = pl.pallas_call(
        functools.partial(precond_kernel, scale),
        out_shape=[jax.ShapeDtypeStruct((quarter, 2 * rows), F32)] * 2
        + [jax.ShapeDtypeStruct((quarter, 4 * rows), BF16)],
        in_specs=[VMEM] * 3,
        out_specs=[VMEM] * 3,
        compiler_params=PARAMS,
    )(h, k_a, k_b)

    def by_bit(mine, other, b):
        return jnp.where((me & b) == 0, jnp.concatenate([mine, other], 1), jnp.concatenate([other, mine], 1))

    gram_keep, gram_send = pl.pallas_call(
        gram_kernel,
        out_shape=[jax.ShapeDtypeStruct((2, 2 * quarter, width), F32)] * 2,
        in_specs=[VMEM] * 2,
        out_specs=[VMEM] * 2,
        scratch_shapes=[pltpu.VMEM((2, width, width), F32)],
        compiler_params=PARAMS,
    )(flat_grads, next_own[1])
    gram_keep, gram_send, two_own = behind((gram_keep, gram_send, two_own), p_t)
    core_own = swap(two_own, 1)
    gram = gram_keep + swap(gram_send, 1)
    for b in zbits[:-1]:
        p_t = by_bit(p_t, swap(p_t, b), b)

    two_x = behind(two_x, p_t)
    core_x = swap(two_x, 1)
    gram = behind(gram, p_t)
    gram = gram[0] + swap(gram[1], 2)
    low = cols * quarter
    last = lax.axis_index("layer") == lax.axis_size("layer") - 1
    p_t = by_bit(after(p_t), after(p_t, zbits[-1]), zbits[-1])
    p_t = jnp.where(last, jnp.zeros_like(p_t), p_t)

    out_width = full + 2 * width
    cross_t, cross_half = pl.pallas_call(
        functools.partial(cross_kernel, side),
        out_shape=[
            jax.ShapeDtypeStruct((quarter, out_width), F32),
            jax.ShapeDtypeStruct((quarter, out_width + 2 * width), BF16),
        ],
        in_specs=[VMEM] * 6,
        out_specs=[VMEM] * 2,
        compiler_params=PARAMS,
    )(two_own, two_x, core_own, core_x, p_t, gram)

    place = (jnp.arange(width)[None, :] == low + jnp.arange(quarter)[:, None]).astype(F32)
    main_a, main_b = behind((main_a, main_b), cross_half)
    g_scaled = behind(g_inv, cross_half) * (scale * scale)
    main = jnp.stack([dot_t(main_a, place, precision=HIGH), dot_t(main_b, place, precision=HIGH)])
    cross_t, gram = cross_t[:, :full], cross_t[:, full:]
    for b in zbits:
        other = swap(cross_half, b).astype(F32)
        cross_t = cross_t + other[:, :full]
        gram = gram + (other[:, full:out_width] + other[:, out_width:])
        high = lax.reduce_precision(gram, 8, 7)
        rest = lax.reduce_precision(gram - high, 8, 7)
        gram = high + rest
        cross_half = jnp.concatenate([cross_t, high, rest], axis=1).astype(BF16)

    out, send = pl.pallas_call(
        update_kernel,
        out_shape=[jax.ShapeDtypeStruct((2, rows, width), F32)] * 2,
        in_specs=[VMEM] * 6,
        out_specs=[VMEM] * 2,
        compiler_params=PARAMS,
    )(cross_t, gram[:, width:], g_scaled, k_a, k_b, main)
    gram = behind(gram, out) * scale
    gram = jnp.stack([gram, swap(gram, 2)])
    out = out + swap(send, 2)
    gram = jnp.stack([gram, swap(gram, 1)])
    update = out[0] + swap(out[1], 1)
    gram = jnp.where(xbit == 0, gram, gram[:, ::-1])
    gram = jnp.where(core == 0, gram, gram[::-1])
    gram = gram.reshape(width, 2, width).transpose(1, 2, 0)
    return (update[None], gram[None])


def solution(mesh):
    return jax.shard_map(
        per_device,
        mesh=mesh,
        in_specs=(
            P("layer", "pos", None, None, None),
            P("layer", "pos", None, None, None),
            P("layer", "pos", None),
            P("layer", None, None),
        ),
        out_specs=(P("layer", "pos", None), P("layer", None, None, None)),
        check_vma=False,
    )
```

```python
import functools

import jax
import jax.numpy as jnp
from jax import lax
from jax.experimental import pallas as pl
from jax.experimental.pallas import tpu as pltpu
from jax.sharding import PartitionSpec as P

F32 = jnp.float32
BF16 = jnp.bfloat16
HIGH = lax.Precision.HIGHEST
F16 = jnp.float16
TOP = 13.0


def behind(block, point):
    return lax.optimization_barrier((block, point))[0]


def after(block, bit=0):
    layers, group = lax.axis_size("layer"), lax.axis_size("pos")
    route = [(((i + 1) % layers) * group + (p ^ bit), i * group + p) for i in range(layers) for p in range(group)]
    return lax.ppermute(block, ("layer", "pos"), route)


def swap(block, bit):
    return lax.ppermute(block, "pos", [(i, i ^ bit) for i in range(lax.axis_size("pos"))])


def dot_t(a, b, **kw):
    return lax.dot_general(a, b, (((0,), (0,)), ((), ())), preferred_element_type=F32, **kw)


def dot_nt(a, b, **kw):
    return lax.dot_general(a, b, (((1,), (1,)), ((), ())), preferred_element_type=F32, **kw)


def shifted(block, dy, dx, side):
    lanes = block.shape[1]
    place = lax.broadcasted_iota(jnp.int32, (1, lanes), 1)
    x = place % side
    y = (place // side) % side
    if dx:
        block = jnp.where((x + dx >= 0) & (x + dx < side), pltpu.roll(block, (-dx) % lanes, 1), 0.0)
    if dy:
        block = jnp.where((y + dy >= 0) & (y + dy < side), pltpu.roll(block, (-dy * side) % lanes, 1), 0.0)
    return block


def taps_to_rows(block, side):
    moved = []
    for r in range(3):
        for s in range(3):
            moved.append(shifted(shifted(block, 0, 1 - s, side), 1 - r, 0, side).astype(BF16))
    return jnp.concatenate(moved, axis=0)


def patches(maps, side):
    count, width = maps.shape
    wide = maps.astype(F32)
    x = lax.broadcasted_iota(jnp.int32, (count, 1), 0) % side
    area = side * side
    edge = jnp.zeros((side, width), BF16)
    columns = []
    for s in range(3):
        moved = maps
        if s != 1:
            inside = (x + (s - 1) >= 0) & (x + (s - 1) < side)
            moved = jnp.where(inside, pltpu.roll(wide, (1 - s) % count, 0), 0.0).astype(BF16)
        columns.append(moved)
    pieces = []
    for r in range(3):
        for s in range(3):
            parts = []
            for first in range(0, count, area):
                image = columns[s][first : first + area]
                if r == 0:
                    parts += [edge, image[: area - side]]
                elif r == 1:
                    parts += [image]
                else:
                    parts += [image[side:], edge]
            pieces.append(jnp.concatenate(parts, axis=0))
    return jnp.concatenate(pieces, axis=1)


def exponent(block):
    top = jnp.maximum(jnp.max(jnp.abs(block)), 1e-30)
    return jnp.ceil(jnp.log2(top))


def grad_kernel(
    side, maps_in, grads_in, g_in, k_in, keep, send, k_parts, k_send, all_rows, maps, grads, g_inv, k_rows, sems
):
    copies = [
        pltpu.make_async_copy(source, target, sems.at[i])
        for i, (source, target) in enumerate(
            [(g_in, g_inv), (grads_in, grads), (maps_in, maps), (k_in, k_rows)]
        )
    ]
    for copy in copies:
        copy.start()
    copies[0].wait()
    copies[1].wait()
    width = maps.shape[1]
    g_t = g_inv[...]
    first = g_t.astype(BF16)
    rest = g_t - first.astype(F32)
    second = rest.astype(BF16)
    third = (rest - second.astype(F32)).astype(BF16)
    g = grads[...]

    def mix(part):
        return lax.dot_general(part, g, (((0,), (1,)), ((), ())), preferred_element_type=F32)

    mixed = mix(first) + (mix(second) + mix(third))
    copies[2].wait()
    both = jnp.dot(two_parts(mixed), patches(maps[...], side), preferred_element_type=F32)
    both = both[:width] + both[width:]
    all_rows[...] = both
    core, xbit = place_bits()
    mine = 2 * core + xbit
    quarter = width // 4
    level = jnp.full((quarter, width), exponent(both), F32)
    for j in range(4):
        block = all_rows[pl.ds(pl.multiple_of((mine ^ j) * quarter, quarter), quarter), :]
        target = keep if j < 2 else send
        for tap in range(9):
            target[j % 2, tap] = block[:, tap * width : (tap + 1) * width]
        target[j % 2, 9] = level
    copies[3].wait()
    k = k_rows[...]
    high = k.astype(BF16)
    rest = (k - high.astype(F32)).astype(BF16)
    level = jnp.maximum(exponent(k), -99.0)
    factor = jnp.exp2(jnp.full((1, width), TOP - level, F32))
    for tap in range(9):
        part = slice(tap * width, (tap + 1) * width)
        k_parts[0, tap] = high[:, part]
        k_parts[1, tap] = rest[:, part]
        k_send[tap] = k[:, part] * factor
    k_send[9] = jnp.full((k.shape[0], width), level, F32)


def cross_kernel(side, part_0, part_1, part_2, part_3, precond_t, out, out_half):
    quarter = precond_t.shape[0]
    width = part_0.shape[2]
    taps = jnp.concatenate([precond_t[:, t * width : (t + 1) * width] for t in range(9)], axis=0)
    both = None
    for device in (part_0, part_1, part_2, part_3):
        spread = dot_nt(taps, device[1])
        mapped = None
        for s in range(3):
            column = None
            for r in range(3):
                low = quarter * (3 * r + s)
                part = shifted(spread[low : low + quarter], r - 1, 0, side)
                column = part if column is None else column + part
            column = shifted(column, 0, s - 1, side)
            mapped = column if mapped is None else mapped + column
        mapped = mapped.astype(BF16).astype(F32)
        part = jnp.dot(taps_to_rows(mapped, side), device[0], preferred_element_type=F32)
        both = part if both is None else both + part
    for tap in range(9):
        part = both[quarter * tap : quarter * (tap + 1)]
        out[:, tap * width : (tap + 1) * width] = part
        out_half[:, tap * width : (tap + 1) * width] = part.astype(BF16)


def two_parts(block):
    high = block.astype(BF16)
    return jnp.concatenate([high, (block - high.astype(F32)).astype(BF16)], axis=0)


def place_bits():
    me = lax.axis_index("pos")
    return me & 1, (me >> 1) & 1


def taps_to_lanes(block):
    return jnp.concatenate([block[tap] for tap in range(9)], axis=1)


def precond_kernel(scale, e_t, k_a, k_b, main_a, main_b, precond_t):
    core, xbit = place_bits()
    count = e_t.shape[1]
    rows = k_a.shape[2] // 2
    parts = two_parts(taps_to_lanes(e_t) * scale)
    total = None
    for flip, k, main in ((0, k_a, main_a), (1, k_b, main_b)):
        product = dot_nt(parts, taps_to_lanes(k.at[0])) + dot_nt(parts, taps_to_lanes(k.at[1]))
        product = product[:count] + product[count:]
        main[...] = product
        source = lax.broadcasted_iota(jnp.int32, (2 * rows, 4 * rows), 0)
        target = lax.broadcasted_iota(jnp.int32, (2 * rows, 4 * rows), 1)
        second = (source >= rows).astype(jnp.int32)
        block = 2 * (xbit ^ second) + (core ^ flip)
        one_hot = (source - second * rows + block * rows == target).astype(F32).astype(BF16)
        placed = jnp.dot(product.astype(BF16), one_hot, preferred_element_type=F32)
        total = placed if total is None else total + placed
    precond_t[...] = total.astype(BF16)


def update_kernel(cross_t, mixed_in, k_a, k_b, main, keep, send):
    rows = k_a.shape[2] // 2
    mixed = jnp.concatenate([mixed_in[...], mixed_in[...]], axis=0)
    parts = two_parts(cross_t[...])
    for i, k in enumerate((k_a, k_b)):
        product = dot_nt(taps_to_lanes(k.at[0]), parts) + dot_nt(taps_to_lanes(k.at[1]), parts)
        result = main[i] - jnp.dot(product, mixed, precision=HIGH)
        keep[i] = result[:rows]
        send[i] = result[rows:]


def gram_kernel(grads, next_grads, out):
    g = grads[...]
    last = lax.axis_index("layer") == lax.axis_size("layer") - 1
    out[0] = dot_t(g, g)
    out[1] = jnp.where(last, 0.0, dot_t(g, next_grads[...]))


VMEM = pl.BlockSpec(memory_space=pltpu.VMEM)
HBM = pl.BlockSpec(memory_space=pltpu.HBM)
PARAMS = pltpu.CompilerParams(vmem_limit_bytes=16 * 1024 * 1024)


def per_device(layer_inputs, output_grads, input_inverse, grad_inverse):
    maps = layer_inputs[0]
    grads = output_grads[0]
    k_rows = input_inverse[0]
    g_inv = grad_inverse[0]
    side = maps.shape[1]
    width = maps.shape[3]
    group = lax.axis_size("pos")
    rows, full = k_rows.shape
    scale = 1.0 / (maps.shape[0] * maps.shape[1] * maps.shape[2] * group)
    me = lax.axis_index("pos")
    core = me & 1
    xbit = (me >> 1) & 1
    cols = 2 * core + xbit
    zbits = [b for b in (1 << i for i in range(2, 32)) if b < group]
    quarter = width // 4
    flat_maps = maps.reshape(-1, width)
    flat_grads = grads.reshape(-1, width)

    keep, send, k_own, k_send = pl.pallas_call(
        functools.partial(grad_kernel, side),
        out_shape=[jax.ShapeDtypeStruct((2, 10, quarter, width), F32)] * 2
        + [
            jax.ShapeDtypeStruct((2, 9, rows, width), BF16),
            jax.ShapeDtypeStruct((10, rows, width), F32),
        ],
        in_specs=[HBM] * 4,
        out_specs=[VMEM] * 4,
        scratch_shapes=[
            pltpu.VMEM((width, full), F32),
            pltpu.VMEM(flat_maps.shape, BF16),
            pltpu.VMEM(flat_grads.shape, BF16),
            pltpu.VMEM(g_inv.shape, F32),
            pltpu.VMEM(k_rows.shape, F32),
            pltpu.SemaphoreType.DMA((4,)),
        ],
        compiler_params=PARAMS,
    )(*(pltpu.with_memory_space_constraint(a, pltpu.HBM) for a in (flat_maps, flat_grads, g_inv, k_rows)))

    def message(values, level):
        level = jnp.maximum(level, -99.0)
        return jnp.concatenate([values * jnp.exp2(TOP - level)[None], level[None]], axis=0).astype(F16)

    def received(parcel):
        parcel = parcel.astype(F32)
        return parcel[:9] * jnp.exp2(parcel[9] - TOP)[None], parcel[9]

    other = swap(send, 1)
    h = keep[:, :9] + other[:, :9]
    level = jnp.maximum(keep[:, 9], other[:, 9]) + 1
    k_half = behind(k_send, h).astype(F16)
    k_others = [swap(k_half, 2), swap(k_half, 1), swap(k_half, 3)]
    own = behind(jnp.stack([flat_maps, flat_grads]), h)
    next_own = after(own)

    def add(values, level, bit):
        more, other_level = received(swap(message(values[1], level[1]) if bit == 2 else message(values, level), bit))
        if bit == 2:
            values, level = values[0], level[0]
        return values + more, jnp.maximum(level, other_level) + 1

    h, level = add(h, level, 2)
    h, level = add(h, level, zbits[0])
    h, k_others[0], k_others[1] = lax.optimization_barrier((h, k_others[0], k_others[1]))
    next_own = behind(next_own, h)
    two_own = jnp.stack([flat_maps, next_own[0]])
    two_x = swap(two_own, 2)
    for b in zbits[1:]:
        h, level = add(h, level, b)

    def k_pair(parts):
        return jnp.concatenate(parts, axis=2)

    def k_split(parcel):
        values, _ = received(parcel)
        high = lax.reduce_precision(values, 8, 7)
        return jnp.stack([high, values - high]).astype(BF16)

    k_a = k_pair([k_own, k_split(k_others[0])])
    k_b = k_pair([k_split(k_others[1]), k_split(k_others[2])])

    main_a, main_b, p_t = pl.pallas_call(
        functools.partial(precond_kernel, scale),
        out_shape=[jax.ShapeDtypeStruct((quarter, 2 * rows), F32)] * 2
        + [jax.ShapeDtypeStruct((quarter, 4 * rows), BF16)],
        in_specs=[VMEM] * 3,
        out_specs=[VMEM] * 3,
        compiler_params=PARAMS,
    )(h, k_a, k_b)

    def by_bit(mine, other, b):
        return jnp.where((me & b) == 0, jnp.concatenate([mine, other], 1), jnp.concatenate([other, mine], 1))

    gram = pl.pallas_call(
        gram_kernel,
        out_shape=jax.ShapeDtypeStruct((2, width, width), F32),
        in_specs=[VMEM] * 2,
        out_specs=VMEM,
        compiler_params=PARAMS,
    )(flat_grads, next_own[1])
    gram, two_own = behind((gram, two_own), p_t)
    core_own = swap(two_own, 1)
    for b in zbits[:-1]:
        gram = gram + swap(gram, b)
        p_t = by_bit(p_t, swap(p_t, b), b)

    two_x, gram = behind((two_x, gram), p_t)
    core_x = swap(two_x, 1)
    gram = gram + swap(gram, zbits[-1])
    low = cols * quarter
    last = lax.axis_index("layer") == lax.axis_size("layer") - 1
    p_t = by_bit(after(p_t), after(p_t, zbits[-1]), zbits[-1])
    p_t = jnp.where(last, jnp.zeros_like(p_t), p_t)

    cross_t, cross_half = pl.pallas_call(
        functools.partial(cross_kernel, side),
        out_shape=[jax.ShapeDtypeStruct((quarter, full), F32), jax.ShapeDtypeStruct((quarter, full), BF16)],
        in_specs=[VMEM] * 5,
        out_specs=[VMEM] * 2,
        compiler_params=PARAMS,
    )(two_own, two_x, core_own, core_x, p_t)

    gram = behind(gram, cross_half)
    gram = gram + swap(gram, 1)
    place = (jnp.arange(width)[None, :] == low + jnp.arange(quarter)[:, None]).astype(F32)
    main_a, main_b = behind((main_a, main_b), cross_half)
    main = jnp.stack([dot_t(main_a, place, precision=HIGH), dot_t(main_b, place, precision=HIGH)])
    for i, b in enumerate(zbits):
        cross_t = cross_t + swap(cross_half, b).astype(F32)
        cross_half = cross_t.astype(BF16)
        if i == 0:
            gram = behind(gram, cross_half)
            gram = gram + swap(gram, 2)
            mixed = dot_t(gram[1], g_inv, precision=HIGH) * (scale * scale)
            mixed = lax.dynamic_slice_in_dim(mixed, low, quarter, 0)

    out, send = pl.pallas_call(
        update_kernel,
        out_shape=[jax.ShapeDtypeStruct((2, rows, width), F32)] * 2,
        in_specs=[VMEM] * 5,
        out_specs=[VMEM] * 2,
        compiler_params=PARAMS,
    )(cross_t, mixed, k_a, k_b, main)
    out = out + swap(send, 2)
    update = out[0] + swap(out[1], 1)
    return (update[None], (gram * scale)[None])


def solution(mesh):
    return jax.shard_map(
        per_device,
        mesh=mesh,
        in_specs=(
            P("layer", "pos", None, None, None),
            P("layer", "pos", None, None, None),
            P("layer", "pos", None),
            P("layer", None, None),
        ),
        out_specs=(P("layer", "pos", None), P("layer", None, None, None)),
        check_vma=False,
    )
```

```python
import functools

import jax
import jax.numpy as jnp
from jax import lax
from jax.experimental import pallas as pl
from jax.experimental.pallas import tpu as pltpu
from jax.sharding import PartitionSpec as P

F32 = jnp.float32
BF16 = jnp.bfloat16
HIGH = lax.Precision.HIGHEST
F16 = jnp.float16
TOP = 13.0


def behind(block, point):
    return lax.optimization_barrier((block, point))[0]


def after(block, bit=0):
    layers, group = lax.axis_size("layer"), lax.axis_size("pos")
    route = [(((i + 1) % layers) * group + (p ^ bit), i * group + p) for i in range(layers) for p in range(group)]
    return lax.ppermute(block, ("layer", "pos"), route)


def swap(block, bit):
    return lax.ppermute(block, "pos", [(i, i ^ bit) for i in range(lax.axis_size("pos"))])


def dot_t(a, b, **kw):
    return lax.dot_general(a, b, (((0,), (0,)), ((), ())), preferred_element_type=F32, **kw)


def dot_nt(a, b, **kw):
    return lax.dot_general(a, b, (((1,), (1,)), ((), ())), preferred_element_type=F32, **kw)


def shifted(block, dy, dx, side):
    lanes = block.shape[1]
    place = lax.broadcasted_iota(jnp.int32, (1, lanes), 1)
    x = place % side
    y = (place // side) % side
    if dx:
        block = jnp.where((x + dx >= 0) & (x + dx < side), pltpu.roll(block, (-dx) % lanes, 1), 0.0)
    if dy:
        block = jnp.where((y + dy >= 0) & (y + dy < side), pltpu.roll(block, (-dy * side) % lanes, 1), 0.0)
    return block


def taps_to_rows(block, side):
    moved = []
    for r in range(3):
        for s in range(3):
            moved.append(shifted(shifted(block, 0, 1 - s, side), 1 - r, 0, side).astype(BF16))
    return jnp.concatenate(moved, axis=0)


def patches(maps, side):
    count, width = maps.shape
    wide = maps.astype(F32)
    x = lax.broadcasted_iota(jnp.int32, (count, 1), 0) % side
    area = side * side
    edge = jnp.zeros((side, width), BF16)
    columns = []
    for s in range(3):
        moved = maps
        if s != 1:
            inside = (x + (s - 1) >= 0) & (x + (s - 1) < side)
            moved = jnp.where(inside, pltpu.roll(wide, (1 - s) % count, 0), 0.0).astype(BF16)
        columns.append(moved)
    pieces = []
    for r in range(3):
        for s in range(3):
            parts = []
            for first in range(0, count, area):
                image = columns[s][first : first + area]
                if r == 0:
                    parts += [edge, image[: area - side]]
                elif r == 1:
                    parts += [image]
                else:
                    parts += [image[side:], edge]
            pieces.append(jnp.concatenate(parts, axis=0))
    return jnp.concatenate(pieces, axis=1)


def exponent(block):
    top = jnp.maximum(jnp.max(jnp.abs(block)), 1e-30)
    return jnp.ceil(jnp.log2(top))


def grad_kernel(
    side, maps_in, grads_in, g_in, k_in, keep, send, k_parts, k_send, all_rows, maps, grads, g_inv, k_rows, sems
):
    copies = [
        pltpu.make_async_copy(source, target, sems.at[i])
        for i, (source, target) in enumerate(
            [(g_in, g_inv), (grads_in, grads), (maps_in, maps), (k_in, k_rows)]
        )
    ]
    for copy in copies:
        copy.start()
    copies[0].wait()
    copies[1].wait()
    width = maps.shape[1]
    g_t = g_inv[...]
    first = g_t.astype(BF16)
    rest = g_t - first.astype(F32)
    second = rest.astype(BF16)
    third = (rest - second.astype(F32)).astype(BF16)
    g = grads[...]

    def mix(part):
        return lax.dot_general(part, g, (((0,), (1,)), ((), ())), preferred_element_type=F32)

    mixed = mix(first) + (mix(second) + mix(third))
    copies[2].wait()
    both = jnp.dot(two_parts(mixed), patches(maps[...], side), preferred_element_type=F32)
    both = both[:width] + both[width:]
    all_rows[...] = both
    core, xbit = place_bits()
    mine = 2 * core + xbit
    quarter = width // 4
    level = jnp.full((quarter, width), exponent(both), F32)
    for j in range(4):
        block = all_rows[pl.ds(pl.multiple_of((mine ^ j) * quarter, quarter), quarter), :]
        target = keep if j < 2 else send
        for tap in range(9):
            target[j % 2, tap] = block[:, tap * width : (tap + 1) * width]
        target[j % 2, 9] = level
    copies[3].wait()
    k = k_rows[...]
    high = k.astype(BF16)
    rest = (k - high.astype(F32)).astype(BF16)
    level = jnp.maximum(exponent(k), -99.0)
    factor = jnp.exp2(jnp.full((1, width), TOP - level, F32))
    for tap in range(9):
        part = slice(tap * width, (tap + 1) * width)
        k_parts[0, tap] = high[:, part]
        k_parts[1, tap] = rest[:, part]
        k_send[tap] = k[:, part] * factor
    k_send[9] = jnp.full((k.shape[0], width), level, F32)


def cross_kernel(side, part_0, part_1, part_2, part_3, precond_t, out, out_half):
    quarter = precond_t.shape[0]
    width = part_0.shape[2]
    taps = jnp.concatenate([precond_t[:, t * width : (t + 1) * width] for t in range(9)], axis=0)
    both = None
    for device in (part_0, part_1, part_2, part_3):
        spread = dot_nt(taps, device[1])
        mapped = None
        for s in range(3):
            column = None
            for r in range(3):
                low = quarter * (3 * r + s)
                part = shifted(spread[low : low + quarter], r - 1, 0, side)
                column = part if column is None else column + part
            column = shifted(column, 0, s - 1, side)
            mapped = column if mapped is None else mapped + column
        mapped = mapped.astype(BF16).astype(F32)
        part = jnp.dot(taps_to_rows(mapped, side), device[0], preferred_element_type=F32)
        both = part if both is None else both + part
    for tap in range(9):
        part = both[quarter * tap : quarter * (tap + 1)]
        out[:, tap * width : (tap + 1) * width] = part
        out_half[:, tap * width : (tap + 1) * width] = part.astype(BF16)


def two_parts(block):
    high = block.astype(BF16)
    return jnp.concatenate([high, (block - high.astype(F32)).astype(BF16)], axis=0)


def place_bits():
    me = lax.axis_index("pos")
    return me & 1, (me >> 1) & 1


def taps_to_lanes(block):
    return jnp.concatenate([block[tap] for tap in range(9)], axis=1)


def precond_kernel(scale, e_t, k_a, k_b, main_a, main_b, precond_t):
    core, xbit = place_bits()
    count = e_t.shape[1]
    rows = k_a.shape[2] // 2
    parts = two_parts(taps_to_lanes(e_t) * scale)
    total = None
    for flip, k, main in ((0, k_a, main_a), (1, k_b, main_b)):
        product = dot_nt(parts, taps_to_lanes(k.at[0])) + dot_nt(parts, taps_to_lanes(k.at[1]))
        product = product[:count] + product[count:]
        main[...] = product
        source = lax.broadcasted_iota(jnp.int32, (2 * rows, 4 * rows), 0)
        target = lax.broadcasted_iota(jnp.int32, (2 * rows, 4 * rows), 1)
        second = (source >= rows).astype(jnp.int32)
        block = 2 * (xbit ^ second) + (core ^ flip)
        one_hot = (source - second * rows + block * rows == target).astype(F32).astype(BF16)
        placed = jnp.dot(product.astype(BF16), one_hot, preferred_element_type=F32)
        total = placed if total is None else total + placed
    precond_t[...] = total.astype(BF16)


def update_kernel(cross_t, mixed_in, k_a, k_b, main, keep, send):
    rows = k_a.shape[2] // 2
    mixed = jnp.concatenate([mixed_in[...], mixed_in[...]], axis=0)
    parts = two_parts(cross_t[...])
    for i, k in enumerate((k_a, k_b)):
        product = dot_nt(taps_to_lanes(k.at[0]), parts) + dot_nt(taps_to_lanes(k.at[1]), parts)
        result = main[i] - jnp.dot(product, mixed, precision=HIGH)
        keep[i] = result[:rows]
        send[i] = result[rows:]


def gram_kernel(grads, next_grads, *refs):
    outs, scratch = refs[:4], refs[4]
    core, xbit = place_bits()
    mine = 2 * core + xbit
    width = grads.shape[1]
    quarter = width // 4
    g = grads[...]
    last = lax.axis_index("layer") == lax.axis_size("layer") - 1
    scratch[0] = dot_t(g, g)
    scratch[1] = jnp.where(last, 0.0, dot_t(next_grads[...], g))
    for j in range(4):
        for i in range(2):
            outs[j][i * quarter : (i + 1) * quarter] = scratch[
                i, pl.ds(pl.multiple_of((mine ^ j) * quarter, quarter), quarter), :
            ]


VMEM = pl.BlockSpec(memory_space=pltpu.VMEM)
HBM = pl.BlockSpec(memory_space=pltpu.HBM)
PARAMS = pltpu.CompilerParams(vmem_limit_bytes=16 * 1024 * 1024)


def per_device(layer_inputs, output_grads, input_inverse, grad_inverse):
    maps = layer_inputs[0]
    grads = output_grads[0]
    k_rows = input_inverse[0]
    g_inv = grad_inverse[0]
    side = maps.shape[1]
    width = maps.shape[3]
    group = lax.axis_size("pos")
    rows, full = k_rows.shape
    scale = 1.0 / (maps.shape[0] * maps.shape[1] * maps.shape[2] * group)
    me = lax.axis_index("pos")
    core = me & 1
    xbit = (me >> 1) & 1
    cols = 2 * core + xbit
    zbits = [b for b in (1 << i for i in range(2, 32)) if b < group]
    quarter = width // 4
    flat_maps = maps.reshape(-1, width)
    flat_grads = grads.reshape(-1, width)

    keep, send, k_own, k_send = pl.pallas_call(
        functools.partial(grad_kernel, side),
        out_shape=[jax.ShapeDtypeStruct((2, 10, quarter, width), F32)] * 2
        + [
            jax.ShapeDtypeStruct((2, 9, rows, width), BF16),
            jax.ShapeDtypeStruct((10, rows, width), F32),
        ],
        in_specs=[HBM] * 4,
        out_specs=[VMEM] * 4,
        scratch_shapes=[
            pltpu.VMEM((width, full), F32),
            pltpu.VMEM(flat_maps.shape, BF16),
            pltpu.VMEM(flat_grads.shape, BF16),
            pltpu.VMEM(g_inv.shape, F32),
            pltpu.VMEM(k_rows.shape, F32),
            pltpu.SemaphoreType.DMA((4,)),
        ],
        compiler_params=PARAMS,
    )(*(pltpu.with_memory_space_constraint(a, pltpu.HBM) for a in (flat_maps, flat_grads, g_inv, k_rows)))

    def message(values, level):
        level = jnp.maximum(level, -99.0)
        return jnp.concatenate([values * jnp.exp2(TOP - level)[None], level[None]], axis=0).astype(F16)

    def received(parcel):
        parcel = parcel.astype(F32)
        return parcel[:9] * jnp.exp2(parcel[9] - TOP)[None], parcel[9]

    other = swap(send, 1)
    h = keep[:, :9] + other[:, :9]
    level = jnp.maximum(keep[:, 9], other[:, 9]) + 1
    k_half = behind(k_send, h).astype(F16)
    k_others = [swap(k_half, 2), swap(k_half, 1), swap(k_half, 3)]
    own = behind(jnp.stack([flat_maps, flat_grads]), h)
    next_own = after(own)

    def add(values, level, bit):
        more, other_level = received(swap(message(values[1], level[1]) if bit == 2 else message(values, level), bit))
        if bit == 2:
            values, level = values[0], level[0]
        return values + more, jnp.maximum(level, other_level) + 1

    h, level = add(h, level, 2)
    h, level = add(h, level, zbits[0])
    next_own = behind(next_own, h)
    two_own = jnp.stack([flat_maps, next_own[0]])
    two_x = swap(two_own, 2)
    for b in zbits[1:]:
        h, level = add(h, level, b)

    def k_pair(parts):
        return jnp.concatenate(parts, axis=2)

    def k_split(parcel):
        values, _ = received(parcel)
        high = lax.reduce_precision(values, 8, 7)
        return jnp.stack([high, values - high]).astype(BF16)

    k_a = k_pair([k_own, k_split(k_others[0])])
    k_b = k_pair([k_split(k_others[1]), k_split(k_others[2])])

    main_a, main_b, p_t = pl.pallas_call(
        functools.partial(precond_kernel, scale),
        out_shape=[jax.ShapeDtypeStruct((quarter, 2 * rows), F32)] * 2
        + [jax.ShapeDtypeStruct((quarter, 4 * rows), BF16)],
        in_specs=[VMEM] * 3,
        out_specs=[VMEM] * 3,
        compiler_params=PARAMS,
    )(h, k_a, k_b)

    def by_bit(mine, other, b):
        return jnp.where((me & b) == 0, jnp.concatenate([mine, other], 1), jnp.concatenate([other, mine], 1))

    grams = pl.pallas_call(
        gram_kernel,
        out_shape=[jax.ShapeDtypeStruct((2 * quarter, width), F32)] * 4,
        in_specs=[VMEM] * 2,
        out_specs=[VMEM] * 4,
        scratch_shapes=[pltpu.VMEM((2, width, width), F32)],
        compiler_params=PARAMS,
    )(flat_grads, next_own[1])
    grams = behind(grams, p_t)
    grams = [grams[0]] + [swap(grams[j], bits) for j, bits in ((1, 2), (2, 1), (3, 3))]
    for b in zbits[:-1]:
        p_t = by_bit(p_t, swap(p_t, b), b)

    two_own, two_x, grams = behind((two_own, two_x, grams), p_t)
    core_own = swap(two_own, 1)
    core_x = swap(two_x, 1)
    gram = (grams[0] + grams[1]) + (grams[2] + grams[3])
    for b in zbits[:-1]:
        gram = gram + swap(gram, b)
    low = cols * quarter
    last = lax.axis_index("layer") == lax.axis_size("layer") - 1
    p_t = by_bit(after(p_t), after(p_t, zbits[-1]), zbits[-1])
    p_t = jnp.where(last, jnp.zeros_like(p_t), p_t)

    cross_t, cross_half = pl.pallas_call(
        functools.partial(cross_kernel, side),
        out_shape=[jax.ShapeDtypeStruct((quarter, full), F32), jax.ShapeDtypeStruct((quarter, full), BF16)],
        in_specs=[VMEM] * 5,
        out_specs=[VMEM] * 2,
        compiler_params=PARAMS,
    )(two_own, two_x, core_own, core_x, p_t)

    gram = behind(gram, cross_half)
    gram = gram + swap(gram, zbits[-1])
    place = (jnp.arange(width)[None, :] == low + jnp.arange(quarter)[:, None]).astype(F32)
    main_a, main_b = behind((main_a, main_b), cross_half)
    main = jnp.stack([dot_t(main_a, place, precision=HIGH), dot_t(main_b, place, precision=HIGH)])
    for i, b in enumerate(zbits):
        cross_t = cross_t + swap(cross_half, b).astype(F32)
        cross_half = cross_t.astype(BF16)
        if i == 0:
            gram = behind(gram, cross_half)
            mixed = jnp.dot(gram[quarter:], g_inv, precision=HIGH) * (scale * scale)
            grams = [gram] + [swap(gram, bits) for bits in (2, 1, 3)]

    out, send = pl.pallas_call(
        update_kernel,
        out_shape=[jax.ShapeDtypeStruct((2, rows, width), F32)] * 2,
        in_specs=[VMEM] * 5,
        out_specs=[VMEM] * 2,
        compiler_params=PARAMS,
    )(cross_t, mixed, k_a, k_b, main)
    out = out + swap(send, 2)
    update = out[0] + swap(out[1], 1)

    grams = jnp.stack(behind(grams, out)).reshape(2, 2, 2, quarter, width) * scale
    grams = jnp.where(xbit == 0, grams, grams[:, ::-1])
    grams = jnp.where(core == 0, grams, grams[::-1])
    grams = grams.transpose(2, 4, 0, 1, 3).reshape(2, width, width)
    return (update[None], grams[None])


def solution(mesh):
    return jax.shard_map(
        per_device,
        mesh=mesh,
        in_specs=(
            P("layer", "pos", None, None, None),
            P("layer", "pos", None, None, None),
            P("layer", "pos", None),
            P("layer", None, None),
        ),
        out_specs=(P("layer", "pos", None), P("layer", None, None, None)),
        check_vma=False,
    )
```

```python
import functools

import jax
import jax.numpy as jnp
from jax import lax
from jax.experimental import pallas as pl
from jax.experimental.pallas import tpu as pltpu
from jax.sharding import PartitionSpec as P

F32 = jnp.float32
BF16 = jnp.bfloat16
HIGH = lax.Precision.HIGHEST
F16 = jnp.float16
TOP = 13.0


def behind(block, point):
    return lax.optimization_barrier((block, point))[0]


def after(block, bit=0):
    layers, group = lax.axis_size("layer"), lax.axis_size("pos")
    route = [(((i + 1) % layers) * group + (p ^ bit), i * group + p) for i in range(layers) for p in range(group)]
    return lax.ppermute(block, ("layer", "pos"), route)


def swap(block, bit):
    return lax.ppermute(block, "pos", [(i, i ^ bit) for i in range(lax.axis_size("pos"))])


def dot_t(a, b, **kw):
    return lax.dot_general(a, b, (((0,), (0,)), ((), ())), preferred_element_type=F32, **kw)


def dot_nt(a, b, **kw):
    return lax.dot_general(a, b, (((1,), (1,)), ((), ())), preferred_element_type=F32, **kw)


def shifted(block, dy, dx, side):
    lanes = block.shape[1]
    place = lax.broadcasted_iota(jnp.int32, (1, lanes), 1)
    x = place % side
    y = (place // side) % side
    if dx:
        block = jnp.where((x + dx >= 0) & (x + dx < side), pltpu.roll(block, (-dx) % lanes, 1), 0.0)
    if dy:
        block = jnp.where((y + dy >= 0) & (y + dy < side), pltpu.roll(block, (-dy * side) % lanes, 1), 0.0)
    return block


def taps_to_rows(block, side):
    moved = []
    for r in range(3):
        for s in range(3):
            moved.append(shifted(shifted(block, 0, 1 - s, side), 1 - r, 0, side).astype(BF16))
    return jnp.concatenate(moved, axis=0)


def patches(maps, side):
    count, width = maps.shape
    wide = maps.astype(F32)
    x = lax.broadcasted_iota(jnp.int32, (count, 1), 0) % side
    area = side * side
    edge = jnp.zeros((side, width), BF16)
    columns = []
    for s in range(3):
        moved = maps
        if s != 1:
            inside = (x + (s - 1) >= 0) & (x + (s - 1) < side)
            moved = jnp.where(inside, pltpu.roll(wide, (1 - s) % count, 0), 0.0).astype(BF16)
        columns.append(moved)
    pieces = []
    for r in range(3):
        for s in range(3):
            parts = []
            for first in range(0, count, area):
                image = columns[s][first : first + area]
                if r == 0:
                    parts += [edge, image[: area - side]]
                elif r == 1:
                    parts += [image]
                else:
                    parts += [image[side:], edge]
            pieces.append(jnp.concatenate(parts, axis=0))
    return jnp.concatenate(pieces, axis=1)


def exponent(block):
    top = jnp.maximum(jnp.max(jnp.abs(block)), 1e-30)
    return jnp.ceil(jnp.log2(top))


def grad_kernel(
    side, maps_in, grads_in, g_in, k_in, keep, send, k_parts, k_send, all_rows, maps, grads, g_inv, k_rows, sems
):
    copies = [
        pltpu.make_async_copy(source, target, sems.at[i])
        for i, (source, target) in enumerate(
            [(g_in, g_inv), (grads_in, grads), (maps_in, maps), (k_in, k_rows)]
        )
    ]
    for copy in copies:
        copy.start()
    copies[0].wait()
    copies[1].wait()
    width = maps.shape[1]
    g_t = g_inv[...]
    first = g_t.astype(BF16)
    rest = g_t - first.astype(F32)
    second = rest.astype(BF16)
    third = (rest - second.astype(F32)).astype(BF16)
    g = grads[...]

    def mix(part):
        return lax.dot_general(part, g, (((0,), (1,)), ((), ())), preferred_element_type=F32)

    mixed = mix(first) + (mix(second) + mix(third))
    copies[2].wait()
    both = jnp.dot(two_parts(mixed), patches(maps[...], side), preferred_element_type=F32)
    both = both[:width] + both[width:]
    all_rows[...] = both
    core, xbit = place_bits()
    mine = 2 * core + xbit
    quarter = width // 4
    level = jnp.full((8, width), exponent(both), F32)
    for j in range(4):
        block = all_rows[pl.ds(pl.multiple_of((mine ^ j) * quarter, quarter), quarter), :]
        target = keep if j < 2 else send
        for tap in range(9):
            target[j % 2, tap * quarter : (tap + 1) * quarter] = block[:, tap * width : (tap + 1) * width]
        target[j % 2, 9 * quarter :] = level
    copies[3].wait()
    k = k_rows[...]
    high = k.astype(BF16)
    rest = (k - high.astype(F32)).astype(BF16)
    level = jnp.maximum(exponent(k), -99.0)
    factor = jnp.exp2(jnp.full((1, width), TOP - level, F32))
    rows = k.shape[0]
    for tap in range(9):
        part = slice(tap * width, (tap + 1) * width)
        k_parts[0, tap] = high[:, part]
        k_parts[1, tap] = rest[:, part]
        k_send[tap * rows : (tap + 1) * rows] = k[:, part] * factor
    k_send[9 * rows :] = jnp.full((8, width), level, F32)


def cross_kernel(side, part_0, part_1, part_2, part_3, precond_t, gram_0, gram_1, gram_2, gram_3, out, gram, levels):
    quarter = precond_t.shape[0]
    width = part_0.shape[2]
    taps = jnp.concatenate([precond_t[:, t * width : (t + 1) * width] for t in range(9)], axis=0)
    both = None
    for device in (part_0, part_1, part_2, part_3):
        spread = dot_nt(taps, device[1])
        mapped = None
        for s in range(3):
            column = None
            for r in range(3):
                low = quarter * (3 * r + s)
                part = shifted(spread[low : low + quarter], r - 1, 0, side)
                column = part if column is None else column + part
            column = shifted(column, 0, s - 1, side)
            mapped = column if mapped is None else mapped + column
        mapped = mapped.astype(BF16).astype(F32)
        part = jnp.dot(taps_to_rows(mapped, side), device[0], preferred_element_type=F32)
        both = part if both is None else both + part
    out[...] = both
    grams = (gram_0[...] + gram_1[...]) + (gram_2[...] + gram_3[...])
    gram[...] = grams
    levels[0] = jnp.full((8, width), exponent(both), F32)
    levels[1] = jnp.full((8, width), exponent(grams), F32)


def two_parts(block):
    high = block.astype(BF16)
    return jnp.concatenate([high, (block - high.astype(F32)).astype(BF16)], axis=0)


def place_bits():
    me = lax.axis_index("pos")
    return me & 1, (me >> 1) & 1


def taps_to_lanes(block):
    return jnp.concatenate([block[tap] for tap in range(9)], axis=1)


def rows_to_lanes(block):
    count = block.shape[0] // 9
    return jnp.concatenate([block[tap * count : (tap + 1) * count] for tap in range(9)], axis=1)


def precond_kernel(scale, e_t, k_a, k_b, main_a, main_b, precond_t):
    core, xbit = place_bits()
    count = e_t.shape[0] // 9
    rows = k_a.shape[2] // 2
    parts = two_parts(rows_to_lanes(e_t) * scale)
    total = None
    for flip, k, main in ((0, k_a, main_a), (1, k_b, main_b)):
        product = dot_nt(parts, taps_to_lanes(k.at[0])) + dot_nt(parts, taps_to_lanes(k.at[1]))
        product = product[:count] + product[count:]
        main[...] = product
        source = lax.broadcasted_iota(jnp.int32, (2 * rows, 4 * rows), 0)
        target = lax.broadcasted_iota(jnp.int32, (2 * rows, 4 * rows), 1)
        second = (source >= rows).astype(jnp.int32)
        block = 2 * (xbit ^ second) + (core ^ flip)
        one_hot = (source - second * rows + block * rows == target).astype(F32).astype(BF16)
        placed = jnp.dot(product.astype(BF16), one_hot, preferred_element_type=F32)
        total = placed if total is None else total + placed
    precond_t[...] = total.astype(BF16)


def update_kernel(cross_t, mixed_in, k_a, k_b, main, gram, keep, send):
    rows = k_a.shape[2] // 2
    mixed = jnp.concatenate([mixed_in[...], mixed_in[...]], axis=0)
    parts = two_parts(rows_to_lanes(cross_t))
    for i, k in enumerate((k_a, k_b)):
        product = dot_nt(taps_to_lanes(k.at[0]), parts) + dot_nt(taps_to_lanes(k.at[1]), parts)
        result = main[i] - jnp.dot(product, mixed, precision=HIGH)
        keep[i] = result[:rows]
        send[i * rows : (i + 1) * rows] = result[rows:]
    send[2 * rows :] = gram[...]


def gram_kernel(grads, next_grads, *refs):
    outs, scratch = refs[:4], refs[4]
    core, xbit = place_bits()
    mine = 2 * core + xbit
    width = grads.shape[1]
    quarter = width // 4
    g = grads[...]
    last = lax.axis_index("layer") == lax.axis_size("layer") - 1
    scratch[0] = dot_t(g, g)
    scratch[1] = jnp.where(last, 0.0, dot_t(next_grads[...], g))
    for j in range(4):
        for i in range(2):
            outs[j][i * quarter : (i + 1) * quarter] = scratch[
                i, pl.ds(pl.multiple_of((mine ^ j) * quarter, quarter), quarter), :
            ]


VMEM = pl.BlockSpec(memory_space=pltpu.VMEM)
HBM = pl.BlockSpec(memory_space=pltpu.HBM)
PARAMS = pltpu.CompilerParams(vmem_limit_bytes=16 * 1024 * 1024)


def per_device(layer_inputs, output_grads, input_inverse, grad_inverse):
    maps = layer_inputs[0]
    grads = output_grads[0]
    k_rows = input_inverse[0]
    g_inv = grad_inverse[0]
    side = maps.shape[1]
    width = maps.shape[3]
    group = lax.axis_size("pos")
    rows, full = k_rows.shape
    scale = 1.0 / (maps.shape[0] * maps.shape[1] * maps.shape[2] * group)
    me = lax.axis_index("pos")
    core = me & 1
    xbit = (me >> 1) & 1
    cols = 2 * core + xbit
    zbits = [b for b in (1 << i for i in range(2, 32)) if b < group]
    quarter = width // 4
    flat_maps = maps.reshape(-1, width)
    flat_grads = grads.reshape(-1, width)

    keep, send, k_own, k_send = pl.pallas_call(
        functools.partial(grad_kernel, side),
        out_shape=[jax.ShapeDtypeStruct((2, 9 * quarter + 8, width), F32)] * 2
        + [
            jax.ShapeDtypeStruct((2, 9, rows, width), BF16),
            jax.ShapeDtypeStruct((9 * rows + 8, width), F32),
        ],
        in_specs=[HBM] * 4,
        out_specs=[VMEM] * 4,
        scratch_shapes=[
            pltpu.VMEM((width, full), F32),
            pltpu.VMEM(flat_maps.shape, BF16),
            pltpu.VMEM(flat_grads.shape, BF16),
            pltpu.VMEM(g_inv.shape, F32),
            pltpu.VMEM(k_rows.shape, F32),
            pltpu.SemaphoreType.DMA((4,)),
        ],
        compiler_params=PARAMS,
    )(*(pltpu.with_memory_space_constraint(a, pltpu.HBM) for a in (flat_maps, flat_grads, g_inv, k_rows)))

    def packed(groups):
        groups = [(values, jnp.maximum(level, -99.0)) for values, level in groups]
        scaled = [lax.reduce_precision(values * jnp.exp2(TOP - level[:1]), 5, 10) for values, level in groups]
        return jnp.concatenate(scaled + [level for _, level in groups], axis=0)

    def opened(parcel, sizes):
        parcel = parcel.astype(F32)
        groups = []
        start, at = 0, sum(sizes)
        for size in sizes:
            level = parcel[at : at + 8]
            groups.append((parcel[start : start + size] * jnp.exp2(level[:1] - TOP), level))
            start, at = start + size, at + 8
        return groups

    def summed(values, level, sent, bit):
        (more, other_level), = opened(swap(packed([sent]).astype(F16), bit), [9 * quarter])
        return values + more, jnp.maximum(level, other_level) + 1

    wide = 9 * quarter
    other = swap(send, 1)
    h = keep[:, :wide] + other[:, :wide]
    level = jnp.maximum(keep[:, wide:], other[:, wide:]) + 1
    k_half = behind(k_send, h).astype(F16)
    k_others = [swap(k_half, 2), swap(k_half, 1), swap(k_half, 3)]
    h, level = summed(h[0], level[0], (h[1], level[1]), 2)
    h, level = summed(h, level, (h, level), zbits[0])
    own = behind(jnp.stack([flat_maps, flat_grads]), h)
    next_own = after(own)
    two_own = jnp.stack([flat_maps, next_own[0]])
    for b in zbits[1:]:
        h, level = summed(h, level, (h, level), b)

    def k_pair(parts):
        return jnp.concatenate(parts, axis=2)

    def k_split(parcel):
        (values, _), = opened(parcel, [9 * rows])
        values = values.reshape(9, rows, width)
        high = lax.reduce_precision(values, 8, 7)
        return jnp.stack([high, values - high]).astype(BF16)

    k_a = k_pair([k_own, k_split(k_others[0])])
    k_b = k_pair([k_split(k_others[1]), k_split(k_others[2])])

    main_a, main_b, p_t = pl.pallas_call(
        functools.partial(precond_kernel, scale),
        out_shape=[jax.ShapeDtypeStruct((quarter, 2 * rows), F32)] * 2
        + [jax.ShapeDtypeStruct((quarter, 4 * rows), BF16)],
        in_specs=[VMEM] * 3,
        out_specs=[VMEM] * 3,
        compiler_params=PARAMS,
    )(h, k_a, k_b)

    def by_bit(mine, other, b):
        return jnp.where((me & b) == 0, jnp.concatenate([mine, other], 1), jnp.concatenate([other, mine], 1))

    two_x = swap(behind(two_own, p_t), 2)
    grams = pl.pallas_call(
        gram_kernel,
        out_shape=[jax.ShapeDtypeStruct((2 * quarter, width), F32)] * 4,
        in_specs=[VMEM] * 2,
        out_specs=[VMEM] * 4,
        scratch_shapes=[pltpu.VMEM((2, width, width), F32)],
        compiler_params=PARAMS,
    )(flat_grads, next_own[1])
    grams = behind(grams, p_t)
    grams = [grams[0]] + [swap(grams[j], bits) for j, bits in ((1, 2), (2, 1), (3, 3))]
    for b in zbits[:-1]:
        p_t = by_bit(p_t, swap(p_t, b), b)

    two_own, two_x = behind((two_own, two_x), p_t)
    core_own = swap(two_own, 1)
    core_x = swap(two_x, 1)
    low = cols * quarter
    last = lax.axis_index("layer") == lax.axis_size("layer") - 1
    p_t = by_bit(after(p_t), after(p_t, zbits[-1]), zbits[-1])
    p_t = jnp.where(last, jnp.zeros_like(p_t), p_t)

    cross_t, gram, levels = pl.pallas_call(
        functools.partial(cross_kernel, side),
        out_shape=[
            jax.ShapeDtypeStruct((wide, width), F32),
            jax.ShapeDtypeStruct((2 * quarter, width), F32),
            jax.ShapeDtypeStruct((2, 8, width), F32),
        ],
        in_specs=[VMEM] * 9,
        out_specs=[VMEM] * 3,
        compiler_params=PARAMS,
    )(two_own, two_x, core_own, core_x, p_t, *grams)

    place = (jnp.arange(width)[None, :] == low + jnp.arange(quarter)[:, None]).astype(F32)
    main_a, main_b = behind((main_a, main_b), cross_t)
    main = jnp.stack([dot_t(main_a, place, precision=HIGH), dot_t(main_b, place, precision=HIGH)])
    sizes = [wide, 2 * quarter]
    cross_level, gram_level = levels[0], levels[1]
    for b in zbits:
        mine = packed([(cross_t, cross_level), (gram, gram_level)])
        (more, level), (more_gram, level_gram) = opened(swap(mine.astype(F16), b), sizes)
        cross_t = cross_t + more
        gram = opened(mine, sizes)[1][0] + more_gram
        cross_level = jnp.maximum(cross_level, level) + 1
        gram_level = jnp.maximum(gram_level, level_gram) + 1
    mixed = jnp.dot(gram[quarter:], g_inv, precision=HIGH) * (scale * scale)

    out, send = pl.pallas_call(
        update_kernel,
        out_shape=[
            jax.ShapeDtypeStruct((2, rows, width), F32),
            jax.ShapeDtypeStruct((2 * rows + 2 * quarter, width), F32),
        ],
        in_specs=[VMEM] * 6,
        out_specs=[VMEM] * 2,
        compiler_params=PARAMS,
    )(cross_t, mixed, k_a, k_b, main, gram)
    other = swap(send, 2)
    keep = out[0] + other[:rows]
    send = jnp.concatenate([out[1] + other[rows : 2 * rows], gram, other[2 * rows :]], axis=0)
    other = swap(send, 1)
    update = keep + other[:rows]
    grams = jnp.concatenate([send[rows:], other[rows:]], axis=0)

    grams = grams.reshape(2, 2, 2, quarter, width) * scale
    grams = jnp.where(xbit == 0, grams, grams[:, ::-1])
    grams = jnp.where(core == 0, grams, grams[::-1])
    grams = grams.transpose(2, 4, 0, 1, 3).reshape(2, width, width)
    return (update[None], grams[None])


def solution(mesh):
    return jax.shard_map(
        per_device,
        mesh=mesh,
        in_specs=(
            P("layer", "pos", None, None, None),
            P("layer", "pos", None, None, None),
            P("layer", "pos", None),
            P("layer", None, None),
        ),
        out_specs=(P("layer", "pos", None), P("layer", None, None, None)),
        check_vma=False,
    )
```

```python
import functools

import jax
import jax.numpy as jnp
from jax import lax
from jax.experimental import pallas as pl
from jax.experimental.pallas import tpu as pltpu
from jax.sharding import PartitionSpec as P

F32 = jnp.float32
BF16 = jnp.bfloat16
HIGH = lax.Precision.HIGHEST
F16 = jnp.float16
TOP = 13.0


def behind(block, point):
    return lax.optimization_barrier((block, point))[0]


def after(block, bit=0):
    layers, group = lax.axis_size("layer"), lax.axis_size("pos")
    route = [(((i + 1) % layers) * group + (p ^ bit), i * group + p) for i in range(layers) for p in range(group)]
    return lax.ppermute(block, ("layer", "pos"), route)


def swap(block, bit):
    return lax.ppermute(block, "pos", [(i, i ^ bit) for i in range(lax.axis_size("pos"))])


def dot_t(a, b, **kw):
    return lax.dot_general(a, b, (((0,), (0,)), ((), ())), preferred_element_type=F32, **kw)


def dot_nt(a, b, **kw):
    return lax.dot_general(a, b, (((1,), (1,)), ((), ())), preferred_element_type=F32, **kw)


def shifted(block, dy, dx, side):
    lanes = block.shape[1]
    place = lax.broadcasted_iota(jnp.int32, (1, lanes), 1)
    x = place % side
    y = (place // side) % side
    if dx:
        block = jnp.where((x + dx >= 0) & (x + dx < side), pltpu.roll(block, (-dx) % lanes, 1), 0.0)
    if dy:
        block = jnp.where((y + dy >= 0) & (y + dy < side), pltpu.roll(block, (-dy * side) % lanes, 1), 0.0)
    return block


def taps_to_rows(block, side):
    moved = []
    for r in range(3):
        for s in range(3):
            moved.append(shifted(shifted(block, 0, 1 - s, side), 1 - r, 0, side).astype(BF16))
    return jnp.concatenate(moved, axis=0)


def patches(maps, side):
    count, width = maps.shape
    wide = maps.astype(F32)
    x = lax.broadcasted_iota(jnp.int32, (count, 1), 0) % side
    area = side * side
    edge = jnp.zeros((side, width), BF16)
    columns = []
    for s in range(3):
        moved = maps
        if s != 1:
            inside = (x + (s - 1) >= 0) & (x + (s - 1) < side)
            moved = jnp.where(inside, pltpu.roll(wide, (1 - s) % count, 0), 0.0).astype(BF16)
        columns.append(moved)
    pieces = []
    for r in range(3):
        for s in range(3):
            parts = []
            for first in range(0, count, area):
                image = columns[s][first : first + area]
                if r == 0:
                    parts += [edge, image[: area - side]]
                elif r == 1:
                    parts += [image]
                else:
                    parts += [image[side:], edge]
            pieces.append(jnp.concatenate(parts, axis=0))
    return jnp.concatenate(pieces, axis=1)


def exponent(block):
    top = jnp.maximum(jnp.max(jnp.abs(block)), 1e-30)
    return jnp.ceil(jnp.log2(top))


def grad_kernel(
    side, maps_in, grads_in, g_in, k_in, keep, send, k_parts, all_rows, maps, grads, g_inv, k_rows, sems
):
    copies = [
        pltpu.make_async_copy(source, target, sems.at[i])
        for i, (source, target) in enumerate(
            [(g_in, g_inv), (grads_in, grads), (maps_in, maps), (k_in, k_rows)]
        )
    ]
    for copy in copies:
        copy.start()
    copies[0].wait()
    copies[1].wait()
    width = maps.shape[1]
    g_t = g_inv[...]
    first = g_t.astype(BF16)
    rest = g_t - first.astype(F32)
    second = rest.astype(BF16)
    third = (rest - second.astype(F32)).astype(BF16)
    g = grads[...]

    def mix(part):
        return lax.dot_general(part, g, (((0,), (1,)), ((), ())), preferred_element_type=F32)

    mixed = mix(first) + (mix(second) + mix(third))
    copies[2].wait()
    both = jnp.dot(two_parts(mixed), patches(maps[...], side), preferred_element_type=F32)
    both = both[:width] + both[width:]
    all_rows[...] = both
    core, xbit = place_bits()
    mine = 2 * core + xbit
    quarter = width // 4
    level = jnp.maximum(exponent(both), -99.0)
    factor = jnp.exp2(jnp.full((1, width), TOP - level, F32))
    level = jnp.full((8, width), level, F32)
    size = 9 * quarter + 8
    for j in range(4):
        block = all_rows[pl.ds(pl.multiple_of((mine ^ j) * quarter, quarter), quarter), :]
        for tap in range(9):
            part = block[:, tap * width : (tap + 1) * width]
            if j < 2:
                keep[j, tap * quarter : (tap + 1) * quarter] = part
            else:
                low = (j - 2) * size + tap * quarter
                send[low : low + quarter] = part * factor
        if j < 2:
            keep[j, size - 8 :] = level
        else:
            send[(j - 1) * size - 8 : (j - 1) * size] = level
    copies[3].wait()
    k = k_rows[...]
    high = k.astype(BF16)
    rest = (k - high.astype(F32)).astype(BF16)
    level = jnp.maximum(exponent(k), -99.0)
    factor = jnp.exp2(jnp.full((1, width), TOP - level, F32))
    rows = k.shape[0]
    for tap in range(9):
        part = slice(tap * width, (tap + 1) * width)
        k_parts[0, tap] = high[:, part]
        k_parts[1, tap] = rest[:, part]
        low = 2 * size + tap * rows
        send[low : low + rows] = k[:, part] * factor
    send[2 * size + 9 * rows :] = jnp.full((8, width), level, F32)


def cross_kernel(side, part_0, part_1, part_2, part_3, precond_t, gram_0, gram_1, gram_2, gram_3, out, gram, levels):
    quarter = precond_t.shape[0]
    width = part_0.shape[2]
    taps = jnp.concatenate([precond_t[:, t * width : (t + 1) * width] for t in range(9)], axis=0)
    both = None
    for device in (part_0, part_1, part_2, part_3):
        spread = dot_nt(taps, device[1])
        mapped = None
        for s in range(3):
            column = None
            for r in range(3):
                low = quarter * (3 * r + s)
                part = shifted(spread[low : low + quarter], r - 1, 0, side)
                column = part if column is None else column + part
            column = shifted(column, 0, s - 1, side)
            mapped = column if mapped is None else mapped + column
        mapped = mapped.astype(BF16).astype(F32)
        part = jnp.dot(taps_to_rows(mapped, side), device[0], preferred_element_type=F32)
        both = part if both is None else both + part
    out[...] = both
    grams = (gram_0[...] + gram_1[...]) + (gram_2[...] + gram_3[...])
    gram[...] = grams
    levels[0] = jnp.full((8, width), exponent(both), F32)
    levels[1] = jnp.full((8, width), exponent(grams), F32)


def two_parts(block):
    high = block.astype(BF16)
    return jnp.concatenate([high, (block - high.astype(F32)).astype(BF16)], axis=0)


def place_bits():
    me = lax.axis_index("pos")
    return me & 1, (me >> 1) & 1


def taps_to_lanes(block):
    return jnp.concatenate([block[tap] for tap in range(9)], axis=1)


def rows_to_lanes(block):
    count = block.shape[0] // 9
    return jnp.concatenate([block[tap * count : (tap + 1) * count] for tap in range(9)], axis=1)


def precond_kernel(scale, e_t, k_a, k_b, main_a, main_b, precond_t):
    core, xbit = place_bits()
    count = e_t.shape[0] // 9
    rows = k_a.shape[2] // 2
    parts = two_parts(rows_to_lanes(e_t) * scale)
    total = None
    for flip, k, main in ((0, k_a, main_a), (1, k_b, main_b)):
        product = dot_nt(parts, taps_to_lanes(k.at[0])) + dot_nt(parts, taps_to_lanes(k.at[1]))
        product = product[:count] + product[count:]
        main[...] = product
        source = lax.broadcasted_iota(jnp.int32, (2 * rows, 4 * rows), 0)
        target = lax.broadcasted_iota(jnp.int32, (2 * rows, 4 * rows), 1)
        second = (source >= rows).astype(jnp.int32)
        block = 2 * (xbit ^ second) + (core ^ flip)
        one_hot = (source - second * rows + block * rows == target).astype(F32).astype(BF16)
        placed = jnp.dot(product.astype(BF16), one_hot, preferred_element_type=F32)
        total = placed if total is None else total + placed
    precond_t[...] = total.astype(BF16)


def update_kernel(cross_t, mixed_in, k_a, k_b, main, gram, keep, send):
    rows = k_a.shape[2] // 2
    mixed = jnp.concatenate([mixed_in[...], mixed_in[...]], axis=0)
    parts = two_parts(rows_to_lanes(cross_t))
    for i, k in enumerate((k_a, k_b)):
        product = dot_nt(taps_to_lanes(k.at[0]), parts) + dot_nt(taps_to_lanes(k.at[1]), parts)
        result = main[i] - jnp.dot(product, mixed, precision=HIGH)
        keep[i] = result[:rows]
        send[i * rows : (i + 1) * rows] = result[rows:]
    send[2 * rows :] = gram[...]


def finish_kernel(scale, keep, mine, other, update, grams, scratch):
    core, xbit = place_bits()
    first = 2 * core + xbit
    rows, width = update.shape
    quarter = width // 4
    update[...] = keep[...] + other[:rows]
    for j in range(4):
        source = mine if j < 2 else other
        for i in range(2):
            low = rows + 2 * quarter * (j % 2) + i * quarter
            place = pl.ds(pl.multiple_of((first ^ j) * quarter, quarter), quarter)
            scratch[i, place, :] = source[low : low + quarter] * scale
    grams[0] = scratch[0]
    grams[1] = scratch[1].T


def gram_kernel(grads, next_grads, *refs):
    outs, scratch = refs[:4], refs[4]
    core, xbit = place_bits()
    mine = 2 * core + xbit
    width = grads.shape[1]
    quarter = width // 4
    g = grads[...]
    last = lax.axis_index("layer") == lax.axis_size("layer") - 1
    scratch[0] = dot_t(g, g)
    scratch[1] = jnp.where(last, 0.0, dot_t(next_grads[...], g))
    for j in range(4):
        for i in range(2):
            outs[j][i * quarter : (i + 1) * quarter] = scratch[
                i, pl.ds(pl.multiple_of((mine ^ j) * quarter, quarter), quarter), :
            ]


VMEM = pl.BlockSpec(memory_space=pltpu.VMEM)
HBM = pl.BlockSpec(memory_space=pltpu.HBM)
PARAMS = pltpu.CompilerParams(vmem_limit_bytes=16 * 1024 * 1024)


def per_device(layer_inputs, output_grads, input_inverse, grad_inverse):
    maps = layer_inputs[0]
    grads = output_grads[0]
    k_rows = input_inverse[0]
    g_inv = grad_inverse[0]
    side = maps.shape[1]
    width = maps.shape[3]
    group = lax.axis_size("pos")
    rows, full = k_rows.shape
    scale = 1.0 / (maps.shape[0] * maps.shape[1] * maps.shape[2] * group)
    me = lax.axis_index("pos")
    core = me & 1
    xbit = (me >> 1) & 1
    cols = 2 * core + xbit
    zbits = [b for b in (1 << i for i in range(2, 32)) if b < group]
    quarter = width // 4
    flat_maps = maps.reshape(-1, width)
    flat_grads = grads.reshape(-1, width)

    wide = 9 * quarter
    keep, send, k_own = pl.pallas_call(
        functools.partial(grad_kernel, side),
        out_shape=[
            jax.ShapeDtypeStruct((2, wide + 8, width), F32),
            jax.ShapeDtypeStruct((2 * (wide + 8) + 9 * rows + 8, width), F32),
            jax.ShapeDtypeStruct((2, 9, rows, width), BF16),
        ],
        in_specs=[HBM] * 4,
        out_specs=[VMEM] * 3,
        scratch_shapes=[
            pltpu.VMEM((width, full), F32),
            pltpu.VMEM(flat_maps.shape, BF16),
            pltpu.VMEM(flat_grads.shape, BF16),
            pltpu.VMEM(g_inv.shape, F32),
            pltpu.VMEM(k_rows.shape, F32),
            pltpu.SemaphoreType.DMA((4,)),
        ],
        compiler_params=PARAMS,
    )(*(pltpu.with_memory_space_constraint(a, pltpu.HBM) for a in (flat_maps, flat_grads, g_inv, k_rows)))

    def packed(groups):
        groups = [(values, jnp.maximum(level, -99.0)) for values, level in groups]
        scaled = [lax.reduce_precision(values * jnp.exp2(TOP - level[:1]), 5, 10) for values, level in groups]
        return jnp.concatenate(scaled + [level for _, level in groups], axis=0)

    def opened(parcel, sizes):
        parcel = parcel.astype(F32)
        groups = []
        start, at = 0, sum(sizes)
        for size in sizes:
            level = parcel[at : at + 8]
            groups.append((parcel[start : start + size] * jnp.exp2(level[:1] - TOP), level))
            start, at = start + size, at + 8
        return groups

    def summed(values, level, sent, bit):
        (more, other_level), = opened(swap(packed([sent]).astype(F16), bit), [9 * quarter])
        return values + more, jnp.maximum(level, other_level) + 1

    sent = send.astype(F16)
    other = swap(sent, 1)
    e_rows = 2 * (wide + 8)
    h, level = [], []
    for j in range(2):
        (more, other_level), = opened(other[j * (wide + 8) : (j + 1) * (wide + 8)], [wide])
        h.append(keep[j, :wide] + more)
        level.append(jnp.maximum(keep[j, wide:], other_level) + 1)
    k_core = other[e_rows:]
    k_sent = jnp.concatenate(behind((sent[e_rows:], k_core), h[0]), axis=0)
    k_x, k_diagonal = jnp.split(swap(k_sent, 2), 2, axis=0)
    own = behind(jnp.stack([flat_maps, flat_grads]), h[0])
    next_own = after(own)
    h, level = summed(h[0], level[0], (h[1], level[1]), 2)
    h, level = summed(h, level, (h, level), zbits[0])
    next_own = behind(next_own, h)
    two_own = jnp.stack([flat_maps, next_own[0]])
    two_x = swap(two_own, 2)
    for b in zbits[1:]:
        h, level = summed(h, level, (h, level), b)

    def k_pair(parts):
        return jnp.concatenate(parts, axis=2)

    def k_split(parcel):
        (values, _), = opened(parcel, [9 * rows])
        values = values.reshape(9, rows, width)
        high = lax.reduce_precision(values, 8, 7)
        return jnp.stack([high, values - high]).astype(BF16)

    k_a = k_pair([k_own, k_split(k_x)])
    k_b = k_pair([k_split(k_core), k_split(k_diagonal)])

    main_a, main_b, p_t = pl.pallas_call(
        functools.partial(precond_kernel, scale),
        out_shape=[jax.ShapeDtypeStruct((quarter, 2 * rows), F32)] * 2
        + [jax.ShapeDtypeStruct((quarter, 4 * rows), BF16)],
        in_specs=[VMEM] * 3,
        out_specs=[VMEM] * 3,
        compiler_params=PARAMS,
    )(h, k_a, k_b)

    def by_bit(mine, other, b):
        return jnp.where((me & b) == 0, jnp.concatenate([mine, other], 1), jnp.concatenate([other, mine], 1))

    grams = pl.pallas_call(
        gram_kernel,
        out_shape=[jax.ShapeDtypeStruct((2 * quarter, width), F32)] * 4,
        in_specs=[VMEM] * 2,
        out_specs=[VMEM] * 4,
        scratch_shapes=[pltpu.VMEM((2, width, width), F32)],
        compiler_params=PARAMS,
    )(flat_grads, next_own[1])
    grams = behind(grams, p_t)
    grams = [grams[0]] + [swap(grams[j], bits) for j, bits in ((1, 2), (2, 1), (3, 3))]
    for b in zbits[:-1]:
        p_t = by_bit(p_t, swap(p_t, b), b)

    two_own, two_x = behind((two_own, two_x), p_t)
    core_own = swap(two_own, 1)
    core_x = swap(two_x, 1)
    low = cols * quarter
    last = lax.axis_index("layer") == lax.axis_size("layer") - 1
    p_t = by_bit(after(p_t), after(p_t, zbits[-1]), zbits[-1])
    p_t = jnp.where(last, jnp.zeros_like(p_t), p_t)

    cross_t, gram, levels = pl.pallas_call(
        functools.partial(cross_kernel, side),
        out_shape=[
            jax.ShapeDtypeStruct((wide, width), F32),
            jax.ShapeDtypeStruct((2 * quarter, width), F32),
            jax.ShapeDtypeStruct((2, 8, width), F32),
        ],
        in_specs=[VMEM] * 9,
        out_specs=[VMEM] * 3,
        compiler_params=PARAMS,
    )(two_own, two_x, core_own, core_x, p_t, *grams)

    place = (jnp.arange(width)[None, :] == low + jnp.arange(quarter)[:, None]).astype(F32)
    main_a, main_b = behind((main_a, main_b), cross_t)
    main = jnp.stack([dot_t(main_a, place, precision=HIGH), dot_t(main_b, place, precision=HIGH)])
    sizes = [wide, 2 * quarter]
    cross_level, gram_level = levels[0], levels[1]
    for b in zbits:
        mine = packed([(cross_t, cross_level), (gram, gram_level)])
        (more, level), (more_gram, level_gram) = opened(swap(mine.astype(F16), b), sizes)
        cross_t = cross_t + more
        gram = opened(mine, sizes)[1][0] + more_gram
        cross_level = jnp.maximum(cross_level, level) + 1
        gram_level = jnp.maximum(gram_level, level_gram) + 1
    mixed = jnp.dot(gram[quarter:], g_inv, precision=HIGH) * (scale * scale)

    out, send = pl.pallas_call(
        update_kernel,
        out_shape=[
            jax.ShapeDtypeStruct((2, rows, width), F32),
            jax.ShapeDtypeStruct((2 * rows + 2 * quarter, width), F32),
        ],
        in_specs=[VMEM] * 6,
        out_specs=[VMEM] * 2,
        compiler_params=PARAMS,
    )(cross_t, mixed, k_a, k_b, main, gram)
    other = swap(send, 2)
    keep = out[0] + other[:rows]
    send = jnp.concatenate([out[1] + other[rows : 2 * rows], gram, other[2 * rows :]], axis=0)
    update, grams = pl.pallas_call(
        functools.partial(finish_kernel, scale),
        out_shape=[jax.ShapeDtypeStruct((rows, width), F32), jax.ShapeDtypeStruct((2, width, width), F32)],
        in_specs=[VMEM] * 3,
        out_specs=[VMEM] * 2,
        scratch_shapes=[pltpu.VMEM((2, width, width), F32)],
        compiler_params=PARAMS,
    )(keep, send, swap(send, 1))
    return (update[None], grams[None])


def solution(mesh):
    return jax.shard_map(
        per_device,
        mesh=mesh,
        in_specs=(
            P("layer", "pos", None, None, None),
            P("layer", "pos", None, None, None),
            P("layer", "pos", None),
            P("layer", None, None),
        ),
        out_specs=(P("layer", "pos", None), P("layer", None, None, None)),
        check_vma=False,
    )
```

```python
import functools

import jax
import jax.numpy as jnp
from jax import lax
from jax.experimental import pallas as pl
from jax.experimental.pallas import tpu as pltpu
from jax.sharding import PartitionSpec as P

F32 = jnp.float32
BF16 = jnp.bfloat16
HIGH = lax.Precision.HIGHEST
F16 = jnp.float16
TOP = 13.0


def behind(block, point):
    return lax.optimization_barrier((block, point))[0]


def after(block, bit=0):
    layers, group = lax.axis_size("layer"), lax.axis_size("pos")
    route = [(((i + 1) % layers) * group + (p ^ bit), i * group + p) for i in range(layers) for p in range(group)]
    return lax.ppermute(block, ("layer", "pos"), route)


def swap(block, bit):
    return lax.ppermute(block, "pos", [(i, i ^ bit) for i in range(lax.axis_size("pos"))])


def dot_t(a, b, **kw):
    return lax.dot_general(a, b, (((0,), (0,)), ((), ())), preferred_element_type=F32, **kw)


def dot_nt(a, b, **kw):
    return lax.dot_general(a, b, (((1,), (1,)), ((), ())), preferred_element_type=F32, **kw)


def shifted(block, dy, dx, side):
    lanes = block.shape[1]
    place = lax.broadcasted_iota(jnp.int32, (1, lanes), 1)
    x = place % side
    y = (place // side) % side
    if dx:
        block = jnp.where((x + dx >= 0) & (x + dx < side), pltpu.roll(block, (-dx) % lanes, 1), 0.0)
    if dy:
        block = jnp.where((y + dy >= 0) & (y + dy < side), pltpu.roll(block, (-dy * side) % lanes, 1), 0.0)
    return block


def taps_to_rows(block, side):
    moved = []
    for r in range(3):
        for s in range(3):
            moved.append(shifted(shifted(block, 0, 1 - s, side), 1 - r, 0, side).astype(BF16))
    return jnp.concatenate(moved, axis=0)


def patches(maps, side):
    count, width = maps.shape
    wide = maps.astype(F32)
    x = lax.broadcasted_iota(jnp.int32, (count, 1), 0) % side
    area = side * side
    edge = jnp.zeros((side, width), BF16)
    columns = []
    for s in range(3):
        moved = maps
        if s != 1:
            inside = (x + (s - 1) >= 0) & (x + (s - 1) < side)
            moved = jnp.where(inside, pltpu.roll(wide, (1 - s) % count, 0), 0.0).astype(BF16)
        columns.append(moved)
    pieces = []
    for r in range(3):
        for s in range(3):
            parts = []
            for first in range(0, count, area):
                image = columns[s][first : first + area]
                if r == 0:
                    parts += [edge, image[: area - side]]
                elif r == 1:
                    parts += [image]
                else:
                    parts += [image[side:], edge]
            pieces.append(jnp.concatenate(parts, axis=0))
    return jnp.concatenate(pieces, axis=1)


def exponent(block):
    top = jnp.maximum(jnp.max(jnp.abs(block)), 1e-30)
    return jnp.ceil(jnp.log2(top))


def grad_kernel(
    side, maps_in, grads_in, g_in, k_in, keep, send, k_parts, k_send, all_rows, maps, grads, g_inv, k_rows, sems
):
    copies = [
        pltpu.make_async_copy(source, target, sems.at[i])
        for i, (source, target) in enumerate(
            [(g_in, g_inv), (grads_in, grads), (maps_in, maps), (k_in, k_rows)]
        )
    ]
    for copy in copies:
        copy.start()
    copies[0].wait()
    copies[1].wait()
    width = maps.shape[1]
    g_t = g_inv[...]
    first = g_t.astype(BF16)
    rest = g_t - first.astype(F32)
    second = rest.astype(BF16)
    third = (rest - second.astype(F32)).astype(BF16)
    g = grads[...]

    def mix(part):
        return lax.dot_general(part, g, (((0,), (1,)), ((), ())), preferred_element_type=F32)

    mixed = mix(first) + (mix(second) + mix(third))
    copies[2].wait()
    both = jnp.dot(two_parts(mixed), patches(maps[...], side), preferred_element_type=F32)
    both = both[:width] + both[width:]
    all_rows[...] = both
    core, xbit = place_bits()
    mine = 2 * core + xbit
    quarter = width // 4
    level = jnp.full((quarter, width), exponent(both), F32)
    for j in range(4):
        block = all_rows[pl.ds(pl.multiple_of((mine ^ j) * quarter, quarter), quarter), :]
        target = keep if j < 2 else send
        for tap in range(9):
            target[j % 2, tap] = block[:, tap * width : (tap + 1) * width]
        target[j % 2, 9] = level
    copies[3].wait()
    k = k_rows[...]
    high = k.astype(BF16)
    rest = (k - high.astype(F32)).astype(BF16)
    level = jnp.maximum(exponent(k), -99.0)
    factor = jnp.exp2(jnp.full((1, width), TOP - level, F32))
    for tap in range(9):
        part = slice(tap * width, (tap + 1) * width)
        k_parts[0, tap] = high[:, part]
        k_parts[1, tap] = rest[:, part]
        k_send[tap] = k[:, part] * factor
    k_send[9] = jnp.full((k.shape[0], width), level, F32)


def cross_kernel(side, part_0, part_1, part_2, part_3, precond_t, gram, out, out_half):
    quarter = precond_t.shape[0]
    width = part_0.shape[2]
    full = precond_t.shape[1]
    taps = jnp.concatenate([precond_t[:, t * width : (t + 1) * width] for t in range(9)], axis=0)
    both = None
    for device in (part_0, part_1, part_2, part_3):
        spread = dot_nt(taps, device[1])
        mapped = None
        for s in range(3):
            column = None
            for r in range(3):
                low = quarter * (3 * r + s)
                part = shifted(spread[low : low + quarter], r - 1, 0, side)
                column = part if column is None else column + part
            column = shifted(column, 0, s - 1, side)
            mapped = column if mapped is None else mapped + column
        mapped = mapped.astype(BF16).astype(F32)
        part = jnp.dot(taps_to_rows(mapped, side), device[0], preferred_element_type=F32)
        both = part if both is None else both + part
    for tap in range(9):
        part = both[quarter * tap : quarter * (tap + 1)]
        out[:, tap * width : (tap + 1) * width] = part
        out_half[:, tap * width : (tap + 1) * width] = part.astype(BF16)
    for i in range(2):
        part = gram[i * quarter : (i + 1) * quarter]
        high = part.astype(BF16)
        rest = (part - high.astype(F32)).astype(BF16)
        low = full + i * width
        out[:, low : low + width] = high.astype(F32) + rest.astype(F32)
        out_half[:, low : low + width] = high
        out_half[:, low + 2 * width : low + 3 * width] = rest


def two_parts(block):
    high = block.astype(BF16)
    return jnp.concatenate([high, (block - high.astype(F32)).astype(BF16)], axis=0)


def place_bits():
    me = lax.axis_index("pos")
    return me & 1, (me >> 1) & 1


def taps_to_lanes(block):
    return jnp.concatenate([block[tap] for tap in range(9)], axis=1)


def precond_kernel(scale, e_t, k_a, k_b, main_a, main_b, precond_t):
    core, xbit = place_bits()
    count = e_t.shape[1]
    rows = k_a.shape[2] // 2
    parts = two_parts(taps_to_lanes(e_t) * scale)
    total = None
    for flip, k, main in ((0, k_a, main_a), (1, k_b, main_b)):
        product = dot_nt(parts, taps_to_lanes(k.at[0])) + dot_nt(parts, taps_to_lanes(k.at[1]))
        product = product[:count] + product[count:]
        main[...] = product
        source = lax.broadcasted_iota(jnp.int32, (2 * rows, 4 * rows), 0)
        target = lax.broadcasted_iota(jnp.int32, (2 * rows, 4 * rows), 1)
        second = (source >= rows).astype(jnp.int32)
        block = 2 * (xbit ^ second) + (core ^ flip)
        one_hot = (source - second * rows + block * rows == target).astype(F32).astype(BF16)
        placed = jnp.dot(product.astype(BF16), one_hot, preferred_element_type=F32)
        total = placed if total is None else total + placed
    precond_t[...] = total.astype(BF16)


def update_kernel(cross_t, gram, g_inv, k_a, k_b, main, keep, send):
    rows = k_a.shape[2] // 2
    mixed = jnp.dot(gram[...], g_inv[...], precision=HIGH)
    mixed = jnp.concatenate([mixed, mixed], axis=0)
    parts = two_parts(cross_t[...])
    for i, k in enumerate((k_a, k_b)):
        product = dot_nt(taps_to_lanes(k.at[0]), parts) + dot_nt(taps_to_lanes(k.at[1]), parts)
        result = main[i] - jnp.dot(product, mixed, precision=HIGH)
        keep[i] = result[:rows]
        send[i] = result[rows:]


def gram_kernel(grads, next_grads, keep, send, scratch):
    core, xbit = place_bits()
    mine = 2 * core + xbit
    width = grads.shape[1]
    quarter = width // 4
    g = grads[...]
    last = lax.axis_index("layer") == lax.axis_size("layer") - 1
    scratch[0] = dot_t(g, g)
    scratch[1] = jnp.where(last, 0.0, dot_t(next_grads[...], g))
    for j in range(4):
        for i in range(2):
            (keep if j < 2 else send)[j % 2, i * quarter : (i + 1) * quarter] = scratch[
                i, pl.ds(pl.multiple_of((mine ^ j) * quarter, quarter), quarter), :
            ]


VMEM = pl.BlockSpec(memory_space=pltpu.VMEM)
HBM = pl.BlockSpec(memory_space=pltpu.HBM)
PARAMS = pltpu.CompilerParams(vmem_limit_bytes=16 * 1024 * 1024)


def per_device(layer_inputs, output_grads, input_inverse, grad_inverse):
    maps = layer_inputs[0]
    grads = output_grads[0]
    k_rows = input_inverse[0]
    g_inv = grad_inverse[0]
    side = maps.shape[1]
    width = maps.shape[3]
    group = lax.axis_size("pos")
    rows, full = k_rows.shape
    scale = 1.0 / (maps.shape[0] * maps.shape[1] * maps.shape[2] * group)
    me = lax.axis_index("pos")
    core = me & 1
    xbit = (me >> 1) & 1
    cols = 2 * core + xbit
    zbits = [b for b in (1 << i for i in range(2, 32)) if b < group]
    quarter = width // 4
    flat_maps = maps.reshape(-1, width)
    flat_grads = grads.reshape(-1, width)

    keep, send, k_own, k_send = pl.pallas_call(
        functools.partial(grad_kernel, side),
        out_shape=[jax.ShapeDtypeStruct((2, 10, quarter, width), F32)] * 2
        + [
            jax.ShapeDtypeStruct((2, 9, rows, width), BF16),
            jax.ShapeDtypeStruct((10, rows, width), F32),
        ],
        in_specs=[HBM] * 4,
        out_specs=[VMEM] * 4,
        scratch_shapes=[
            pltpu.VMEM((width, full), F32),
            pltpu.VMEM(flat_maps.shape, BF16),
            pltpu.VMEM(flat_grads.shape, BF16),
            pltpu.VMEM(g_inv.shape, F32),
            pltpu.VMEM(k_rows.shape, F32),
            pltpu.SemaphoreType.DMA((4,)),
        ],
        compiler_params=PARAMS,
    )(*(pltpu.with_memory_space_constraint(a, pltpu.HBM) for a in (flat_maps, flat_grads, g_inv, k_rows)))

    def message(values, level):
        level = jnp.maximum(level, -99.0)
        return jnp.concatenate([values * jnp.exp2(TOP - level)[None], level[None]], axis=0).astype(F16)

    def received(parcel):
        parcel = parcel.astype(F32)
        return parcel[:9] * jnp.exp2(parcel[9] - TOP)[None], parcel[9]

    other = swap(send, 1)
    h = keep[:, :9] + other[:, :9]
    level = jnp.maximum(keep[:, 9], other[:, 9]) + 1
    k_half = behind(k_send, h).astype(F16)
    k_others = [swap(k_half, 2), swap(k_half, 1), swap(k_half, 3)]
    own = behind(jnp.stack([flat_maps, flat_grads]), h)
    next_own = after(own)

    def add(values, level, bit):
        more, other_level = received(swap(message(values[1], level[1]) if bit == 2 else message(values, level), bit))
        if bit == 2:
            values, level = values[0], level[0]
        return values + more, jnp.maximum(level, other_level) + 1

    h, level = add(h, level, 2)
    h, level = add(h, level, zbits[0])
    next_own = behind(next_own, h)
    two_own = jnp.stack([flat_maps, next_own[0]])
    two_x = swap(two_own, 2)
    for b in zbits[1:]:
        h, level = add(h, level, b)

    def k_pair(parts):
        return jnp.concatenate(parts, axis=2)

    def k_split(parcel):
        values, _ = received(parcel)
        high = lax.reduce_precision(values, 8, 7)
        return jnp.stack([high, values - high]).astype(BF16)

    k_a = k_pair([k_own, k_split(k_others[0])])
    k_b = k_pair([k_split(k_others[1]), k_split(k_others[2])])

    main_a, main_b, p_t = pl.pallas_call(
        functools.partial(precond_kernel, scale),
        out_shape=[jax.ShapeDtypeStruct((quarter, 2 * rows), F32)] * 2
        + [jax.ShapeDtypeStruct((quarter, 4 * rows), BF16)],
        in_specs=[VMEM] * 3,
        out_specs=[VMEM] * 3,
        compiler_params=PARAMS,
    )(h, k_a, k_b)

    def by_bit(mine, other, b):
        return jnp.where((me & b) == 0, jnp.concatenate([mine, other], 1), jnp.concatenate([other, mine], 1))

    gram_keep, gram_send = pl.pallas_call(
        gram_kernel,
        out_shape=[jax.ShapeDtypeStruct((2, 2 * quarter, width), F32)] * 2,
        in_specs=[VMEM] * 2,
        out_specs=[VMEM] * 2,
        scratch_shapes=[pltpu.VMEM((2, width, width), F32)],
        compiler_params=PARAMS,
    )(flat_grads, next_own[1])
    gram_keep, gram_send, two_own = behind((gram_keep, gram_send, two_own), p_t)
    core_own = swap(two_own, 1)
    gram = gram_keep + swap(gram_send, 1)
    for b in zbits[:-1]:
        p_t = by_bit(p_t, swap(p_t, b), b)

    two_x = behind(two_x, p_t)
    core_x = swap(two_x, 1)
    gram = behind(gram, p_t)
    gram = gram[0] + swap(gram[1], 2)
    low = cols * quarter
    last = lax.axis_index("layer") == lax.axis_size("layer") - 1
    p_t = by_bit(after(p_t), after(p_t, zbits[-1]), zbits[-1])
    p_t = jnp.where(last, jnp.zeros_like(p_t), p_t)

    out_width = full + 2 * width
    cross_t, cross_half = pl.pallas_call(
        functools.partial(cross_kernel, side),
        out_shape=[
            jax.ShapeDtypeStruct((quarter, out_width), F32),
            jax.ShapeDtypeStruct((quarter, out_width + 2 * width), BF16),
        ],
        in_specs=[VMEM] * 6,
        out_specs=[VMEM] * 2,
        compiler_params=PARAMS,
    )(two_own, two_x, core_own, core_x, p_t, gram)

    place = (jnp.arange(width)[None, :] == low + jnp.arange(quarter)[:, None]).astype(F32)
    main_a, main_b = behind((main_a, main_b), cross_half)
    g_scaled = behind(g_inv, cross_half) * (scale * scale)
    main = jnp.stack([dot_t(main_a, place, precision=HIGH), dot_t(main_b, place, precision=HIGH)])
    cross_t, gram = cross_t[:, :full], cross_t[:, full:]
    for b in zbits:
        other = swap(cross_half, b).astype(F32)
        cross_t = cross_t + other[:, :full]
        gram = gram + (other[:, full:out_width] + other[:, out_width:])
        high = lax.reduce_precision(gram, 8, 7)
        rest = lax.reduce_precision(gram - high, 8, 7)
        gram = high + rest
        cross_half = jnp.concatenate([cross_t, high, rest], axis=1).astype(BF16)

    out, send = pl.pallas_call(
        update_kernel,
        out_shape=[jax.ShapeDtypeStruct((2, rows, width), F32)] * 2,
        in_specs=[VMEM] * 6,
        out_specs=[VMEM] * 2,
        compiler_params=PARAMS,
    )(cross_t, gram[:, width:], g_scaled, k_a, k_b, main)
    gram = behind(gram, out) * scale
    gram = jnp.stack([gram, swap(gram, 2)])
    out = out + swap(send, 2)
    gram = jnp.stack([gram, swap(gram, 1)])
    update = out[0] + swap(out[1], 1)
    gram = jnp.where(xbit == 0, gram, gram[:, ::-1])
    gram = jnp.where(core == 0, gram, gram[::-1])
    gram = gram.reshape(width, 2, width).transpose(1, 2, 0)
    return (update[None], gram[None])


def solution(mesh):
    return jax.shard_map(
        per_device,
        mesh=mesh,
        in_specs=(
            P("layer", "pos", None, None, None),
            P("layer", "pos", None, None, None),
            P("layer", "pos", None),
            P("layer", None, None),
        ),
        out_specs=(P("layer", "pos", None), P("layer", None, None, None)),
        check_vma=False,
    )
```

```python
import functools

import jax
import jax.numpy as jnp
from jax import lax
from jax.experimental import pallas as pl
from jax.experimental.pallas import tpu as pltpu
from jax.sharding import PartitionSpec as P

F32 = jnp.float32
BF16 = jnp.bfloat16
HIGH = lax.Precision.HIGHEST
F16 = jnp.float16
TOP = 13.0


def behind(block, point):
    return lax.optimization_barrier((block, point))[0]


def after(block, bit=0):
    layers, group = lax.axis_size("layer"), lax.axis_size("pos")
    route = [(((i + 1) % layers) * group + (p ^ bit), i * group + p) for i in range(layers) for p in range(group)]
    return lax.ppermute(block, ("layer", "pos"), route)


def swap(block, bit):
    return lax.ppermute(block, "pos", [(i, i ^ bit) for i in range(lax.axis_size("pos"))])


def dot_t(a, b, **kw):
    return lax.dot_general(a, b, (((0,), (0,)), ((), ())), preferred_element_type=F32, **kw)


def dot_nt(a, b, **kw):
    return lax.dot_general(a, b, (((1,), (1,)), ((), ())), preferred_element_type=F32, **kw)


def shifted(block, dy, dx, side):
    lanes = block.shape[1]
    place = lax.broadcasted_iota(jnp.int32, (1, lanes), 1)
    x = place % side
    y = (place // side) % side
    if dx:
        block = jnp.where((x + dx >= 0) & (x + dx < side), pltpu.roll(block, (-dx) % lanes, 1), 0.0)
    if dy:
        block = jnp.where((y + dy >= 0) & (y + dy < side), pltpu.roll(block, (-dy * side) % lanes, 1), 0.0)
    return block


def taps_to_rows(block, side):
    moved = []
    for r in range(3):
        for s in range(3):
            moved.append(shifted(shifted(block, 0, 1 - s, side), 1 - r, 0, side).astype(BF16))
    return jnp.concatenate(moved, axis=0)


def patches(maps, side):
    count, width = maps.shape
    wide = maps.astype(F32)
    x = lax.broadcasted_iota(jnp.int32, (count, 1), 0) % side
    area = side * side
    edge = jnp.zeros((side, width), BF16)
    columns = []
    for s in range(3):
        moved = maps
        if s != 1:
            inside = (x + (s - 1) >= 0) & (x + (s - 1) < side)
            moved = jnp.where(inside, pltpu.roll(wide, (1 - s) % count, 0), 0.0).astype(BF16)
        columns.append(moved)
    pieces = []
    for r in range(3):
        for s in range(3):
            parts = []
            for first in range(0, count, area):
                image = columns[s][first : first + area]
                if r == 0:
                    parts += [edge, image[: area - side]]
                elif r == 1:
                    parts += [image]
                else:
                    parts += [image[side:], edge]
            pieces.append(jnp.concatenate(parts, axis=0))
    return jnp.concatenate(pieces, axis=1)


def exponent(block):
    top = jnp.maximum(jnp.max(jnp.abs(block)), 1e-30)
    return jnp.ceil(jnp.log2(top))


def grad_kernel(
    side, maps_in, grads_in, g_in, k_in, keep, send, k_parts, k_send, all_rows, maps, grads, g_inv, k_rows, sems
):
    copies = [
        pltpu.make_async_copy(source, target, sems.at[i])
        for i, (source, target) in enumerate(
            [(g_in, g_inv), (grads_in, grads), (maps_in, maps), (k_in, k_rows)]
        )
    ]
    for copy in copies:
        copy.start()
    copies[0].wait()
    copies[1].wait()
    width = maps.shape[1]
    g_t = g_inv[...]
    first = g_t.astype(BF16)
    rest = g_t - first.astype(F32)
    second = rest.astype(BF16)
    third = (rest - second.astype(F32)).astype(BF16)
    g = grads[...]

    def mix(part):
        return lax.dot_general(part, g, (((0,), (1,)), ((), ())), preferred_element_type=F32)

    mixed = mix(first) + (mix(second) + mix(third))
    copies[2].wait()
    both = jnp.dot(two_parts(mixed), patches(maps[...], side), preferred_element_type=F32)
    both = both[:width] + both[width:]
    all_rows[...] = both
    core, xbit = place_bits()
    mine = 2 * core + xbit
    quarter = width // 4
    level = jnp.full((quarter, width), exponent(both), F32)
    for j in range(4):
        block = all_rows[pl.ds(pl.multiple_of((mine ^ j) * quarter, quarter), quarter), :]
        target = keep if j < 2 else send
        for tap in range(9):
            target[j % 2, tap] = block[:, tap * width : (tap + 1) * width]
        target[j % 2, 9] = level
    copies[3].wait()
    k = k_rows[...]
    high = k.astype(BF16)
    rest = (k - high.astype(F32)).astype(BF16)
    level = jnp.maximum(exponent(k), -99.0)
    factor = jnp.exp2(jnp.full((1, width), TOP - level, F32))
    for tap in range(9):
        part = slice(tap * width, (tap + 1) * width)
        k_parts[0, tap] = high[:, part]
        k_parts[1, tap] = rest[:, part]
        k_send[tap] = k[:, part] * factor
    k_send[9] = jnp.full((k.shape[0], width), level, F32)


def cross_kernel(side, part_0, part_1, part_2, part_3, precond_t, gram, out, out_half):
    quarter = precond_t.shape[0]
    width = part_0.shape[2]
    full = precond_t.shape[1]
    taps = jnp.concatenate([precond_t[:, t * width : (t + 1) * width] for t in range(9)], axis=0)
    both = None
    for device in (part_0, part_1, part_2, part_3):
        spread = dot_nt(taps, device[1])
        mapped = None
        for s in range(3):
            column = None
            for r in range(3):
                low = quarter * (3 * r + s)
                part = shifted(spread[low : low + quarter], r - 1, 0, side)
                column = part if column is None else column + part
            column = shifted(column, 0, s - 1, side)
            mapped = column if mapped is None else mapped + column
        mapped = mapped.astype(BF16).astype(F32)
        part = jnp.dot(taps_to_rows(mapped, side), device[0], preferred_element_type=F32)
        both = part if both is None else both + part
    for tap in range(9):
        part = both[quarter * tap : quarter * (tap + 1)]
        out[:, tap * width : (tap + 1) * width] = part
        out_half[:, tap * width : (tap + 1) * width] = part.astype(BF16)
    for i in range(2):
        part = gram[i * quarter : (i + 1) * quarter]
        high = part.astype(BF16)
        rest = (part - high.astype(F32)).astype(BF16)
        low = full + i * width
        out[:, low : low + width] = high.astype(F32) + rest.astype(F32)
        out_half[:, low : low + width] = high
        out_half[:, low + 2 * width : low + 3 * width] = rest


def two_parts(block):
    high = block.astype(BF16)
    return jnp.concatenate([high, (block - high.astype(F32)).astype(BF16)], axis=0)


def place_bits():
    me = lax.axis_index("pos")
    return me & 1, (me >> 1) & 1


def taps_to_lanes(block):
    return jnp.concatenate([block[tap] for tap in range(9)], axis=1)


def precond_kernel(scale, e_t, k_a, k_b, main_a, main_b, precond_t):
    core, xbit = place_bits()
    count = e_t.shape[1]
    rows = k_a.shape[2] // 2
    parts = two_parts(taps_to_lanes(e_t) * scale)
    total = None
    for flip, k, main in ((0, k_a, main_a), (1, k_b, main_b)):
        product = dot_nt(parts, taps_to_lanes(k.at[0])) + dot_nt(parts, taps_to_lanes(k.at[1]))
        product = product[:count] + product[count:]
        main[...] = product
        source = lax.broadcasted_iota(jnp.int32, (2 * rows, 4 * rows), 0)
        target = lax.broadcasted_iota(jnp.int32, (2 * rows, 4 * rows), 1)
        second = (source >= rows).astype(jnp.int32)
        block = 2 * (xbit ^ second) + (core ^ flip)
        one_hot = (source - second * rows + block * rows == target).astype(F32).astype(BF16)
        placed = jnp.dot(product.astype(BF16), one_hot, preferred_element_type=F32)
        total = placed if total is None else total + placed
    precond_t[...] = total.astype(BF16)


def update_kernel(cross_t, gram, g_inv, k_a, k_b, main, keep, send_x, send_core, send_diagonal):
    rows = k_a.shape[2] // 2
    width = main.shape[2]
    mixed = jnp.dot(gram[:, width:], g_inv[...], precision=HIGH)
    mixed = jnp.concatenate([mixed, mixed], axis=0)
    parts = two_parts(cross_t[...])
    quarter = gram.shape[0]
    for i, (k, targets) in enumerate(((k_a, (keep, send_x)), (k_b, (send_core, send_diagonal)))):
        product = dot_nt(taps_to_lanes(k.at[0]), parts) + dot_nt(taps_to_lanes(k.at[1]), parts)
        result = main[i] - jnp.dot(product, mixed, precision=HIGH)
        targets[0][:rows] = result[:rows]
        targets[1][:rows] = result[rows:]
    for target in (keep, send_x, send_core, send_diagonal):
        target[rows : rows + quarter] = gram[:, :width]
        target[rows + quarter :] = gram[:, width:]


def finish_kernel(scale, mine, from_x, from_core, from_diagonal, update, grams, scratch):
    core, xbit = place_bits()
    first = 2 * core + xbit
    rows, width = update.shape
    quarter = width // 4
    update[...] = (mine[:rows] + from_x[:rows]) + (from_core[:rows] + from_diagonal[:rows])
    for j, source in enumerate((mine, from_x, from_core, from_diagonal)):
        place = pl.ds(pl.multiple_of((first ^ j) * quarter, quarter), quarter)
        for i in range(2):
            scratch[i, place, :] = source[rows + i * quarter : rows + (i + 1) * quarter] * scale
    grams[0] = scratch[0]
    grams[1] = scratch[1].T


def gram_kernel(grads, next_grads, keep, send, scratch):
    core, xbit = place_bits()
    mine = 2 * core + xbit
    width = grads.shape[1]
    quarter = width // 4
    g = grads[...]
    last = lax.axis_index("layer") == lax.axis_size("layer") - 1
    scratch[0] = dot_t(g, g)
    scratch[1] = jnp.where(last, 0.0, dot_t(next_grads[...], g))
    for j in range(4):
        for i in range(2):
            (keep if j < 2 else send)[j % 2, i * quarter : (i + 1) * quarter] = scratch[
                i, pl.ds(pl.multiple_of((mine ^ j) * quarter, quarter), quarter), :
            ]


VMEM = pl.BlockSpec(memory_space=pltpu.VMEM)
HBM = pl.BlockSpec(memory_space=pltpu.HBM)
PARAMS = pltpu.CompilerParams(vmem_limit_bytes=16 * 1024 * 1024)


def per_device(layer_inputs, output_grads, input_inverse, grad_inverse):
    maps = layer_inputs[0]
    grads = output_grads[0]
    k_rows = input_inverse[0]
    g_inv = grad_inverse[0]
    side = maps.shape[1]
    width = maps.shape[3]
    group = lax.axis_size("pos")
    rows, full = k_rows.shape
    scale = 1.0 / (maps.shape[0] * maps.shape[1] * maps.shape[2] * group)
    me = lax.axis_index("pos")
    core = me & 1
    xbit = (me >> 1) & 1
    cols = 2 * core + xbit
    zbits = [b for b in (1 << i for i in range(2, 32)) if b < group]
    quarter = width // 4
    flat_maps = maps.reshape(-1, width)
    flat_grads = grads.reshape(-1, width)

    keep, send, k_own, k_send = pl.pallas_call(
        functools.partial(grad_kernel, side),
        out_shape=[jax.ShapeDtypeStruct((2, 10, quarter, width), F32)] * 2
        + [
            jax.ShapeDtypeStruct((2, 9, rows, width), BF16),
            jax.ShapeDtypeStruct((10, rows, width), F32),
        ],
        in_specs=[HBM] * 4,
        out_specs=[VMEM] * 4,
        scratch_shapes=[
            pltpu.VMEM((width, full), F32),
            pltpu.VMEM(flat_maps.shape, BF16),
            pltpu.VMEM(flat_grads.shape, BF16),
            pltpu.VMEM(g_inv.shape, F32),
            pltpu.VMEM(k_rows.shape, F32),
            pltpu.SemaphoreType.DMA((4,)),
        ],
        compiler_params=PARAMS,
    )(*(pltpu.with_memory_space_constraint(a, pltpu.HBM) for a in (flat_maps, flat_grads, g_inv, k_rows)))

    def message(values, level):
        level = jnp.maximum(level, -99.0)
        return jnp.concatenate([values * jnp.exp2(TOP - level)[None], level[None]], axis=0).astype(F16)

    def received(parcel):
        parcel = parcel.astype(F32)
        return parcel[:9] * jnp.exp2(parcel[9] - TOP)[None], parcel[9]

    other = swap(send, 1)
    h = keep[:, :9] + other[:, :9]
    level = jnp.maximum(keep[:, 9], other[:, 9]) + 1
    k_half = behind(k_send, h).astype(F16)
    k_others = [swap(k_half, 2), swap(k_half, 1), swap(k_half, 3)]
    own = behind(jnp.stack([flat_maps, flat_grads]), h)
    next_own = after(own)

    def add(values, level, bit):
        more, other_level = received(swap(message(values[1], level[1]) if bit == 2 else message(values, level), bit))
        if bit == 2:
            values, level = values[0], level[0]
        return values + more, jnp.maximum(level, other_level) + 1

    h, level = add(h, level, 2)
    h, level = add(h, level, zbits[0])
    next_own = behind(next_own, h)
    two_own = jnp.stack([flat_maps, next_own[0]])
    two_x = swap(two_own, 2)
    for b in zbits[1:]:
        h, level = add(h, level, b)

    def k_pair(parts):
        return jnp.concatenate(parts, axis=2)

    def k_split(parcel):
        values, _ = received(parcel)
        high = lax.reduce_precision(values, 8, 7)
        return jnp.stack([high, values - high]).astype(BF16)

    k_a = k_pair([k_own, k_split(k_others[0])])
    k_b = k_pair([k_split(k_others[1]), k_split(k_others[2])])

    main_a, main_b, p_t = pl.pallas_call(
        functools.partial(precond_kernel, scale),
        out_shape=[jax.ShapeDtypeStruct((quarter, 2 * rows), F32)] * 2
        + [jax.ShapeDtypeStruct((quarter, 4 * rows), BF16)],
        in_specs=[VMEM] * 3,
        out_specs=[VMEM] * 3,
        compiler_params=PARAMS,
    )(h, k_a, k_b)

    def by_bit(mine, other, b):
        return jnp.where((me & b) == 0, jnp.concatenate([mine, other], 1), jnp.concatenate([other, mine], 1))

    gram_keep, gram_send = pl.pallas_call(
        gram_kernel,
        out_shape=[jax.ShapeDtypeStruct((2, 2 * quarter, width), F32)] * 2,
        in_specs=[VMEM] * 2,
        out_specs=[VMEM] * 2,
        scratch_shapes=[pltpu.VMEM((2, width, width), F32)],
        compiler_params=PARAMS,
    )(flat_grads, next_own[1])
    gram_keep, gram_send, two_own = behind((gram_keep, gram_send, two_own), p_t)
    core_own = swap(two_own, 1)
    gram = gram_keep + swap(gram_send, 1)
    for b in zbits[:-1]:
        p_t = by_bit(p_t, swap(p_t, b), b)

    two_x = behind(two_x, p_t)
    core_x = swap(two_x, 1)
    gram = behind(gram, p_t)
    gram = gram[0] + swap(gram[1], 2)
    low = cols * quarter
    last = lax.axis_index("layer") == lax.axis_size("layer") - 1
    p_t = by_bit(after(p_t), after(p_t, zbits[-1]), zbits[-1])
    p_t = jnp.where(last, jnp.zeros_like(p_t), p_t)

    out_width = full + 2 * width
    cross_t, cross_half = pl.pallas_call(
        functools.partial(cross_kernel, side),
        out_shape=[
            jax.ShapeDtypeStruct((quarter, out_width), F32),
            jax.ShapeDtypeStruct((quarter, out_width + 2 * width), BF16),
        ],
        in_specs=[VMEM] * 6,
        out_specs=[VMEM] * 2,
        compiler_params=PARAMS,
    )(two_own, two_x, core_own, core_x, p_t, gram)

    place = (jnp.arange(width)[None, :] == low + jnp.arange(quarter)[:, None]).astype(F32)
    main_a, main_b = behind((main_a, main_b), cross_half)
    g_scaled = behind(g_inv, cross_half) * (scale * scale)
    main = jnp.stack([dot_t(main_a, place, precision=HIGH), dot_t(main_b, place, precision=HIGH)])
    cross_t, gram = cross_t[:, :full], cross_t[:, full:]
    for b in zbits:
        other = swap(cross_half, b).astype(F32)
        cross_t = cross_t + other[:, :full]
        gram = gram + (other[:, full:out_width] + other[:, out_width:])
        high = lax.reduce_precision(gram, 8, 7)
        rest = lax.reduce_precision(gram - high, 8, 7)
        gram = high + rest
        cross_half = jnp.concatenate([cross_t, high, rest], axis=1).astype(BF16)

    parcels = pl.pallas_call(
        update_kernel,
        out_shape=[jax.ShapeDtypeStruct((rows + 2 * quarter, width), F32)] * 4,
        in_specs=[VMEM] * 6,
        out_specs=[VMEM] * 4,
        compiler_params=PARAMS,
    )(cross_t, gram, g_scaled, k_a, k_b, main)
    parcels = [parcels[0]] + [swap(parcels[j], bits) for j, bits in ((1, 2), (2, 1), (3, 3))]
    update, grams = pl.pallas_call(
        functools.partial(finish_kernel, scale),
        out_shape=[jax.ShapeDtypeStruct((rows, width), F32), jax.ShapeDtypeStruct((2, width, width), F32)],
        in_specs=[VMEM] * 4,
        out_specs=[VMEM] * 2,
        scratch_shapes=[pltpu.VMEM((2, width, width), F32)],
        compiler_params=PARAMS,
    )(*parcels)
    return (update[None], grams[None])


def solution(mesh):
    return jax.shard_map(
        per_device,
        mesh=mesh,
        in_specs=(
            P("layer", "pos", None, None, None),
            P("layer", "pos", None, None, None),
            P("layer", "pos", None),
            P("layer", None, None),
        ),
        out_specs=(P("layer", "pos", None), P("layer", None, None, None)),
        check_vma=False,
    )
```

```python
import functools

import jax
import jax.numpy as jnp
from jax import lax
from jax.experimental import pallas as pl
from jax.experimental.pallas import tpu as pltpu
from jax.sharding import PartitionSpec as P

F32 = jnp.float32
BF16 = jnp.bfloat16
HIGH = lax.Precision.HIGHEST
F16 = jnp.float16
TOP = 13.0


def behind(block, point):
    return lax.optimization_barrier((block, point))[0]


def after(block, bit=0):
    layers, group = lax.axis_size("layer"), lax.axis_size("pos")
    route = [(((i + 1) % layers) * group + (p ^ bit), i * group + p) for i in range(layers) for p in range(group)]
    return lax.ppermute(block, ("layer", "pos"), route)


def swap(block, bit):
    return lax.ppermute(block, "pos", [(i, i ^ bit) for i in range(lax.axis_size("pos"))])


def dot_t(a, b, **kw):
    return lax.dot_general(a, b, (((0,), (0,)), ((), ())), preferred_element_type=F32, **kw)


def dot_nt(a, b, **kw):
    return lax.dot_general(a, b, (((1,), (1,)), ((), ())), preferred_element_type=F32, **kw)


def shifted(block, dy, dx, side):
    lanes = block.shape[1]
    place = lax.broadcasted_iota(jnp.int32, (1, lanes), 1)
    x = place % side
    y = (place // side) % side
    if dx:
        block = jnp.where((x + dx >= 0) & (x + dx < side), pltpu.roll(block, (-dx) % lanes, 1), 0.0)
    if dy:
        block = jnp.where((y + dy >= 0) & (y + dy < side), pltpu.roll(block, (-dy * side) % lanes, 1), 0.0)
    return block


def taps_to_rows(block, side):
    moved = []
    for r in range(3):
        for s in range(3):
            moved.append(shifted(shifted(block, 0, 1 - s, side), 1 - r, 0, side).astype(BF16))
    return jnp.concatenate(moved, axis=0)


def patches(maps, side):
    count, width = maps.shape
    wide = maps.astype(F32)
    x = lax.broadcasted_iota(jnp.int32, (count, 1), 0) % side
    area = side * side
    edge = jnp.zeros((side, width), BF16)
    columns = []
    for s in range(3):
        moved = maps
        if s != 1:
            inside = (x + (s - 1) >= 0) & (x + (s - 1) < side)
            moved = jnp.where(inside, pltpu.roll(wide, (1 - s) % count, 0), 0.0).astype(BF16)
        columns.append(moved)
    pieces = []
    for r in range(3):
        for s in range(3):
            parts = []
            for first in range(0, count, area):
                image = columns[s][first : first + area]
                if r == 0:
                    parts += [edge, image[: area - side]]
                elif r == 1:
                    parts += [image]
                else:
                    parts += [image[side:], edge]
            pieces.append(jnp.concatenate(parts, axis=0))
    return jnp.concatenate(pieces, axis=1)


def exponent(block):
    top = jnp.maximum(jnp.max(jnp.abs(block)), 1e-30)
    return jnp.ceil(jnp.log2(top))


def grad_kernel(
    side, maps_in, grads_in, g_in, k_in, keep, send, k_parts, all_rows, maps, grads, g_inv, k_rows, sems
):
    copies = [
        pltpu.make_async_copy(source, target, sems.at[i])
        for i, (source, target) in enumerate(
            [(g_in, g_inv), (grads_in, grads), (maps_in, maps), (k_in, k_rows)]
        )
    ]
    for copy in copies:
        copy.start()
    copies[0].wait()
    copies[1].wait()
    width = maps.shape[1]
    g_t = g_inv[...]
    first = g_t.astype(BF16)
    rest = g_t - first.astype(F32)
    second = rest.astype(BF16)
    third = (rest - second.astype(F32)).astype(BF16)
    g = grads[...]

    def mix(part):
        return lax.dot_general(part, g, (((0,), (1,)), ((), ())), preferred_element_type=F32)

    mixed = mix(first) + (mix(second) + mix(third))
    copies[2].wait()
    both = jnp.dot(two_parts(mixed), patches(maps[...], side), preferred_element_type=F32)
    both = both[:width] + both[width:]
    all_rows[...] = both
    core, xbit = place_bits()
    mine = 2 * core + xbit
    quarter = width // 4
    level = jnp.maximum(exponent(both), -99.0)
    factor = jnp.exp2(jnp.full((1, width), TOP - level, F32))
    level = jnp.full((8, width), level, F32)
    size = 9 * quarter + 8
    for j in range(4):
        block = all_rows[pl.ds(pl.multiple_of((mine ^ j) * quarter, quarter), quarter), :]
        for tap in range(9):
            part = block[:, tap * width : (tap + 1) * width]
            if j < 2:
                keep[j, tap * quarter : (tap + 1) * quarter] = part
            else:
                low = (j - 2) * size + tap * quarter
                send[low : low + quarter] = part * factor
        if j < 2:
            keep[j, size - 8 :] = level
        else:
            send[(j - 1) * size - 8 : (j - 1) * size] = level
    copies[3].wait()
    k = k_rows[...]
    high = k.astype(BF16)
    rest = (k - high.astype(F32)).astype(BF16)
    level = jnp.maximum(exponent(k), -99.0)
    factor = jnp.exp2(jnp.full((1, width), TOP - level, F32))
    rows = k.shape[0]
    for tap in range(9):
        part = slice(tap * width, (tap + 1) * width)
        k_parts[0, tap] = high[:, part]
        k_parts[1, tap] = rest[:, part]
        low = 2 * size + tap * rows
        send[low : low + rows] = k[:, part] * factor
    send[2 * size + 9 * rows :] = jnp.full((8, width), level, F32)


def cross_kernel(side, part_0, part_1, part_2, part_3, precond_t, gram, out, levels):
    quarter = precond_t.shape[0]
    width = part_0.shape[2]
    taps = jnp.concatenate([precond_t[:, t * width : (t + 1) * width] for t in range(9)], axis=0)
    both = None
    for device in (part_0, part_1, part_2, part_3):
        spread = dot_nt(taps, device[1])
        mapped = None
        for s in range(3):
            column = None
            for r in range(3):
                low = quarter * (3 * r + s)
                part = shifted(spread[low : low + quarter], r - 1, 0, side)
                column = part if column is None else column + part
            column = shifted(column, 0, s - 1, side)
            mapped = column if mapped is None else mapped + column
        mapped = mapped.astype(BF16).astype(F32)
        part = jnp.dot(taps_to_rows(mapped, side), device[0], preferred_element_type=F32)
        both = part if both is None else both + part
    out[...] = both
    level = jnp.maximum(exponent(both), -99.0)
    gram_level = jnp.maximum(exponent(gram[...]), -99.0)
    levels[0] = jnp.full((8, width), level, F32)
    levels[1] = jnp.full((8, width), gram_level, F32)


def two_parts(block):
    high = block.astype(BF16)
    return jnp.concatenate([high, (block - high.astype(F32)).astype(BF16)], axis=0)


def place_bits():
    me = lax.axis_index("pos")
    return me & 1, (me >> 1) & 1


def taps_to_lanes(block):
    return jnp.concatenate([block[tap] for tap in range(9)], axis=1)


def rows_to_lanes(block):
    count = block.shape[0] // 9
    return jnp.concatenate([block[tap * count : (tap + 1) * count] for tap in range(9)], axis=1)


def precond_kernel(scale, e_t, k_a, k_b, main_a, main_b, precond_t):
    core, xbit = place_bits()
    count = e_t.shape[0] // 9
    rows = k_a.shape[2] // 2
    parts = two_parts(rows_to_lanes(e_t) * scale)
    total = None
    for flip, k, main in ((0, k_a, main_a), (1, k_b, main_b)):
        product = dot_nt(parts, taps_to_lanes(k.at[0])) + dot_nt(parts, taps_to_lanes(k.at[1]))
        product = product[:count] + product[count:]
        main[...] = product
        source = lax.broadcasted_iota(jnp.int32, (2 * rows, 4 * rows), 0)
        target = lax.broadcasted_iota(jnp.int32, (2 * rows, 4 * rows), 1)
        second = (source >= rows).astype(jnp.int32)
        block = 2 * (xbit ^ second) + (core ^ flip)
        one_hot = (source - second * rows + block * rows == target).astype(F32).astype(BF16)
        placed = jnp.dot(product.astype(BF16), one_hot, preferred_element_type=F32)
        total = placed if total is None else total + placed
    precond_t[...] = total.astype(BF16)


def update_kernel(cross_t, gram, g_inv, k_a, k_b, main, keep, send_x, send_core, send_diagonal):
    rows = k_a.shape[2] // 2
    width = main.shape[2]
    mixed = jnp.dot(gram[gram.shape[0] // 2 :], g_inv[...], precision=HIGH)
    mixed = jnp.concatenate([mixed, mixed], axis=0)
    parts = two_parts(rows_to_lanes(cross_t))
    quarter = gram.shape[0] // 2
    for i, (k, targets) in enumerate(((k_a, (keep, send_x)), (k_b, (send_core, send_diagonal)))):
        product = dot_nt(taps_to_lanes(k.at[0]), parts) + dot_nt(taps_to_lanes(k.at[1]), parts)
        result = main[i] - jnp.dot(product, mixed, precision=HIGH)
        targets[0][:rows] = result[:rows]
        targets[1][:rows] = result[rows:]
    for target in (keep, send_x, send_core, send_diagonal):
        target[rows : rows + quarter] = gram[:quarter]
        target[rows + quarter :] = gram[quarter:]


def finish_kernel(scale, mine, from_x, from_core, from_diagonal, update, grams, scratch):
    core, xbit = place_bits()
    first = 2 * core + xbit
    rows, width = update.shape
    quarter = width // 4
    update[...] = (mine[:rows] + from_x[:rows]) + (from_core[:rows] + from_diagonal[:rows])
    for j, source in enumerate((mine, from_x, from_core, from_diagonal)):
        place = pl.ds(pl.multiple_of((first ^ j) * quarter, quarter), quarter)
        for i in range(2):
            scratch[i, place, :] = source[rows + i * quarter : rows + (i + 1) * quarter] * scale
    grams[0] = scratch[0]
    grams[1] = scratch[1].T


def gram_kernel(grads, next_grads, keep, send, scratch):
    core, xbit = place_bits()
    mine = 2 * core + xbit
    width = grads.shape[1]
    quarter = width // 4
    g = grads[...]
    last = lax.axis_index("layer") == lax.axis_size("layer") - 1
    scratch[0] = dot_t(g, g)
    scratch[1] = jnp.where(last, 0.0, dot_t(next_grads[...], g))
    for j in range(4):
        for i in range(2):
            (keep if j < 2 else send)[j % 2, i * quarter : (i + 1) * quarter] = scratch[
                i, pl.ds(pl.multiple_of((mine ^ j) * quarter, quarter), quarter), :
            ]


VMEM = pl.BlockSpec(memory_space=pltpu.VMEM)
HBM = pl.BlockSpec(memory_space=pltpu.HBM)
PARAMS = pltpu.CompilerParams(vmem_limit_bytes=16 * 1024 * 1024)


def per_device(layer_inputs, output_grads, input_inverse, grad_inverse):
    maps = layer_inputs[0]
    grads = output_grads[0]
    k_rows = input_inverse[0]
    g_inv = grad_inverse[0]
    side = maps.shape[1]
    width = maps.shape[3]
    group = lax.axis_size("pos")
    rows, full = k_rows.shape
    scale = 1.0 / (maps.shape[0] * maps.shape[1] * maps.shape[2] * group)
    me = lax.axis_index("pos")
    core = me & 1
    xbit = (me >> 1) & 1
    cols = 2 * core + xbit
    zbits = [b for b in (1 << i for i in range(2, 32)) if b < group]
    quarter = width // 4
    flat_maps = maps.reshape(-1, width)
    flat_grads = grads.reshape(-1, width)

    wide = 9 * quarter
    keep, send, k_own = pl.pallas_call(
        functools.partial(grad_kernel, side),
        out_shape=[
            jax.ShapeDtypeStruct((2, wide + 8, width), F32),
            jax.ShapeDtypeStruct((2 * (wide + 8) + 9 * rows + 8, width), F32),
            jax.ShapeDtypeStruct((2, 9, rows, width), BF16),
        ],
        in_specs=[HBM] * 4,
        out_specs=[VMEM] * 3,
        scratch_shapes=[
            pltpu.VMEM((width, full), F32),
            pltpu.VMEM(flat_maps.shape, BF16),
            pltpu.VMEM(flat_grads.shape, BF16),
            pltpu.VMEM(g_inv.shape, F32),
            pltpu.VMEM(k_rows.shape, F32),
            pltpu.SemaphoreType.DMA((4,)),
        ],
        compiler_params=PARAMS,
    )(*(pltpu.with_memory_space_constraint(a, pltpu.HBM) for a in (flat_maps, flat_grads, g_inv, k_rows)))

    def packed(groups):
        groups = [(values, jnp.maximum(level, -99.0)) for values, level in groups]
        scaled = [lax.reduce_precision(values * jnp.exp2(TOP - level[:1]), 5, 10) for values, level in groups]
        return jnp.concatenate(scaled + [level for _, level in groups], axis=0)

    def opened(parcel, sizes):
        parcel = parcel.astype(F32)
        groups = []
        start, at = 0, sum(sizes)
        for size in sizes:
            level = parcel[at : at + 8]
            groups.append((parcel[start : start + size] * jnp.exp2(level[:1] - TOP), level))
            start, at = start + size, at + 8
        return groups

    def summed(values, level, sent, bit):
        (more, other_level), = opened(swap(packed([sent]).astype(F16), bit), [9 * quarter])
        return values + more, jnp.maximum(level, other_level) + 1

    sent = send.astype(F16)
    other = swap(sent, 1)
    e_rows = 2 * (wide + 8)
    h, level = [], []
    for j in range(2):
        (more, other_level), = opened(other[j * (wide + 8) : (j + 1) * (wide + 8)], [wide])
        h.append(keep[j, :wide] + more)
        level.append(jnp.maximum(keep[j, wide:], other_level) + 1)
    k_core = other[e_rows:]
    k_sent, k_late = behind((sent[e_rows:], k_core), h[0])
    k_x, k_diagonal = swap(k_sent, 2), swap(k_late, 2)
    own = behind(jnp.stack([flat_maps, flat_grads]), sent)
    next_own = after(own)
    h, level = summed(h[0], level[0], (h[1], level[1]), 2)
    h, level = summed(h, level, (h, level), zbits[0])
    next_own = behind(next_own, h)
    two_own = jnp.stack([flat_maps, next_own[0]])
    two_x = swap(behind(two_own, h), 2)
    for b in zbits[1:]:
        h, level = summed(h, level, (h, level), b)

    def k_pair(parts):
        return jnp.concatenate(parts, axis=2)

    def k_split(parcel):
        (values, _), = opened(parcel, [9 * rows])
        values = values.reshape(9, rows, width)
        high = lax.reduce_precision(values, 8, 7)
        return jnp.stack([high, values - high]).astype(BF16)

    k_a = k_pair([k_own, k_split(k_x)])
    k_b = k_pair([k_split(k_core), k_split(k_diagonal)])

    main_a, main_b, p_t = pl.pallas_call(
        functools.partial(precond_kernel, scale),
        out_shape=[jax.ShapeDtypeStruct((quarter, 2 * rows), F32)] * 2
        + [jax.ShapeDtypeStruct((quarter, 4 * rows), BF16)],
        in_specs=[VMEM] * 3,
        out_specs=[VMEM] * 3,
        compiler_params=PARAMS,
    )(h, k_a, k_b)

    def by_bit(mine, other, b):
        return jnp.where((me & b) == 0, jnp.concatenate([mine, other], 1), jnp.concatenate([other, mine], 1))

    gram_keep, gram_send = pl.pallas_call(
        gram_kernel,
        out_shape=[jax.ShapeDtypeStruct((2, 2 * quarter, width), F32)] * 2,
        in_specs=[VMEM] * 2,
        out_specs=[VMEM] * 2,
        scratch_shapes=[pltpu.VMEM((2, width, width), F32)],
        compiler_params=PARAMS,
    )(flat_grads, next_own[1])
    gram_keep, gram_send = behind((gram_keep, gram_send), p_t)
    gram = gram_keep + swap(gram_send, 1)
    for b in zbits[:-1]:
        p_t = by_bit(p_t, swap(p_t, b), b)

    two_x = behind(two_x, p_t)
    core_x = swap(two_x, 1)
    two_own = behind(two_own, p_t)
    core_own = swap(two_own, 1)
    gram = behind(gram, p_t)
    gram = gram[0] + swap(gram[1], 2)
    low = cols * quarter
    last = lax.axis_index("layer") == lax.axis_size("layer") - 1
    p_t = by_bit(after(p_t), after(p_t, zbits[-1]), zbits[-1])
    p_t = jnp.where(last, jnp.zeros_like(p_t), p_t)

    wide = 9 * quarter
    cross_t, levels = pl.pallas_call(
        functools.partial(cross_kernel, side),
        out_shape=[jax.ShapeDtypeStruct((wide, width), F32), jax.ShapeDtypeStruct((2, 8, width), F32)],
        in_specs=[VMEM] * 6,
        out_specs=[VMEM] * 2,
        compiler_params=PARAMS,
    )(two_own, two_x, core_own, core_x, p_t, gram)

    place = (jnp.arange(width)[None, :] == low + jnp.arange(quarter)[:, None]).astype(F32)
    main_a, main_b = behind((main_a, main_b), cross_t)
    g_scaled = behind(g_inv, cross_t) * (scale * scale)
    main = jnp.stack([dot_t(main_a, place, precision=HIGH), dot_t(main_b, place, precision=HIGH)])
    level, gram_level = levels[0], levels[1]
    edge = wide + 2 * quarter
    for b in zbits:
        scaled = lax.reduce_precision(gram * jnp.exp2(TOP - gram_level[:1]), 5, 10)
        mine = jnp.concatenate([cross_t * jnp.exp2(TOP - level[:1]), scaled, level, gram_level], axis=0)
        other = swap(mine.astype(F16), b).astype(F32)
        cross_t = cross_t + other[:wide] * jnp.exp2(other[edge : edge + 1] - TOP)
        gram = scaled * jnp.exp2(gram_level[:1] - TOP) + other[wide:edge] * jnp.exp2(other[edge + 8 : edge + 9] - TOP)
        level = jnp.maximum(level, other[edge : edge + 8]) + 1
        gram_level = jnp.maximum(gram_level, other[edge + 8 :]) + 1

    parcels = pl.pallas_call(
        update_kernel,
        out_shape=[jax.ShapeDtypeStruct((rows + 2 * quarter, width), F32)] * 4,
        in_specs=[VMEM] * 6,
        out_specs=[VMEM] * 4,
        compiler_params=PARAMS,
    )(cross_t, gram, g_scaled, k_a, k_b, main)
    parcels = [parcels[0]] + [swap(parcels[j], bits) for j, bits in ((1, 2), (2, 1), (3, 3))]
    update, grams = pl.pallas_call(
        functools.partial(finish_kernel, scale),
        out_shape=[jax.ShapeDtypeStruct((rows, width), F32), jax.ShapeDtypeStruct((2, width, width), F32)],
        in_specs=[VMEM] * 4,
        out_specs=[VMEM] * 2,
        scratch_shapes=[pltpu.VMEM((2, width, width), F32)],
        compiler_params=PARAMS,
    )(*parcels)
    return (update[None], grams[None])


def solution(mesh):
    return jax.shard_map(
        per_device,
        mesh=mesh,
        in_specs=(
            P("layer", "pos", None, None, None),
            P("layer", "pos", None, None, None),
            P("layer", "pos", None),
            P("layer", None, None),
        ),
        out_specs=(P("layer", "pos", None), P("layer", None, None, None)),
        check_vma=False,
    )
```

```python
import functools

import jax
import jax.numpy as jnp
from jax import lax
from jax.experimental import pallas as pl
from jax.experimental.pallas import tpu as pltpu
from jax.sharding import PartitionSpec as P

F32 = jnp.float32
BF16 = jnp.bfloat16
HIGH = lax.Precision.HIGHEST
F16 = jnp.float16
TOP = 13.0


def behind(block, point):
    return lax.optimization_barrier((block, point))[0]


def after(block, bit=0):
    layers, group = lax.axis_size("layer"), lax.axis_size("pos")
    route = [(((i + 1) % layers) * group + (p ^ bit), i * group + p) for i in range(layers) for p in range(group)]
    return lax.ppermute(block, ("layer", "pos"), route)


def swap(block, bit):
    return lax.ppermute(block, "pos", [(i, i ^ bit) for i in range(lax.axis_size("pos"))])


def dot_t(a, b, **kw):
    return lax.dot_general(a, b, (((0,), (0,)), ((), ())), preferred_element_type=F32, **kw)


def dot_nt(a, b, **kw):
    return lax.dot_general(a, b, (((1,), (1,)), ((), ())), preferred_element_type=F32, **kw)


def shifted(block, dy, dx, side):
    lanes = block.shape[1]
    place = lax.broadcasted_iota(jnp.int32, (1, lanes), 1)
    x = place % side
    y = (place // side) % side
    if dx:
        block = jnp.where((x + dx >= 0) & (x + dx < side), pltpu.roll(block, (-dx) % lanes, 1), 0.0)
    if dy:
        block = jnp.where((y + dy >= 0) & (y + dy < side), pltpu.roll(block, (-dy * side) % lanes, 1), 0.0)
    return block


def taps_to_rows(block, side):
    moved = []
    for r in range(3):
        for s in range(3):
            moved.append(shifted(shifted(block, 0, 1 - s, side), 1 - r, 0, side).astype(BF16))
    return jnp.concatenate(moved, axis=0)


def patches(maps, side):
    count, width = maps.shape
    wide = maps.astype(F32)
    x = lax.broadcasted_iota(jnp.int32, (count, 1), 0) % side
    area = side * side
    edge = jnp.zeros((side, width), BF16)
    columns = []
    for s in range(3):
        moved = maps
        if s != 1:
            inside = (x + (s - 1) >= 0) & (x + (s - 1) < side)
            moved = jnp.where(inside, pltpu.roll(wide, (1 - s) % count, 0), 0.0).astype(BF16)
        columns.append(moved)
    pieces = []
    for r in range(3):
        for s in range(3):
            parts = []
            for first in range(0, count, area):
                image = columns[s][first : first + area]
                if r == 0:
                    parts += [edge, image[: area - side]]
                elif r == 1:
                    parts += [image]
                else:
                    parts += [image[side:], edge]
            pieces.append(jnp.concatenate(parts, axis=0))
    return jnp.concatenate(pieces, axis=1)


def exponent(block):
    top = jnp.maximum(jnp.max(jnp.abs(block)), 1e-30)
    return jnp.ceil(jnp.log2(top))


def grad_kernel(
    side, maps_in, grads_in, g_in, k_in, keep, send, k_parts, all_rows, maps, grads, g_inv, k_rows, sems
):
    copies = [
        pltpu.make_async_copy(source, target, sems.at[i])
        for i, (source, target) in enumerate(
            [(g_in, g_inv), (grads_in, grads), (maps_in, maps), (k_in, k_rows)]
        )
    ]
    for copy in copies:
        copy.start()
    copies[0].wait()
    copies[1].wait()
    width = maps.shape[1]
    g_t = g_inv[...]
    first = g_t.astype(BF16)
    rest = g_t - first.astype(F32)
    second = rest.astype(BF16)
    third = (rest - second.astype(F32)).astype(BF16)
    g = grads[...]

    def mix(part):
        return lax.dot_general(part, g, (((0,), (1,)), ((), ())), preferred_element_type=F32)

    mixed = mix(first) + (mix(second) + mix(third))
    copies[2].wait()
    both = jnp.dot(two_parts(mixed), patches(maps[...], side), preferred_element_type=F32)
    both = both[:width] + both[width:]
    all_rows[...] = both
    core, xbit = place_bits()
    mine = 2 * core + xbit
    quarter = width // 4
    level = jnp.maximum(exponent(both), -99.0)
    factor = jnp.exp2(jnp.full((1, width), TOP - level, F32))
    level = jnp.full((8, width), level, F32)
    size = 9 * quarter + 8
    for j in range(4):
        block = all_rows[pl.ds(pl.multiple_of((mine ^ j) * quarter, quarter), quarter), :]
        for tap in range(9):
            part = block[:, tap * width : (tap + 1) * width]
            if j < 2:
                keep[j, tap * quarter : (tap + 1) * quarter] = part
            else:
                low = (j - 2) * size + tap * quarter
                send[low : low + quarter] = part * factor
        if j < 2:
            keep[j, size - 8 :] = level
        else:
            send[(j - 1) * size - 8 : (j - 1) * size] = level
    copies[3].wait()
    k = k_rows[...]
    high = k.astype(BF16)
    rest = (k - high.astype(F32)).astype(BF16)
    level = jnp.maximum(exponent(k), -99.0)
    factor = jnp.exp2(jnp.full((1, width), TOP - level, F32))
    rows = k.shape[0]
    for tap in range(9):
        part = slice(tap * width, (tap + 1) * width)
        k_parts[0, tap] = high[:, part]
        k_parts[1, tap] = rest[:, part]
        low = 2 * size + tap * rows
        send[low : low + rows] = k[:, part] * factor
    send[2 * size + 9 * rows :] = jnp.full((8, width), level, F32)


def cross_kernel(side, part_0, part_1, part_2, part_3, precond_t, gram, out, levels):
    quarter = precond_t.shape[0]
    width = part_0.shape[2]
    taps = jnp.concatenate([precond_t[:, t * width : (t + 1) * width] for t in range(9)], axis=0)
    both = None
    for device in (part_0, part_1, part_2, part_3):
        spread = dot_nt(taps, device[1])
        mapped = None
        for s in range(3):
            column = None
            for r in range(3):
                low = quarter * (3 * r + s)
                part = shifted(spread[low : low + quarter], r - 1, 0, side)
                column = part if column is None else column + part
            column = shifted(column, 0, s - 1, side)
            mapped = column if mapped is None else mapped + column
        mapped = mapped.astype(BF16).astype(F32)
        part = jnp.dot(taps_to_rows(mapped, side), device[0], preferred_element_type=F32)
        both = part if both is None else both + part
    out[...] = both
    level = jnp.maximum(exponent(both), -99.0)
    gram_level = jnp.maximum(exponent(gram[...]), -99.0)
    levels[0] = jnp.full((8, width), level, F32)
    levels[1] = jnp.full((8, width), gram_level, F32)


def two_parts(block):
    high = block.astype(BF16)
    return jnp.concatenate([high, (block - high.astype(F32)).astype(BF16)], axis=0)


def place_bits():
    me = lax.axis_index("pos")
    return me & 1, (me >> 1) & 1


def taps_to_lanes(block):
    return jnp.concatenate([block[tap] for tap in range(9)], axis=1)


def rows_to_lanes(block):
    count = block.shape[0] // 9
    return jnp.concatenate([block[tap * count : (tap + 1) * count] for tap in range(9)], axis=1)


def precond_kernel(scale, e_t, k_a, k_b, main_a, main_b, precond_t):
    core, xbit = place_bits()
    count = e_t.shape[0] // 9
    rows = k_a.shape[2] // 2
    parts = two_parts(rows_to_lanes(e_t) * scale)
    total = None
    for flip, k, main in ((0, k_a, main_a), (1, k_b, main_b)):
        product = dot_nt(parts, taps_to_lanes(k.at[0])) + dot_nt(parts, taps_to_lanes(k.at[1]))
        product = product[:count] + product[count:]
        main[...] = product
        source = lax.broadcasted_iota(jnp.int32, (2 * rows, 4 * rows), 0)
        target = lax.broadcasted_iota(jnp.int32, (2 * rows, 4 * rows), 1)
        second = (source >= rows).astype(jnp.int32)
        block = 2 * (xbit ^ second) + (core ^ flip)
        one_hot = (source - second * rows + block * rows == target).astype(F32).astype(BF16)
        placed = jnp.dot(product.astype(BF16), one_hot, preferred_element_type=F32)
        total = placed if total is None else total + placed
    precond_t[...] = total.astype(BF16)


def update_kernel(cross_t, gram, g_inv, k_a, k_b, main, keep, send_x, send_core, send_diagonal):
    rows = k_a.shape[2] // 2
    width = main.shape[2]
    mixed = jnp.dot(gram[gram.shape[0] // 2 :], g_inv[...], precision=HIGH)
    high = mixed.astype(BF16)
    rest = (mixed - high.astype(F32)).astype(BF16)
    mixed = jnp.concatenate([high] * 4 + [rest] * 2, axis=0)
    parts = two_parts(rows_to_lanes(cross_t))
    quarter = gram.shape[0] // 2
    for i, (k, targets) in enumerate(((k_a, (keep, send_x)), (k_b, (send_core, send_diagonal)))):
        product = dot_nt(taps_to_lanes(k.at[0]), parts) + dot_nt(taps_to_lanes(k.at[1]), parts)
        high = product.astype(BF16)
        rest = (product - high.astype(F32)).astype(BF16)
        result = main[i] - jnp.dot(
            jnp.concatenate([high, rest, high], axis=1), mixed, preferred_element_type=F32
        )
        targets[0][:rows] = result[:rows]
        targets[1][:rows] = result[rows:]
    for target in (keep, send_x, send_core, send_diagonal):
        target[rows : rows + quarter] = gram[:quarter]
        target[rows + quarter :] = gram[quarter:]


def finish_kernel(scale, mine, from_x, from_core, from_diagonal, update, grams, scratch):
    core, xbit = place_bits()
    first = 2 * core + xbit
    rows, width = update.shape
    quarter = width // 4
    update[...] = (mine[:rows] + from_x[:rows]) + (from_core[:rows] + from_diagonal[:rows])
    for j, source in enumerate((mine, from_x, from_core, from_diagonal)):
        place = pl.ds(pl.multiple_of((first ^ j) * quarter, quarter), quarter)
        for i in range(2):
            scratch[i, place, :] = source[rows + i * quarter : rows + (i + 1) * quarter] * scale
    grams[0] = scratch[0]
    grams[1] = scratch[1].T


def gram_kernel(grads, next_grads, keep, send, scratch):
    core, xbit = place_bits()
    mine = 2 * core + xbit
    width = grads.shape[1]
    quarter = width // 4
    g = grads[...]
    last = lax.axis_index("layer") == lax.axis_size("layer") - 1
    scratch[0] = dot_t(g, g)
    scratch[1] = jnp.where(last, 0.0, dot_t(next_grads[...], g))
    for j in range(4):
        for i in range(2):
            (keep if j < 2 else send)[j % 2, i * quarter : (i + 1) * quarter] = scratch[
                i, pl.ds(pl.multiple_of((mine ^ j) * quarter, quarter), quarter), :
            ]


VMEM = pl.BlockSpec(memory_space=pltpu.VMEM)
HBM = pl.BlockSpec(memory_space=pltpu.HBM)
PARAMS = pltpu.CompilerParams(vmem_limit_bytes=16 * 1024 * 1024)


def per_device(layer_inputs, output_grads, input_inverse, grad_inverse):
    maps = layer_inputs[0]
    grads = output_grads[0]
    k_rows = input_inverse[0]
    g_inv = grad_inverse[0]
    side = maps.shape[1]
    width = maps.shape[3]
    group = lax.axis_size("pos")
    rows, full = k_rows.shape
    scale = 1.0 / (maps.shape[0] * maps.shape[1] * maps.shape[2] * group)
    me = lax.axis_index("pos")
    core = me & 1
    xbit = (me >> 1) & 1
    cols = 2 * core + xbit
    zbits = [b for b in (1 << i for i in range(2, 32)) if b < group]
    quarter = width // 4
    flat_maps = maps.reshape(-1, width)
    flat_grads = grads.reshape(-1, width)

    wide = 9 * quarter
    keep, send, k_own = pl.pallas_call(
        functools.partial(grad_kernel, side),
        out_shape=[
            jax.ShapeDtypeStruct((2, wide + 8, width), F32),
            jax.ShapeDtypeStruct((2 * (wide + 8) + 9 * rows + 8, width), F32),
            jax.ShapeDtypeStruct((2, 9, rows, width), BF16),
        ],
        in_specs=[HBM] * 4,
        out_specs=[VMEM] * 3,
        scratch_shapes=[
            pltpu.VMEM((width, full), F32),
            pltpu.VMEM(flat_maps.shape, BF16),
            pltpu.VMEM(flat_grads.shape, BF16),
            pltpu.VMEM(g_inv.shape, F32),
            pltpu.VMEM(k_rows.shape, F32),
            pltpu.SemaphoreType.DMA((4,)),
        ],
        compiler_params=PARAMS,
    )(*(pltpu.with_memory_space_constraint(a, pltpu.HBM) for a in (flat_maps, flat_grads, g_inv, k_rows)))

    def packed(groups):
        groups = [(values, jnp.maximum(level, -99.0)) for values, level in groups]
        scaled = [lax.reduce_precision(values * jnp.exp2(TOP - level[:1]), 5, 10) for values, level in groups]
        return jnp.concatenate(scaled + [level for _, level in groups], axis=0)

    def opened(parcel, sizes):
        parcel = parcel.astype(F32)
        groups = []
        start, at = 0, sum(sizes)
        for size in sizes:
            level = parcel[at : at + 8]
            groups.append((parcel[start : start + size] * jnp.exp2(level[:1] - TOP), level))
            start, at = start + size, at + 8
        return groups

    def summed(values, level, sent, bit):
        (more, other_level), = opened(swap(packed([sent]).astype(F16), bit), [9 * quarter])
        return values + more, jnp.maximum(level, other_level) + 1

    sent = send.astype(F16)
    other = swap(sent, 1)
    e_rows = 2 * (wide + 8)
    h, level = [], []
    for j in range(2):
        (more, other_level), = opened(other[j * (wide + 8) : (j + 1) * (wide + 8)], [wide])
        h.append(keep[j, :wide] + more)
        level.append(jnp.maximum(keep[j, wide:], other_level) + 1)
    k_core = other[e_rows:]
    k_sent, k_late = behind((sent[e_rows:], k_core), h[0])
    k_x, k_diagonal = swap(k_sent, 2), swap(k_late, 2)
    own = behind(jnp.stack([flat_maps, flat_grads]), sent)
    next_own = after(own)
    h, level = summed(h[0], level[0], (h[1], level[1]), 2)
    h, level = summed(h, level, (h, level), zbits[0])
    next_own = behind(next_own, h)
    two_own = jnp.stack([flat_maps, next_own[0]])
    two_x = swap(behind(two_own, h), 2)
    for b in zbits[1:]:
        h, level = summed(h, level, (h, level), b)

    def k_pair(parts):
        return jnp.concatenate(parts, axis=2)

    def k_split(parcel):
        (values, _), = opened(parcel, [9 * rows])
        values = values.reshape(9, rows, width)
        high = lax.reduce_precision(values, 8, 7)
        return jnp.stack([high, values - high]).astype(BF16)

    k_a = k_pair([k_own, k_split(k_x)])
    k_b = k_pair([k_split(k_core), k_split(k_diagonal)])

    main_a, main_b, p_t = pl.pallas_call(
        functools.partial(precond_kernel, scale),
        out_shape=[jax.ShapeDtypeStruct((quarter, 2 * rows), F32)] * 2
        + [jax.ShapeDtypeStruct((quarter, 4 * rows), BF16)],
        in_specs=[VMEM] * 3,
        out_specs=[VMEM] * 3,
        compiler_params=PARAMS,
    )(h, k_a, k_b)

    def by_bit(mine, other, b):
        return jnp.where((me & b) == 0, jnp.concatenate([mine, other], 1), jnp.concatenate([other, mine], 1))

    gram_keep, gram_send = pl.pallas_call(
        gram_kernel,
        out_shape=[jax.ShapeDtypeStruct((2, 2 * quarter, width), F32)] * 2,
        in_specs=[VMEM] * 2,
        out_specs=[VMEM] * 2,
        scratch_shapes=[pltpu.VMEM((2, width, width), F32)],
        compiler_params=PARAMS,
    )(flat_grads, next_own[1])
    gram_keep, gram_send = behind((gram_keep, gram_send), p_t)
    gram = gram_keep + swap(gram_send, 1)
    for b in zbits[:-1]:
        p_t = by_bit(p_t, swap(p_t, b), b)

    two_x = behind(two_x, p_t)
    core_x = swap(two_x, 1)
    two_own = behind(two_own, p_t)
    core_own = swap(two_own, 1)
    gram = behind(gram, p_t)
    gram = gram[0] + swap(gram[1], 2)
    low = cols * quarter
    last = lax.axis_index("layer") == lax.axis_size("layer") - 1
    p_t = by_bit(after(p_t), after(p_t, zbits[-1]), zbits[-1])
    p_t = jnp.where(last, jnp.zeros_like(p_t), p_t)

    wide = 9 * quarter
    cross_t, levels = pl.pallas_call(
        functools.partial(cross_kernel, side),
        out_shape=[jax.ShapeDtypeStruct((wide, width), F32), jax.ShapeDtypeStruct((2, 8, width), F32)],
        in_specs=[VMEM] * 6,
        out_specs=[VMEM] * 2,
        compiler_params=PARAMS,
    )(two_own, two_x, core_own, core_x, p_t, gram)

    place = (jnp.arange(width)[None, :] == low + jnp.arange(quarter)[:, None]).astype(F32)
    main_a, main_b = behind((main_a, main_b), cross_t)
    g_scaled = behind(g_inv, cross_t) * (scale * scale)
    main = jnp.stack([dot_t(main_a, place, precision=HIGH), dot_t(main_b, place, precision=HIGH)])
    level, gram_level = levels[0], levels[1]
    edge = wide + 2 * quarter
    for b in zbits:
        scaled = lax.reduce_precision(gram * jnp.exp2(TOP - gram_level[:1]), 5, 10)
        mine = jnp.concatenate([cross_t * jnp.exp2(TOP - level[:1]), scaled, level, gram_level], axis=0)
        other = swap(mine.astype(F16), b).astype(F32)
        cross_t = cross_t + other[:wide] * jnp.exp2(other[edge : edge + 1] - TOP)
        gram = scaled * jnp.exp2(gram_level[:1] - TOP) + other[wide:edge] * jnp.exp2(other[edge + 8 : edge + 9] - TOP)
        level = jnp.maximum(level, other[edge : edge + 8]) + 1
        gram_level = jnp.maximum(gram_level, other[edge + 8 :]) + 1

    parcels = pl.pallas_call(
        update_kernel,
        out_shape=[jax.ShapeDtypeStruct((rows + 2 * quarter, width), F32)] * 4,
        in_specs=[VMEM] * 6,
        out_specs=[VMEM] * 4,
        compiler_params=PARAMS,
    )(cross_t, gram, g_scaled, k_a, k_b, main)
    parcels = [parcels[0]] + [swap(parcels[j], bits) for j, bits in ((1, 2), (2, 1), (3, 3))]
    update, grams = pl.pallas_call(
        functools.partial(finish_kernel, scale),
        out_shape=[jax.ShapeDtypeStruct((rows, width), F32), jax.ShapeDtypeStruct((2, width, width), F32)],
        in_specs=[VMEM] * 4,
        out_specs=[VMEM] * 2,
        scratch_shapes=[pltpu.VMEM((2, width, width), F32)],
        compiler_params=PARAMS,
    )(*parcels)
    return (update[None], grams[None])


def solution(mesh):
    return jax.shard_map(
        per_device,
        mesh=mesh,
        in_specs=(
            P("layer", "pos", None, None, None),
            P("layer", "pos", None, None, None),
            P("layer", "pos", None),
            P("layer", None, None),
        ),
        out_specs=(P("layer", "pos", None), P("layer", None, None, None)),
        check_vma=False,
    )
```
